32 devices in a mesh: dp: 8 (over z, x), mp: 4 (over y, core).
Axes of the slice: x: 2, y: 2, z: 4, core: 2. Of those that a mesh axis runs over, the one named last changes fastest.
Arguments:
- inputs: bfloat16 [32, 1024, 512], P('dp', None, 'mp'), may hold values from -6 to 6
- cotangent: bfloat16 [32, 1024, 512], P('dp', None, 'mp'), may hold values from -6 to 6
- lengths: int32 [32], P('dp'), may hold values from 256 to 1024, as said below
- conv_master: float32 [9, 512, 512], P(None, 'dp', 'mp'), may hold values from -0.09375 to 0.09375
- hidden_master: float32 [512, 2048], P('dp', 'mp'), may hold values from -0.25 to 0.25
- output_master: float32 [2048, 512], P('mp', 'dp'), may hold values from -0.125 to 0.125
- conv_first: float32 [9, 512, 512], P(None, 'dp', 'mp'), may hold values from -0.00030517578 to 0.00030517578
- hidden_first: float32 [512, 2048], P('dp', 'mp'), may hold values from -0.00030517578 to 0.00030517578
- output_first: float32 [2048, 512], P('mp', 'dp'), may hold values from -0.00030517578 to 0.00030517578
- conv_second: float32 [9, 512, 512], P(None, 'dp', 'mp'), may hold values from 2.2413645e-10 to 8.965458e-10
- hidden_second: float32 [512, 2048], P('dp', 'mp'), may hold values from 2.2413645e-10 to 8.965458e-10
- output_second: float32 [2048, 512], P('mp', 'dp'), may hold values from 2.2413645e-10 to 8.965458e-10
- vectors: float32 [6, 512], replicated, may hold values from -0.6 to 6.5, as said below
- vector_first: float32 [6, 512], replicated, may hold values from -0.00024414062 to 0.00024414062
- vector_second: float32 [6, 512], replicated, may hold values from 1.1206822e-10 to 4.482729e-10
- hidden_bias: float32 [2048], P('mp'), may hold values from -3 to 3
- bias_first: float32 [2048], P('mp'), may hold values from -0.00010681152 to 0.00010681152
- bias_second: float32 [2048], P('mp'), may hold values from 2.2413644e-11 to 8.9654575e-11
Outputs:
- block_output: bfloat16 [32, 1024, 512], P('dp', None, 'mp')
- input_grad: float32 [32, 1024, 512], P('dp', None, 'mp')
- grad_norm: float32 [], replicated
- conv_weight_new: float32 [9, 512, 512], P(None, 'dp', 'mp')
- conv_first_new: float32 [9, 512, 512], P(None, 'dp', 'mp')
- conv_second_new: float32 [9, 512, 512], P(None, 'dp', 'mp')
- hidden_weight_new: float32 [512, 2048], P('dp', 'mp')
- hidden_first_new: float32 [512, 2048], P('dp', 'mp')
- hidden_second_new: float32 [512, 2048], P('dp', 'mp')
- output_weight_new: float32 [2048, 512], P('mp', 'dp')
- output_first_new: float32 [2048, 512], P('mp', 'dp')
- output_second_new: float32 [2048, 512], P('mp', 'dp')
- vectors_new: float32 [6, 512], replicated
- vector_first_new: float32 [6, 512], replicated
- vector_second_new: float32 [6, 512], replicated
- hidden_bias_new: float32 [2048], P('mp')
- bias_first_new: float32 [2048], P('mp')
- bias_second_new: float32 [2048], P('mp')
The draws below stay inside these ranges and needn't reach their ends.
Inputs may be any that keep to these rules, and one draw needn't show every extreme that they name: `lengths`: each window's valid length is 256, 512 or 1024; the first window has 256 and the last 1024. `vectors`: gains are positive.
All inputs are finite; a program needn't handle non-finite values.
Results may differ from the reference program's by a relative error of at most 0.0095.
Values may be sent and summed in bfloat16 or wider, within the bound.
No kernel may reach another device: no remote copies, remote signals or barrier semaphores. Data moves between devices by JAX's collectives and lax.ppermute only.
A program may use at most 192 MiB of HBM per device.

```python
import math
from functools import partial
import jax
import jax.numpy as jnp
from jax import lax

D = 512
FF = 2048
KERNEL = 9
DILATION = 8
LEN = 1024
STEP = 10
WIN = 32


def draw_lengths(key, part):
    window_ids = jnp.arange(WIN, dtype=jnp.int32)
    levels = 3 * window_ids // WIN + jax.random.randint(key, (WIN,), -1, 2, dtype=jnp.int32)
    levels = jnp.clip(levels, 0, 2)
    levels = jnp.where(window_ids == 0, 0, levels)
    levels = jnp.where(window_ids == WIN - 1, 2, levels)
    factors = jnp.where(levels == 0, 1, jnp.where(levels == 1, 2, 4)).astype(jnp.int32)
    return LEN // 4 * factors


def draw_vectors(key, part):
    subkeys = jax.random.split(key, 6)
    columns = jnp.arange(D, dtype=jnp.float32) / (D - 1)
    rising = 1.0 + 2.0 * columns
    spread = 0.5
    gain_one = rising * jax.random.uniform(subkeys[0], (D,), jnp.float32, 0.7, 1.3)
    shift_one = jax.random.uniform(subkeys[1], (D,), jnp.float32, -spread, spread)
    conv_bias = jax.random.uniform(subkeys[2], (D,), jnp.float32, -spread, spread)
    gain_two = rising * jax.random.uniform(subkeys[3], (D,), jnp.float32, 0.7, 1.3)
    shift_two = jax.random.uniform(subkeys[4], (D,), jnp.float32, -spread, spread)
    out_bias = jax.random.uniform(subkeys[5], (D,), jnp.float32, -spread, spread)
    return jnp.stack([gain_one, shift_one, conv_bias, gain_two, shift_two, out_bias])


def raised(values, own_key, source, target, shards_of, factor):
    owner, partner = [(jnp.arange(values.shape[dim]) // (values.shape[dim] // shards_of)).reshape([-1 if axis == dim else 1 for axis in range(values.ndim)]) for dim in (source, target)]
    chosen = jax.random.permutation(own_key, shards_of)[partner]
    strong = (owner == chosen) | (owner == (partner + shards_of // 2) % shards_of)
    return jnp.where(strong, factor * values, values)


def level_of(key, shape, shards, low, top_value):
    level = 1.0
    for position, parts in shards:
        heights = jax.random.uniform(jax.random.fold_in(jax.random.fold_in(key, 6), position), (parts,), jnp.float32, low / len(shards), top_value / len(shards))
        level = level * jnp.repeat(jnp.exp(heights), shape[position] // parts).reshape((-1,) + (1,) * (len(shape) - 1 - position))
    return level


def centred(rng, extent, deviation, limit, cuts=(), kind=jnp.bfloat16):
    values = deviation * jax.random.normal(rng, extent, jnp.float32)
    if cuts:
        values = values * level_of(rng, extent, cuts, -0.22, 0.18)
    return jnp.clip(values, -limit, limit).astype(kind)


def heavy_noise(own_key, extent, scale, most, pieces, heavy, kind=jnp.bfloat16):
    entries = scale * jax.random.normal(own_key, extent, jnp.float32)
    if pieces:
        entries = entries * level_of(own_key, extent, pieces, -0.22, 0.18)
    return jnp.clip(raised(entries, jax.random.fold_in(own_key, 3), *heavy), -most, most).astype(kind)


def setup_inputs(seed: int = 0) -> dict:
    streams_of = jax.random.split(jax.random.key(seed), 19)
    inputs = heavy_noise(streams_of[0], (WIN, LEN, D), 1.0, 6.0, ((0, 8), (2, 4)), (0, 2, 8, 2.0))
    cotangent = centred(streams_of[1], (WIN, LEN, D), 1.0, 6.0, ((0, 8), (2, 4)))
    lengths = draw_lengths(jax.random.fold_in(streams_of[18], 71), 0)
    conv_master = centred(streams_of[3], (KERNEL, D, D), (KERNEL * D) ** -0.5, 0.09375, ((1, 8), (2, 4)), jnp.float32)
    hidden_master = centred(streams_of[4], (D, FF), D ** -0.5, 0.25, ((0, 8), (1, 4)), jnp.float32)
    output_master = centred(streams_of[5], (FF, D), FF ** -0.5, 0.125, ((0, 4), (1, 8)), jnp.float32)
    conv_first = centred(streams_of[6], (KERNEL, D, D), (0.11 / (KERNEL * D * D + 2 * D * FF + 6 * D + FF) ** 0.5), 0.00030517578, ((1, 8), (2, 4)), jnp.float32)
    hidden_first = centred(streams_of[7], (D, FF), (0.11 / (KERNEL * D * D + 2 * D * FF + 6 * D + FF) ** 0.5), 0.00030517578, ((0, 8), (1, 4)), jnp.float32)
    output_first = centred(streams_of[8], (FF, D), (0.11 / (KERNEL * D * D + 2 * D * FF + 6 * D + FF) ** 0.5), 0.00030517578, ((0, 4), (1, 8)), jnp.float32)
    conv_second = jnp.clip(jnp.exp(math.log(8.965457820586664e-10) - 1.3862944 * jax.random.uniform(streams_of[9], (KERNEL, D, D), jnp.float32) ** level_of(streams_of[9], (KERNEL, D, D), ((1, 8), (2, 4)), -0.2, 0.2)), 2.241364455146666e-10, 8.965457820586664e-10)
    hidden_second = jnp.clip(jnp.exp(math.log(8.965457820586664e-10) - 1.3862944 * jax.random.uniform(streams_of[10], (D, FF), jnp.float32) ** level_of(streams_of[10], (D, FF), ((0, 8), (1, 4)), -0.2, 0.2)), 2.241364455146666e-10, 8.965457820586664e-10)
    output_second = jnp.clip(jnp.exp(math.log(8.965457820586664e-10) - 1.3862944 * jax.random.uniform(streams_of[11], (FF, D), jnp.float32) ** level_of(streams_of[11], (FF, D), ((0, 4), (1, 8)), -0.2, 0.2)), 2.241364455146666e-10, 8.965457820586664e-10)
    vectors = draw_vectors(jax.random.fold_in(streams_of[18], 71), 0)
    vector_first = centred(streams_of[13], (6, D), (0.08 / (KERNEL * D * D + 2 * D * FF + 6 * D + FF) ** 0.5), 0.00024414062, (), jnp.float32)
    vector_second = jnp.clip(jnp.exp(jax.random.uniform(streams_of[14], (6, D), jnp.float32, math.log(1.120682227573333e-10), math.log(4.482728910293332e-10))), 1.120682227573333e-10, 4.482728910293332e-10)
    hidden_bias = centred(streams_of[15], (FF,), 0.5, 3.0, ((0, 4),), jnp.float32)
    bias_first = centred(streams_of[16], (FF,), (0.035 / (KERNEL * D * D + 2 * D * FF + 6 * D + FF) ** 0.5), 0.00010681152, ((0, 4),), jnp.float32)
    bias_second = jnp.clip(jnp.exp(math.log(8.965457543030908e-11) - 1.3862944 * jax.random.uniform(streams_of[17], (FF,), jnp.float32) ** level_of(streams_of[17], (FF,), ((0, 4),), -0.2, 0.2)), 2.241364385757727e-11, 8.965457543030908e-11)
    return {"inputs": inputs, "cotangent": cotangent, "lengths": lengths, "conv_master": conv_master, "hidden_master": hidden_master, "output_master": output_master, "conv_first": conv_first, "hidden_first": hidden_first, "output_first": output_first, "conv_second": conv_second, "hidden_second": hidden_second, "output_second": output_second, "vectors": vectors, "vector_first": vector_first, "vector_second": vector_second, "hidden_bias": hidden_bias, "bias_first": bias_first, "bias_second": bias_second}


NORM_EPS = 1e-05
BETA_ONE = 0.9
BETA_TWO = 0.999
ADAM_EPS = 1e-08
MATRIX_RATE = 0.03
VECTOR_RATE = 0.3
WEIGHT_DECAY = 0.01
CLIP_NORM = 1.0
HIGHEST = lax.Precision.HIGHEST

@jax.custom_vjp
def low(v):
    return lax.optimization_barrier(v.astype(jnp.bfloat16)).astype(jnp.float32)

@jax.custom_vjp
def low_back(v):
    return v

def low_keep(v):
    return (low(v), None)

def low_pass(kept, grad):
    return (grad,)

def back_keep(v):
    return (v, None)

def back_low(kept, grad):
    return (low(grad),)
low.defvjp(low_keep, low_pass)
low_back.defvjp(back_keep, back_low)

def layer_norm(values, gain_vec, shift_vec):
    centre = values - lax.optimization_barrier(jnp.mean(values, axis=-1, keepdims=True))
    variance = lax.optimization_barrier(jnp.mean(centre * centre, axis=-1, keepdims=True))
    return centre * lax.rsqrt(variance + NORM_EPS) * gain_vec + shift_vec

def forward(conv_w, hidden_w, output_w, vector_rows, hidden_b, block_in, row_mask):
    normed = low(row_mask * layer_norm(block_in, vector_rows[0], vector_rows[1]))
    reach = DILATION * (KERNEL // 2)
    padded = jnp.pad(normed, ((0, 0), (reach, reach), (0, 0)))
    conv_out = jnp.zeros(block_in.shape, jnp.float32) + vector_rows[2]
    for tap_index in range(KERNEL):
        window = padded[:, tap_index * DILATION:tap_index * DILATION + LEN, :]
        conv_out = conv_out + jnp.einsum('gpi,io->gpo', window, conv_w[tap_index], precision=HIGHEST)
    conv_out = low_back(conv_out)
    residual = block_in + row_mask * jax.nn.gelu(conv_out, approximate=False)
    second = low(layer_norm(residual, vector_rows[3], vector_rows[4]))
    hidden = low_back(jnp.einsum('gpi,if->gpf', second, hidden_w, precision=HIGHEST) + hidden_b)
    active = low(jax.nn.gelu(hidden, approximate=False))
    mixed_out = low_back(jnp.einsum('gpf,fo->gpo', active, output_w, precision=HIGHEST))
    return residual + row_mask * (mixed_out + vector_rows[5])

def adam_step(weight, first_mom, second, gradient, clip_scale, step_rate, decay_rate):
    clipped = gradient * clip_scale
    first_new = BETA_ONE * first_mom + (1.0 - BETA_ONE) * clipped
    second_new = BETA_TWO * second + (1.0 - BETA_TWO) * clipped * clipped
    update_dir = first_new / (1.0 - BETA_ONE ** STEP) / (jnp.sqrt(second_new / (1.0 - BETA_TWO ** STEP)) + ADAM_EPS)
    return (weight - step_rate * (update_dir + decay_rate * weight), first_new, second_new)

def reference(inputs, cotangent, lengths, conv_master, hidden_master, output_master, conv_first, hidden_first, output_first, conv_second, hidden_second, output_second, vectors, vector_first, vector_second, hidden_bias, bias_first, bias_second):
    conv_w = conv_master.astype(jnp.bfloat16).astype(jnp.float32)
    hidden_w = hidden_master.astype(jnp.bfloat16).astype(jnp.float32)
    output_w = output_master.astype(jnp.bfloat16).astype(jnp.float32)
    groups = WIN // 4
    block_in = inputs.astype(jnp.float32).reshape(groups, 4, LEN, D)
    block_cot = cotangent.astype(jnp.float32).reshape(groups, 4, LEN, D)
    positions = jnp.arange(LEN, dtype=jnp.int32)
    row_masks = (positions[None, :] < lengths[:, None]).astype(jnp.float32).reshape(groups, 4, LEN, 1)

    def one_group(totals, group_item):
        group_in, group_cot, group_mask = group_item
        result, pullback = jax.vjp(partial(forward, row_mask=group_mask), conv_w, hidden_w, output_w, vectors, hidden_bias, group_in)
        gradients = pullback(group_cot)
        totals = jax.tree.map(jnp.add, totals, tuple(gradients[:5]))
        return (totals, (result.astype(jnp.bfloat16), gradients[5]))
    start = (jnp.zeros_like(conv_w), jnp.zeros_like(hidden_w), jnp.zeros_like(output_w), jnp.zeros_like(vectors), jnp.zeros_like(hidden_bias))
    totals, (outputs, input_grads) = lax.scan(one_group, start, (block_in, block_cot, row_masks))
    conv_grad, hidden_grad, output_grad, vector_grad, bias_grad = totals
    total_sq = jnp.sum(conv_grad * conv_grad) + jnp.sum(hidden_grad * hidden_grad) + jnp.sum(output_grad * output_grad) + jnp.sum(vector_grad * vector_grad) + jnp.sum(bias_grad * bias_grad)
    grad_norm = jnp.sqrt(total_sq)
    clip_scale = jnp.minimum(1.0, CLIP_NORM / (grad_norm + 1e-06))
    conv_new = adam_step(conv_master, conv_first, conv_second, conv_grad, clip_scale, MATRIX_RATE, WEIGHT_DECAY)
    hidden_new = adam_step(hidden_master, hidden_first, hidden_second, hidden_grad, clip_scale, MATRIX_RATE, WEIGHT_DECAY)
    output_new = adam_step(output_master, output_first, output_second, output_grad, clip_scale, MATRIX_RATE, WEIGHT_DECAY)
    vector_new = adam_step(vectors, vector_first, vector_second, vector_grad, clip_scale, VECTOR_RATE, 0.0)
    bias_new = adam_step(hidden_bias, bias_first, bias_second, bias_grad, clip_scale, VECTOR_RATE, 0.0)
    return (outputs.reshape(WIN, LEN, D), input_grads.reshape(WIN, LEN, D), grad_norm, conv_new[0], conv_new[1], conv_new[2], hidden_new[0], hidden_new[1], hidden_new[2], output_new[0], output_new[1], output_new[2], vector_new[0], vector_new[1], vector_new[2], bias_new[0], bias_new[1], bias_new[2])
```

```python
import functools

import jax
import jax.numpy as jnp
from jax import lax
from jax.experimental import pallas as pl
from jax.experimental.pallas import tpu as pltpu
from jax.sharding import PartitionSpec as P

KERNEL = 9
DILATION = 8
REACH = DILATION * (KERNEL // 2)
STEP = 10
ROWS = 256

NORM_EPS = 1e-05
BETA_ONE = 0.9
BETA_TWO = 0.999
ADAM_EPS = 1e-08
MATRIX_RATE = 0.03
VECTOR_RATE = 0.3
WEIGHT_DECAY = 0.01
CLIP_NORM = 1.0

f32 = jnp.float32
bf16 = jnp.bfloat16
NN = (((1,), (0,)), ((), ()))
NT = (((1,), (1,)), ((), ()))


def dot(a, b, dims=NN):
    return lax.dot_general(a, b, dims, preferred_element_type=f32)


def phi_of(v):
    return 0.5 * (1.0 + lax.erf(v * 0.7071067811865476))


def slope_of(v, phi):
    return phi + v * jnp.exp(-0.5 * v * v) * 0.3989422804014327


def norm_parts(v):
    centre = v - jnp.mean(v, axis=-1, keepdims=True)
    inverse = lax.rsqrt(jnp.mean(centre * centre, axis=-1, keepdims=True) + NORM_EPS)
    return centre * inverse, inverse


def norm_back(e, s, inverse):
    return inverse * (
        e - jnp.mean(e, axis=-1, keepdims=True) - s * jnp.mean(e * s, axis=-1, keepdims=True)
    )


def mult(v, n):
    return pl.multiple_of(v, n)


def dest_slot(place, d, m):
    dp, mp = place[0], place[1]
    fx = (dp & 1) ^ (d & 1)
    fy = (mp >> 1) ^ (m >> 1)
    dz = (dp >> 1) ^ (d >> 1)
    dc = (mp & 1) ^ (m & 1)
    flip = m & 1
    a = jnp.where(flip == 0, fx, fy)
    b = jnp.where(flip == 0, fy, fx)
    return dc, b, a, dz


def source_of(place, dc, b, a, dz):
    dp, mp = place[0], place[1]
    flip = (mp & 1) ^ dc
    fx = jnp.where(flip == 0, a, b)
    fy = jnp.where(flip == 0, b, a)
    d = ((dp >> 1) ^ dz) * 2 + ((dp & 1) ^ fx)
    m = ((mp >> 1) ^ fy) * 2 + ((mp & 1) ^ dc)
    return d, m


SLOTS = tuple((dc, b, a) for dc in (0, 1) for b, a in ((0, 0), (0, 1), (1, 0), (1, 1)))


def conv_forward(place, x0, x1, x2, x3, vec, *rest):
    pieces, (w_out, x_out, na_out, conv_out, nf, nab) = rest[:8], rest[8:]
    taps, di, own = pieces[0].shape[1:]
    full = vec.shape[1]
    length = place[2]
    blocks = place[3]

    def place_z(z, _):
        for (dc, b, a), piece in zip(SLOTS, pieces):
            d, m = source_of(place, dc, b, a, z)
            col = mult(m * own, own)
            for t in range(taps):
                row = mult(t * full + d * di, di)
                w_out[pl.ds(row, di), pl.ds(col, own)] = piece[z, t]
        return 0

    lax.fori_loop(0, pieces[0].shape[0], place_z, 0)
    for k, xk in enumerate((x0, x1, x2, x3)):
        x_out[:, pl.ds(mult((place[1] ^ k) * own, own), own)] = xk[...]

    nf[...] = jnp.zeros_like(nf)
    na_out[...] = jnp.zeros_like(na_out)
    conv_out[...] = jnp.zeros_like(conv_out)
    gain = vec[0:1, :]
    shift = vec[1:2, :]

    def norm_step(i, _):
        rows = pl.ds(mult(i * 128, 128), 128)
        scaled, _ = norm_parts(x_out[rows, :].astype(f32))
        nf[pl.ds(mult(i * 128 + REACH, 8), 128), :] = scaled * gain + shift
        return 0

    lax.fori_loop(0, blocks * (ROWS // 128), norm_step, 0)
    padded = nab.shape[1]

    def shift_step(i, _):
        row = mult(i * 64, 64)
        nab[0, pl.ds(row, 64), :] = nf[pl.ds(row, 64), :].astype(bf16)
        nab[1, pl.ds(row, 64), :] = nf[pl.ds(mult(row + 8, 8), 64), :].astype(bf16)
        return 0

    lax.fori_loop(0, padded // 64, shift_step, 0)

    def conv_step(i, _):
        row = mult(i * ROWS, ROWS)
        na_out[pl.ds(row, ROWS), :] = nab[0, pl.ds(mult(row + REACH, 32), ROWS), :]
        window = jnp.concatenate(
            [
                nab[t & 1, pl.ds(mult(row + DILATION * (t - (t & 1)), 16), ROWS), :]
                for t in range(KERNEL)
            ],
            axis=1,
        )
        conv_out[pl.ds(row, ROWS), :] = dot(window, w_out[...]) + vec[2:3, :]
        return 0

    lax.fori_loop(0, blocks, conv_step, 0)


def ffn(place, x_full, conv_out, c0, c1, c2, c3, vec, hbias, *rest):
    pieces = rest[:8]
    block_out, resid_out, cg_out, rsb, vgrad, hbgrad = rest[8:14]
    wh, wo, cot, act, hg, sec, mg = rest[14:]
    seq, full = x_full.shape
    hidden = wh.shape[1]
    di, part = pieces[0].shape[2:]
    own = c0.shape[1]
    blocks = place[3]

    def place_z(z, _):
        for (dc, b, a), piece in zip(SLOTS, pieces):
            d, m = source_of(place, dc, b, a, z)
            row = mult(d * di, di)
            col = mult(m * part, part)
            wh[pl.ds(row, di), pl.ds(col, part)] = piece[z, 0]
            wo[pl.ds(row, di), pl.ds(col, part)] = piece[z, 1]
        return 0

    lax.fori_loop(0, pieces[0].shape[0], place_z, 0)
    for k, ck in enumerate((c0, c1, c2, c3)):
        cot[:, pl.ds(mult((place[1] ^ k) * own, own), own)] = ck[...]
    vgrad[...] = jnp.zeros_like(vgrad)
    hbgrad[...] = jnp.zeros_like(hbgrad)

    def out_store(rows, values):
        for m in range(full // own):
            block_out[place[1] ^ m, rows, :] = values[:, m * own : (m + 1) * own]

    def row_step(i, _):
        rows = pl.ds(mult(i * ROWS, ROWS), ROWS)
        conv = conv_out[rows, :]
        residual = x_full[rows, :].astype(f32) + conv * phi_of(conv)
        s, inverse = norm_parts(residual)
        second = (s * vec[3:4, :] + vec[4:5, :]).astype(bf16)
        sec[rows, :] = second
        grad = cot[rows, :]
        mg[rows, :] = grad
        for j in range(hidden // 512):
            cols = slice(j * 512, (j + 1) * 512)
            h = dot(second, wh[:, cols]) + hbias[0:1, cols]
            phi = phi_of(h)
            act[rows, cols] = (h * phi).astype(bf16)
            hidden_grad = (dot(grad, wo[:, cols]) * slope_of(h, phi)).astype(bf16)
            hg[rows, cols] = hidden_grad
            hbgrad[0:1, cols] += jnp.sum(hidden_grad.astype(f32), axis=0, keepdims=True)
        mixed = dot(act[rows, :], wo[...], NT)
        out_store(rows, (residual + (mixed + vec[5:6, :])).astype(bf16))
        second_grad = dot(hg[rows, :], wh[...], NT)
        up = grad.astype(f32)
        vgrad[3:4, :] += jnp.sum(second_grad * s, axis=0, keepdims=True)
        vgrad[4:5, :] += jnp.sum(second_grad, axis=0, keepdims=True)
        vgrad[5:6, :] += jnp.sum(up, axis=0, keepdims=True)
        resid_grad = up + norm_back(second_grad * vec[3:4, :], s, inverse)
        resid_out[rows, :] = resid_grad
        conv = conv_out[rows, :]
        conv_grad = (resid_grad * slope_of(conv, phi_of(conv))).astype(bf16)
        cg_out[rows, :] = conv_grad
        vgrad[2:3, :] += jnp.sum(conv_grad.astype(f32), axis=0, keepdims=True)
        return 0

    def idle_step(i, _):
        rows = pl.ds(mult(i * ROWS, ROWS), ROWS)
        out_store(rows, x_full[rows, :])
        resid_out[rows, :] = cot[rows, :].astype(f32)
        for ref in (cg_out, sec, mg):
            ref[rows, :] = jnp.zeros((ROWS, full), bf16)
        for ref in (act, hg):
            ref[rows, :] = jnp.zeros((ROWS, hidden), bf16)
        return 0

    lax.fori_loop(0, blocks, row_step, 0)
    lax.fori_loop(blocks, seq // ROWS, idle_step, 0)

    sec_t = sec[...].T
    mg_t = mg[...].T
    for m in range(hidden // part):
        cols = slice(m * part, (m + 1) * part)
        for w, (left, right) in enumerate(((sec_t, hg), (mg_t, act))):
            value = dot(left, right[:, cols]).astype(bf16)
            for d in range(full // di):
                dc, b, a, dz = dest_slot(place, d, m)
                rsb[dc, b, a, dz, w] = value[d * di : (d + 1) * di, :]


def conv_backward(place, x_full, na, cg, resid, w, vec, *rest):
    in_grad, rsb, vgrad, cf, cab = rest
    seq, full = x_full.shape
    taps, di, own = rsb.shape[4:]
    blocks = place[3]
    vgrad[...] = jnp.zeros_like(vgrad)
    cf[...] = jnp.zeros_like(cf)

    def widen(i, _):
        row = mult(i * 128, 128)
        cf[pl.ds(mult(row + REACH, 8), 128), :] = cg[pl.ds(row, 128), :].astype(f32)
        return 0

    lax.fori_loop(0, seq // 128, widen, 0)

    def shift_step(i, _):
        row = mult(i * 64, 64)
        cab[0, pl.ds(row, 64), :] = cf[pl.ds(row, 64), :].astype(bf16)
        cab[1, pl.ds(row, 64), :] = cf[pl.ds(mult(row + 8, 8), 64), :].astype(bf16)
        return 0

    lax.fori_loop(0, cab.shape[1] // 64, shift_step, 0)

    def in_store(rows, values):
        values = values.astype(bf16)
        for m in range(full // own):
            in_grad[place[1] ^ m, rows, :] = values[:, m * own : (m + 1) * own]

    def row_step(i, _):
        row = mult(i * ROWS, ROWS)
        rows = pl.ds(row, ROWS)
        total = jnp.zeros((ROWS, full), f32)
        for t in range(KERNEL):
            u = KERNEL - 1 - t
            shifted = cab[u & 1, pl.ds(mult(row + DILATION * (u - (u & 1)), 16), ROWS), :]
            total = total + dot(shifted, w[t * full : (t + 1) * full, :], NT)
        s, inverse = norm_parts(x_full[rows, :].astype(f32))
        vgrad[0:1, :] += jnp.sum(total * s, axis=0, keepdims=True)
        vgrad[1:2, :] += jnp.sum(total, axis=0, keepdims=True)
        in_store(rows, resid[rows, :] + norm_back(total * vec[0:1, :], s, inverse))
        return 0

    def idle_step(i, _):
        rows = pl.ds(mult(i * ROWS, ROWS), ROWS)
        in_store(rows, resid[rows, :])
        return 0

    lax.fori_loop(0, blocks, row_step, 0)
    lax.fori_loop(blocks, seq // ROWS, idle_step, 0)

    na_t = na[...].T

    def tap_step(t, _):
        u = KERNEL - 1 - t
        odd = u & 1
        shifted = cab[odd, pl.ds(mult((u - odd) * DILATION, 16), seq), :]
        value = dot(na_t, shifted).astype(bf16)
        for d in range(full // di):
            for m in range(full // own):
                dc, b, a, dz = dest_slot(place, d, m)
                rsb[dc, b, a, dz, t] = value[d * di : (d + 1) * di, m * own : (m + 1) * own]
        return 0

    lax.fori_loop(0, KERNEL, tap_step, 0)


def call(kernel, place, args, outs, scratch, flops, mib):
    spec = pl.BlockSpec(memory_space=pltpu.VMEM)
    moved = sum(a.size * a.dtype.itemsize for a in (*args, *outs))
    return pl.pallas_call(
        kernel,
        out_shape=outs,
        in_specs=[pl.BlockSpec(memory_space=pltpu.SMEM)] + [spec] * len(args),
        out_specs=[spec] * len(outs),
        scratch_shapes=scratch,
        compiler_params=pltpu.CompilerParams(vmem_limit_bytes=mib * 2**20),
        cost_estimate=pl.CostEstimate(flops=flops, bytes_accessed=moved, transcendentals=0),
    )(place, *args)


def adam_step(weight, first_mom, second, gradient, clip_scale, step_rate, decay_rate):
    clipped = gradient * clip_scale
    first_new = BETA_ONE * first_mom + (1.0 - BETA_ONE) * clipped
    second_new = BETA_TWO * second + (1.0 - BETA_TWO) * clipped * clipped
    update_dir = (
        first_new
        / (1.0 - BETA_ONE**STEP)
        / (jnp.sqrt(second_new / (1.0 - BETA_TWO**STEP)) + ADAM_EPS)
    )
    return (weight - step_rate * (update_dir + decay_rate * weight), first_new, second_new)


def square_sum(values):
    return jnp.sum(values * values)


def per_device(
    ndp,
    nmp,
    inputs,
    cotangent,
    lengths,
    conv_master,
    hidden_master,
    output_master,
    conv_first,
    hidden_first,
    output_first,
    conv_second,
    hidden_second,
    output_second,
    vectors,
    vector_first,
    vector_second,
    hidden_bias,
    bias_first,
    bias_second,
):
    axes = ("dp", "mp")
    nz = ndp // 2
    seq, own = inputs.shape[1:]
    full = vectors.shape[1]
    part = hidden_bias.shape[0]
    hidden = part * nmp
    di = full // ndp
    dp, mp = lax.axis_index("dp"), lax.axis_index("mp")

    def perm(move):
        pairs = []
        for i in range(ndp * nmp):
            d, m = divmod(i, nmp)
            z, x, y, c = move(d >> 1, d & 1, m >> 1, m & 1)
            pairs.append((i, (z * 2 + x) * nmp + y * 2 + c))
        return pairs

    across_z = [perm(lambda z, x, y, c, k=k: (z ^ k, x, y, c)) for k in range(nz)]
    step_a = perm(lambda z, x, y, c: (z, x ^ 1, y, c) if c == 0 else (z, x, y ^ 1, c))
    step_b = perm(lambda z, x, y, c: (z, x, y ^ 1, c) if c == 0 else (z, x ^ 1, y, c))
    step_c = perm(lambda z, x, y, c: (z, x, y, c ^ 1))
    within = [[(i, i ^ k) for i in range(nmp)] for k in range(nmp)]

    def send(values, pairs):
        return lax.ppermute(values, axes, pairs)

    def gather(shard):
        flat = jnp.stack([shard] + [send(shard, across_z[k]) for k in range(1, nz)])
        part_a, part_b = send(flat, step_a), send(flat, step_b)
        mine = [flat, part_a, part_b, send(part_a, step_b)]
        return mine + [send(t, step_c) for t in mine]

    def scatter(parts):
        parts = parts[0].astype(f32) + send(parts[1], step_c).astype(f32)
        parts = parts[0] + send(parts[1].astype(bf16), step_b).astype(f32)
        parts = parts[0] + send(parts[1].astype(bf16), step_a).astype(f32)
        low = parts.astype(bf16)
        total = parts[0]
        for k in range(1, nz):
            total = total + send(low[k], across_z[k]).astype(f32)
        return total

    def to_windows(values):
        blocks = [lax.dynamic_index_in_dim(values, mp ^ k, 0, False) for k in range(nmp)]
        return [blocks[0]] + [lax.ppermute(blocks[k], "mp", within[k]) for k in range(1, nmp)]

    def to_columns(values):
        pieces = [values[0]] + [lax.ppermute(values[k], "mp", within[k]) for k in range(1, nmp)]
        for bit in range(nmp.bit_length() - 1):
            odd = ((mp >> bit) & 1) == 1
            pieces = [jnp.where(odd, pieces[k ^ (1 << bit)], pieces[k]) for k in range(nmp)]
        return jnp.stack(pieces)

    def all_sum(values):
        for pairs in (step_c, step_a, step_b):
            values = values + send(values, pairs)
        step = 1
        while step < nz:
            values = values + send(values, across_z[step])
            step *= 2
        return values

    length = lax.dynamic_index_in_dim(lengths, mp, 0, False)
    place = jnp.stack([dp, mp, length, length // ROWS]).astype(jnp.int32)
    x_parts = to_windows(inputs)
    conv_parts = gather(conv_master.astype(bf16))
    c_parts = to_windows(cotangent)
    ffn_parts = gather(jnp.stack([hidden_master.astype(bf16), output_master.astype(bf16).T]))
    vec = jnp.concatenate([vectors, jnp.zeros((2, full), f32)])
    bias_parts = [hidden_bias] + [lax.ppermute(hidden_bias, "mp", within[k]) for k in range(1, nmp)]
    bias_all = to_columns_local(bias_parts, mp, nmp).reshape(1, hidden)

    S = jax.ShapeDtypeStruct
    padded = seq + 2 * REACH
    w_full, x_full, normed, conv_out = call(
        conv_forward,
        place,
        (*x_parts, vec, *conv_parts),
        (
            S((KERNEL * full, full), bf16),
            S((seq, full), bf16),
            S((seq, full), bf16),
            S((seq, full), f32),
        ),
        [pltpu.VMEM((padded + 8, full), f32), pltpu.VMEM((2, padded, full), bf16)],
        2 * seq * KERNEL * full * full,
        40,
    )
    block_rel, resid_grad, conv_grad, ffn_send, vgrad_two, bias_grad = call(
        ffn,
        place,
        (x_full, conv_out, *c_parts, vec, bias_all, *ffn_parts),
        (
            S((nmp, seq, own), bf16),
            S((seq, full), f32),
            S((seq, full), bf16),
            S((2, 2, 2, nz, 2, di, part), bf16),
            S((8, full), f32),
            S((1, hidden), f32),
        ),
        [
            pltpu.VMEM((full, hidden), bf16),
            pltpu.VMEM((full, hidden), bf16),
            pltpu.VMEM((seq, full), bf16),
            pltpu.VMEM((seq, hidden), bf16),
            pltpu.VMEM((seq, hidden), bf16),
            pltpu.VMEM((seq, full), bf16),
            pltpu.VMEM((seq, full), bf16),
        ],
        12 * seq * hidden * full,
        56,
    )
    in_rel, conv_send, vgrad_one = call(
        conv_backward,
        place,
        (x_full, normed, conv_grad, resid_grad, w_full, vec),
        (
            S((nmp, seq, own), bf16),
            S((2, 2, 2, nz, KERNEL, di, own), bf16),
            S((8, full), f32),
        ),
        [pltpu.VMEM((padded + 8, full), f32), pltpu.VMEM((2, padded, full), bf16)],
        4 * seq * KERNEL * full * full,
        48,
    )
    block_output = to_columns(block_rel)
    ffn_share = scatter(ffn_send)
    conv_share = scatter(conv_send)
    input_grad = to_columns(in_rel).astype(f32)

    small = all_sum(
        jnp.concatenate([(vgrad_one + vgrad_two)[:6], bias_grad.reshape(hidden // full, full)])
    )
    vector_sum, bias_sum = small[:6], small[6:].reshape(hidden)
    hidden_share, output_share = ffn_share[0], ffn_share[1].T
    squares = square_sum(conv_share) + square_sum(ffn_share)
    squares_all = all_sum(jnp.broadcast_to(squares, (8, 128)))[0, 0]
    grad_norm = jnp.sqrt(squares_all + square_sum(small))
    clip_scale = jnp.minimum(1.0, CLIP_NORM / (grad_norm + 1e-06))
    bias_share = lax.dynamic_slice_in_dim(bias_sum, mp * part, part, 0)
    matrices = (
        (conv_master, conv_first, conv_second, conv_share),
        (hidden_master, hidden_first, hidden_second, hidden_share),
        (output_master, output_first, output_second, output_share),
    )
    small_ones = (
        (vectors, vector_first, vector_second, vector_sum),
        (hidden_bias, bias_first, bias_second, bias_share),
    )
    updated = [adam_step(*m, clip_scale, MATRIX_RATE, WEIGHT_DECAY) for m in matrices]
    updated += [adam_step(*m, clip_scale, VECTOR_RATE, 0.0) for m in small_ones]
    return (block_output, input_grad, grad_norm, *(leaf for new in updated for leaf in new))


def to_columns_local(pieces, mp, nmp):
    for bit in range(nmp.bit_length() - 1):
        odd = ((mp >> bit) & 1) == 1
        pieces = [jnp.where(odd, pieces[k ^ (1 << bit)], pieces[k]) for k in range(nmp)]
    return jnp.stack(pieces)


def solution(mesh):
    rows = P("dp", None, "mp")
    conv = P(None, "dp", "mp")
    hid = P("dp", "mp")
    out = P("mp", "dp")
    return jax.shard_map(
        functools.partial(per_device, mesh.shape["dp"], mesh.shape["mp"]),
        mesh=mesh,
        in_specs=(rows, rows, P("dp"), *(conv, hid, out) * 3, *(P(),) * 3, *(P("mp"),) * 3),
        out_specs=(
            rows,
            rows,
            P(),
            *(conv,) * 3,
            *(hid,) * 3,
            *(out,) * 3,
            *(P(),) * 3,
            *(P("mp"),) * 3,
        ),
        check_vma=False,
    )
```

```python
import functools

import jax
import jax.numpy as jnp
from jax import lax
from jax.experimental import pallas as pl
from jax.experimental.pallas import tpu as pltpu
from jax.sharding import PartitionSpec as P

KERNEL = 9
DILATION = 8
REACH = DILATION * (KERNEL // 2)
STEP = 10
ROWS = 256

NORM_EPS = 1e-05
BETA_ONE = 0.9
BETA_TWO = 0.999
ADAM_EPS = 1e-08
MATRIX_RATE = 0.03
VECTOR_RATE = 0.3
WEIGHT_DECAY = 0.01
CLIP_NORM = 1.0

f32 = jnp.float32
bf16 = jnp.bfloat16
NN = (((1,), (0,)), ((), ()))
NT = (((1,), (1,)), ((), ()))


def dot(a, b, dims=NN):
    return lax.dot_general(a, b, dims, preferred_element_type=f32)


def phi_of(v):
    return 0.5 * (1.0 + lax.erf(v * 0.7071067811865476))


def slope_of(v, phi):
    return phi + v * jnp.exp(-0.5 * v * v) * 0.3989422804014327


def norm_parts(v):
    centre = v - jnp.mean(v, axis=-1, keepdims=True)
    inverse = lax.rsqrt(jnp.mean(centre * centre, axis=-1, keepdims=True) + NORM_EPS)
    return centre * inverse, inverse


def norm_back(e, s, inverse):
    return inverse * (
        e - jnp.mean(e, axis=-1, keepdims=True) - s * jnp.mean(e * s, axis=-1, keepdims=True)
    )


def mult(v, n):
    return pl.multiple_of(v, n)


def relative(place, d, m, plain):
    dp, mp = place[0], place[1]
    fx = (dp & 1) ^ (d & 1)
    fy = (mp >> 1) ^ (m >> 1)
    dz = (dp >> 1) ^ (d >> 1)
    if plain or (m & 1):
        return fx, fy, dz
    return fy, fx, dz


def source_of(place, dc, b, a, dz, plain):
    dp, mp = place[0], place[1]
    if plain:
        fx, fy = b, a
    else:
        flip = (mp & 1) ^ dc
        fx = jnp.where(flip == 0, a, b)
        fy = jnp.where(flip == 0, b, a)
    d = ((dp >> 1) ^ dz) * 2 + ((dp & 1) ^ fx)
    m = ((mp >> 1) ^ fy) * 2 + ((mp & 1) ^ dc)
    return d, m


def store_shares(place, keep, give, m, plain, devices, store):
    same = (place[1] & 1) == (m & 1)

    @pl.when(same)
    def _():
        for d in range(devices):
            store(keep, relative(place, d, m, plain), d)

    @pl.when(jnp.logical_not(same))
    def _():
        for d in range(devices):
            store(give, relative(place, d, m, plain), d)


SLOTS = tuple((dc, b, a) for dc in (0, 1) for b, a in ((0, 0), (0, 1), (1, 0), (1, 1)))


def fetch(place, x_parts, x_full, x_sem, pieces, whole, sems):
    seq, own = x_full.shape[0], x_parts[0].shape[1]
    di, cols = pieces[0].shape[2:]
    rows = []
    for k, part in enumerate(x_parts):
        target = x_full.at[:, pl.ds(mult((place[1] ^ k) * own, own), own)]
        rows.append(pltpu.make_async_copy(part.at[pl.ds(0, seq), :], target, x_sem.at[k]))
        rows[-1].start()
    shards = []
    for slot, ((dc, b, a), piece) in enumerate(zip(SLOTS, pieces)):
        for z in range(piece.shape[0]):
            d, m = source_of(place, dc, b, a, z, False)
            target = whole.at[:, pl.ds(mult(d * di, di), di), pl.ds(mult(m * cols, cols), cols)]
            shards.append(pltpu.make_async_copy(piece.at[z], target, sems.at[slot, z]))
            shards[-1].start()
    return rows, shards


def conv_forward(place, x0, x1, x2, x3, vec, *rest):
    pieces = rest[:8]
    w_out, x_out, na_out, conv_out, bias_out, nf, nab, whole, extra, sems, x_sem = rest[8:]
    full = vec.shape[1]
    seq, own = x_out.shape[0], x0.shape[1]
    length = place[2]
    blocks = place[3]

    x_parts = (x0, x1, x2, x3)
    rows, shards = fetch(place, x_parts, x_out, x_sem.at[0], pieces, whole, sems)
    extras = [
        pltpu.make_async_copy(part.at[pl.ds(seq, extra.shape[1]), :], extra.at[k], x_sem.at[1, k])
        for k, part in enumerate(x_parts)
    ]
    for copy in extras:
        copy.start()
    for copy in rows + extras:
        copy.wait()
    for k in range(len(x_parts)):
        values = extra[k].astype(f32)
        units = values.shape[0] // 4
        bias_out[place[1] ^ k] = (values[0:units] + values[units : 2 * units]) + values[
            2 * units : 3 * units
        ]

    nf[...] = jnp.zeros_like(nf)
    na_out[...] = jnp.zeros_like(na_out)
    conv_out[...] = jnp.zeros_like(conv_out)
    gain = vec[0:1, :]
    shift = vec[1:2, :]

    def norm_step(i, _):
        rows = pl.ds(mult(i * 128, 128), 128)
        scaled, _ = norm_parts(x_out[rows, :].astype(f32))
        nf[pl.ds(mult(i * 128 + REACH, 8), 128), :] = scaled * gain + shift
        return 0

    lax.fori_loop(0, blocks * (ROWS // 128), norm_step, 0)
    padded = nab.shape[1]

    def shift_step(i, _):
        row = mult(i * 64, 64)
        nab[0, pl.ds(row, 64), :] = nf[pl.ds(row, 64), :].astype(bf16)
        nab[1, pl.ds(row, 64), :] = nf[pl.ds(mult(row + 8, 8), 64), :].astype(bf16)
        return 0

    lax.fori_loop(0, padded // 64, shift_step, 0)
    for copy in shards:
        copy.wait()
    w_copy = pltpu.make_async_copy(whole, w_out, x_sem.at[2, 0])
    w_copy.start()

    def conv_step(i, _):
        row = mult(i * ROWS, ROWS)
        na_out[pl.ds(row, ROWS), :] = nab[0, pl.ds(mult(row + REACH, 32), ROWS), :]
        window = jnp.concatenate(
            [
                nab[t & 1, pl.ds(mult(row + DILATION * (t - (t & 1)), 16), ROWS), :]
                for t in range(KERNEL)
            ],
            axis=1,
        )
        weights = whole[...].reshape(KERNEL * full, full)
        conv_out[pl.ds(row, ROWS), :] = dot(window, weights) + vec[2:3, :]
        return 0

    lax.fori_loop(0, blocks, conv_step, 0)
    w_copy.wait()


def ffn(place, x_full, conv_out, c0, c1, c2, c3, vec, hbias, *rest):
    pieces = rest[:8]
    block_out, resid_out, cab, keep, give, vgrad, hbgrad = rest[8:15]
    whole, cot, act, hg, sec, mg, cf, sems, c_sem = rest[15:]
    wh, wo = whole.at[0], whole.at[1]
    seq, full = x_full.shape
    hidden = hbias.shape[1]
    di, part = pieces[0].shape[2:]
    own = c0.shape[1]
    blocks = place[3]

    rows, shards = fetch(place, (c0, c1, c2, c3), cot, c_sem.at[0], pieces, whole, sems)
    vgrad[...] = jnp.zeros_like(vgrad)
    hbgrad[...] = jnp.zeros_like(hbgrad)
    cf[...] = jnp.zeros_like(cf)
    for copy in rows + shards:
        copy.wait()

    def out_store(rows, values):
        for m in range(full // own):
            block_out[place[1] ^ m, rows, :] = values[:, m * own : (m + 1) * own]

    def row_step(i, _):
        rows = pl.ds(mult(i * ROWS, ROWS), ROWS)
        conv = conv_out[rows, :]
        residual = x_full[rows, :].astype(f32) + conv * phi_of(conv)
        s, inverse = norm_parts(residual)
        second = (s * vec[3:4, :] + vec[4:5, :]).astype(bf16)
        sec[rows, :] = second
        grad = cot[rows, :]
        mg[rows, :] = grad
        for j in range(hidden // 512):
            cols = slice(j * 512, (j + 1) * 512)
            h = dot(second, wh[:, cols]) + hbias[0:1, cols]
            phi = phi_of(h)
            act[rows, cols] = (h * phi).astype(bf16)
            hidden_grad = (dot(grad, wo[:, cols]) * slope_of(h, phi)).astype(bf16)
            hg[rows, cols] = hidden_grad
            hbgrad[0:1, cols] += jnp.sum(hidden_grad.astype(f32), axis=0, keepdims=True)
        mixed = dot(act[rows, :], wo[...], NT)
        out_store(rows, (residual + (mixed + vec[5:6, :])).astype(bf16))
        second_grad = dot(hg[rows, :], wh[...], NT)
        up = grad.astype(f32)
        vgrad[3:4, :] += jnp.sum(second_grad * s, axis=0, keepdims=True)
        vgrad[4:5, :] += jnp.sum(second_grad, axis=0, keepdims=True)
        vgrad[5:6, :] += jnp.sum(up, axis=0, keepdims=True)
        resid_grad = up + norm_back(second_grad * vec[3:4, :], s, inverse)
        resid_out[rows, :] = resid_grad
        conv = conv_out[rows, :]
        conv_grad = (resid_grad * slope_of(conv, phi_of(conv))).astype(bf16)
        rounded = conv_grad.astype(f32)
        cf[pl.ds(mult(i * ROWS + REACH, 8), ROWS), :] = rounded
        vgrad[2:3, :] += jnp.sum(rounded, axis=0, keepdims=True)
        return 0

    def idle_step(i, _):
        rows = pl.ds(mult(i * ROWS, ROWS), ROWS)
        out_store(rows, x_full[rows, :])
        resid_out[rows, :] = cot[rows, :].astype(f32)
        for ref in (sec, mg):
            ref[rows, :] = jnp.zeros((ROWS, full), bf16)
        for ref in (act, hg):
            ref[rows, :] = jnp.zeros((ROWS, hidden), bf16)
        return 0

    lax.fori_loop(0, blocks, row_step, 0)
    lax.fori_loop(blocks, seq // ROWS, idle_step, 0)

    def shift_step(i, _):
        row = mult(i * 64, 64)
        cab[0, pl.ds(row, 64), :] = cf[pl.ds(row, 64), :].astype(bf16)
        cab[1, pl.ds(row, 64), :] = cf[pl.ds(mult(row + 8, 8), 64), :].astype(bf16)
        return 0

    lax.fori_loop(0, cab.shape[1] // 64, shift_step, 0)

    sec_t = sec[...].T
    mg_t = mg[...].T
    for m in range(hidden // part):
        cols = slice(m * part, (m + 1) * part)
        for w, (left, right) in enumerate(((sec_t, hg), (mg_t, act))):
            value = dot(left, right[:, cols]).astype(bf16)

            def store(ref, index, d):
                ref[(*index, w)] = value[d * di : (d + 1) * di, :]

            store_shares(place, keep, give, m, False, full // di, store)


def shifted_rows(cab, u, row, count):
    odd = u & 1
    return cab[odd, pl.ds(mult(row + (u - odd) * DILATION, 16), count), :]


def conv_weight_grad(place, na, cab, keep, give):
    seq, full = na.shape
    taps, di, own = keep.shape[3:]
    na_t = na[...].T

    def tap_step(t, _):
        value = dot(na_t, shifted_rows(cab, KERNEL - 1 - t, 0, seq)).astype(bf16)
        for m in range(full // own):

            def store(ref, index, d):
                ref[(*index, t)] = value[d * di : (d + 1) * di, m * own : (m + 1) * own]

            store_shares(place, keep, give, m, False, full // di, store)
        return 0

    lax.fori_loop(0, taps, tap_step, 0)


def conv_backward(place, x_full, cab, resid, w, vec, in_grad, vgrad):
    seq, full = x_full.shape
    own = in_grad.shape[2]
    blocks = place[3]
    vgrad[...] = jnp.zeros_like(vgrad)

    def in_store(rows, values):
        values = values.astype(bf16)
        for m in range(full // own):
            in_grad[place[1] ^ m, rows, :] = values[:, m * own : (m + 1) * own]

    def row_step(i, _):
        row = mult(i * ROWS, ROWS)
        rows = pl.ds(row, ROWS)
        total = jnp.zeros((ROWS, full), f32)
        for t in range(KERNEL):
            shifted = shifted_rows(cab, KERNEL - 1 - t, row, ROWS)
            total = total + dot(shifted, w[t], NT)
        s, inverse = norm_parts(x_full[rows, :].astype(f32))
        vgrad[0:1, :] += jnp.sum(total * s, axis=0, keepdims=True)
        vgrad[1:2, :] += jnp.sum(total, axis=0, keepdims=True)
        in_store(rows, resid[rows, :] + norm_back(total * vec[0:1, :], s, inverse))
        return 0

    def idle_step(i, _):
        rows = pl.ds(mult(i * ROWS, ROWS), ROWS)
        in_store(rows, resid[rows, :])
        return 0

    lax.fori_loop(0, blocks, row_step, 0)
    lax.fori_loop(blocks, seq // ROWS, idle_step, 0)


def tie(*values):
    return lax.optimization_barrier(values)


def call(kernel, place, args, outs, scratch, flops, mib, far=(), far_out=()):
    near = pl.BlockSpec(memory_space=pltpu.VMEM)
    left = pl.BlockSpec(memory_space=pl.ANY)
    moved = sum(a.size * a.dtype.itemsize for a in (*args, *outs))
    return pl.pallas_call(
        kernel,
        out_shape=outs,
        in_specs=[pl.BlockSpec(memory_space=pltpu.SMEM)]
        + [left if i in far else near for i in range(len(args))],
        out_specs=[left if i in far_out else near for i in range(len(outs))],
        scratch_shapes=scratch,
        compiler_params=pltpu.CompilerParams(vmem_limit_bytes=mib * 2**20),
        cost_estimate=pl.CostEstimate(flops=flops, bytes_accessed=moved, transcendentals=0),
    )(place, *args)


def adam_step(weight, first_mom, second, gradient, clip_scale, step_rate, decay_rate):
    clipped = gradient * clip_scale
    first_new = BETA_ONE * first_mom + (1.0 - BETA_ONE) * clipped
    second_new = BETA_TWO * second + (1.0 - BETA_TWO) * clipped * clipped
    update_dir = (
        first_new
        / (1.0 - BETA_ONE**STEP)
        / (jnp.sqrt(second_new / (1.0 - BETA_TWO**STEP)) + ADAM_EPS)
    )
    return (weight - step_rate * (update_dir + decay_rate * weight), first_new, second_new)


def square_sum(values):
    return jnp.sum(values * values)


def per_device(
    ndp,
    nmp,
    inputs,
    cotangent,
    lengths,
    conv_master,
    hidden_master,
    output_master,
    conv_first,
    hidden_first,
    output_first,
    conv_second,
    hidden_second,
    output_second,
    vectors,
    vector_first,
    vector_second,
    hidden_bias,
    bias_first,
    bias_second,
):
    axes = ("dp", "mp")
    nz = ndp // 2
    seq, own = inputs.shape[1:]
    full = vectors.shape[1]
    part = hidden_bias.shape[0]
    hidden = part * nmp
    di = full // ndp
    dp, mp = lax.axis_index("dp"), lax.axis_index("mp")

    def perm(move):
        pairs = []
        for i in range(ndp * nmp):
            d, m = divmod(i, nmp)
            z, x, y, c = move(d >> 1, d & 1, m >> 1, m & 1)
            pairs.append((i, (z * 2 + x) * nmp + y * 2 + c))
        return pairs

    across_z = [perm(lambda z, x, y, c, k=k: (z ^ k, x, y, c)) for k in range(nz)]
    step_x = perm(lambda z, x, y, c: (z, x ^ 1, y, c))
    step_y = perm(lambda z, x, y, c: (z, x, y ^ 1, c))
    step_c = perm(lambda z, x, y, c: (z, x, y, c ^ 1))
    step_xy = perm(lambda z, x, y, c: (z, x ^ 1, y, c) if c == 0 else (z, x, y ^ 1, c))
    step_yx = perm(lambda z, x, y, c: (z, x, y ^ 1, c) if c == 0 else (z, x ^ 1, y, c))
    within = [[(i, i ^ k) for i in range(nmp)] for k in range(nmp)]

    def send(values, pairs):
        return lax.ppermute(values, axes, pairs)

    def gather_z(shard):
        return [shard] + [send(shard, across_z[k]) for k in range(1, nz)]

    def add(*terms):
        total = terms[0].astype(f32)
        for term in terms[1:]:
            total = total + term.astype(f32)
        return total

    def scatter_b(k, r):
        return add(k[1], r[1]).astype(bf16)

    def scatter_a(k, r, rb):
        return add(k[0, 1], r[0, 1], rb[1]).astype(bf16)

    def scatter_z(k, r, rb, ra):
        total = add(k[0, 0, 0], r[0, 0, 0], rb[0, 0], ra[0])
        for j in range(1, nz):
            part = add(k[0, 0, j], r[0, 0, j], rb[0, j], ra[j]).astype(bf16)
            total = total + send(part, across_z[j]).astype(f32)
        return total

    def take_windows(values, extra=None):
        blocks = [lax.dynamic_index_in_dim(values, mp ^ k, 0, False) for k in range(nmp)]
        if extra is not None:
            blocks = [jnp.concatenate([block, extra]) for block in blocks]
        return blocks

    def swap(blocks):
        return [blocks[0]] + [lax.ppermute(blocks[k], "mp", within[k]) for k in range(1, nmp)]

    def in_order(pieces):
        for bit in range(nmp.bit_length() - 1):
            odd = ((mp >> bit) & 1) == 1
            pieces = [jnp.where(odd, pieces[k ^ (1 << bit)], pieces[k]) for k in range(nmp)]
        return jnp.stack(pieces)

    def all_sum(values, other):
        values = values + send(values, step_c)
        step = 1
        while step < nz:
            values = values + send(values, across_z[step])
            step *= 2
        values = values + send(values, step_x)
        values, other = tie(values, other)
        return values + send(values, step_y), other

    length = lax.dynamic_index_in_dim(lengths, mp, 0, False)
    place = jnp.stack([dp, mp, length, length // ROWS]).astype(jnp.int32)
    exact, rest = [], hidden_bias
    for _ in range(3):
        exact.append(lax.reduce_precision(rest, 8, 7))
        rest = rest - exact[-1]
    exact.append(jnp.zeros_like(rest))
    exact = jnp.concatenate(exact).reshape(4 * part // own, own).astype(bf16)
    vec = jnp.concatenate([vectors, jnp.zeros((2, full), f32)])
    ffn_shard = jnp.stack([hidden_master.astype(bf16), output_master.astype(bf16).T])

    x_blocks = take_windows(inputs, exact)
    *x_blocks, conv_shard = tie(*x_blocks, conv_master.astype(bf16))
    x_parts = swap(x_blocks)
    conv_z = gather_z(conv_shard)
    *tied, ffn_shard = tie(*x_parts, *conv_z, ffn_shard)
    x_parts, conv_z = tied[:nmp], jnp.stack(tied[nmp:])
    conv_a, conv_b = send(conv_z, step_xy), send(conv_z, step_yx)
    ffn_z = gather_z(ffn_shard)
    conv_z, conv_a, conv_b, *ffn_z = tie(conv_z, conv_a, conv_b, *ffn_z)
    ffn_z = jnp.stack(ffn_z)
    conv_ab = send(conv_a, step_yx)
    conv_far = [send(part_of, step_c) for part_of in (conv_z, conv_a, conv_b)]
    conv_ab, cotangent, *conv_far = tie(conv_ab, cotangent, *conv_far)
    conv_parts = [conv_z, conv_a, conv_b, conv_ab, *conv_far, send(conv_ab, step_c)]
    ffn_a, ffn_b = send(ffn_z, step_xy), send(ffn_z, step_yx)
    c_parts = swap(take_windows(cotangent))

    S = jax.ShapeDtypeStruct
    padded = seq + 2 * REACH
    ffn_a, *x_parts = tie(ffn_a, *x_parts)
    w_full, x_full, normed, conv_out, bias_all = call(
        conv_forward,
        place,
        (*x_parts, vec, *conv_parts),
        (
            S((KERNEL, full, full), bf16),
            S((seq, full), bf16),
            S((seq, full), bf16),
            S((seq, full), f32),
            S((nmp, part // own, own), f32),
        ),
        [
            pltpu.VMEM((padded + 8, full), f32),
            pltpu.VMEM((2, padded, full), bf16),
            pltpu.VMEM((KERNEL, full, full), bf16),
            pltpu.VMEM((nmp, 4 * part // own, own), bf16),
            pltpu.SemaphoreType.DMA((8, nz)),
            pltpu.SemaphoreType.DMA((3, nmp)),
        ],
        2 * seq * KERNEL * full * full,
        24,
        (0, 1, 2, 3, *range(5, 13)),
        (0,),
    )
    ffn_ab = send(ffn_a, step_yx)
    *tied, conv_out = tie(ffn_z, ffn_a, ffn_b, ffn_ab, *c_parts, conv_out)
    ffn_parts, c_parts = tied[:4], tied[4:]
    ffn_parts += [send(part_of, step_c) for part_of in ffn_parts]
    block_rel, resid_grad, conv_grad, ffn_keep, ffn_give, vgrad_two, bias_grad = call(
        ffn,
        place,
        (x_full, conv_out, *c_parts, vec, bias_all.reshape(1, hidden), *ffn_parts),
        (
            S((nmp, seq, own), bf16),
            S((seq, full), f32),
            S((2, padded, full), bf16),
            *(S((2, 2, nz, 2, di, part), bf16),) * 2,
            S((8, full), f32),
            S((1, hidden), f32),
        ),
        [
            pltpu.VMEM((2, full, hidden), bf16),
            pltpu.VMEM((seq, full), bf16),
            pltpu.VMEM((seq, hidden), bf16),
            pltpu.VMEM((seq, hidden), bf16),
            pltpu.VMEM((seq, full), bf16),
            pltpu.VMEM((seq, full), bf16),
            pltpu.VMEM((padded + 8, full), f32),
            pltpu.SemaphoreType.DMA((8, nz)),
            pltpu.SemaphoreType.DMA((1, nmp)),
        ],
        12 * seq * hidden * full,
        44,
        (2, 3, 4, 5, *range(8, 16)),
    )
    ffn_r = send(ffn_give, step_c)
    ffn_sum, conv_grad = tie(scatter_b(ffn_keep, ffn_r), conv_grad)
    ffn_rb = send(ffn_sum, step_yx)
    conv_keep, conv_give = call(
        conv_weight_grad,
        place,
        (normed, conv_grad),
        (S((2, 2, nz, KERNEL, di, own), bf16),) * 2,
        [],
        2 * seq * KERNEL * full * full,
        16,
    )
    conv_give, ffn_rb, conv_grad = tie(conv_give, ffn_rb, conv_grad)
    conv_r = send(conv_give, step_c)
    ffn_ra = send(scatter_a(ffn_keep, ffn_r, ffn_rb), step_xy)
    in_rel, vgrad_one = call(
        conv_backward,
        place,
        (x_full, conv_grad, resid_grad, w_full, vec),
        (S((nmp, seq, own), bf16), S((8, full), f32)),
        [],
        1,
        16,
    )
    conv_sum, ffn_ra, in_rel = tie(scatter_b(conv_keep, conv_r), ffn_ra, in_rel)
    conv_rb = send(conv_sum, step_yx)
    ffn_share = scatter_z(ffn_keep, ffn_r, ffn_rb, ffn_ra)
    conv_sum, ffn_share = tie(scatter_a(conv_keep, conv_r, conv_rb), ffn_share)
    conv_ra = send(conv_sum, step_xy)
    conv_ra, in_rel, block_rel = tie(conv_ra, in_rel, block_rel)
    conv_share = scatter_z(conv_keep, conv_r, conv_rb, conv_ra)
    out_parts = [jnp.stack([block_rel[k], in_rel[k]]) for k in range(nmp)]
    for k in range(1, nmp):
        out_parts[k] = lax.ppermute(out_parts[k], "mp", within[k])
    conv_share, *out_parts[:-1] = tie(conv_share, *out_parts[:-1])

    squares = square_sum(conv_share) + square_sum(ffn_share)
    small = jnp.concatenate(
        [
            (vgrad_one + vgrad_two)[:6],
            bias_grad.reshape(hidden // full, full),
            jnp.broadcast_to(squares, (1, full)),
        ]
    )
    small, out_parts[-1] = all_sum(small, out_parts[-1])
    outputs = in_order(out_parts)
    block_output, input_grad = outputs[:, 0], outputs[:, 1].astype(f32)
    vector_sum, bias_sum = small[:6], small[6:-1].reshape(hidden)
    hidden_share, output_share = ffn_share[0], ffn_share[1].T
    grad_norm = jnp.sqrt(small[-1, 0] + square_sum(small[:-1]))
    clip_scale = jnp.minimum(1.0, CLIP_NORM / (grad_norm + 1e-06))
    bias_share = lax.dynamic_slice_in_dim(bias_sum, mp * part, part, 0)
    matrices = (
        (conv_master, conv_first, conv_second, conv_share),
        (hidden_master, hidden_first, hidden_second, hidden_share),
        (output_master, output_first, output_second, output_share),
    )
    small_ones = (
        (vectors, vector_first, vector_second, vector_sum),
        (hidden_bias, bias_first, bias_second, bias_share),
    )
    updated = [adam_step(*m, clip_scale, MATRIX_RATE, WEIGHT_DECAY) for m in matrices]
    updated += [adam_step(*m, clip_scale, VECTOR_RATE, 0.0) for m in small_ones]
    return (block_output, input_grad, grad_norm, *(leaf for new in updated for leaf in new))


def solution(mesh):
    rows = P("dp", None, "mp")
    conv = P(None, "dp", "mp")
    hid = P("dp", "mp")
    out = P("mp", "dp")
    return jax.shard_map(
        functools.partial(per_device, mesh.shape["dp"], mesh.shape["mp"]),
        mesh=mesh,
        in_specs=(rows, rows, P("dp"), *(conv, hid, out) * 3, *(P(),) * 3, *(P("mp"),) * 3),
        out_specs=(
            rows,
            rows,
            P(),
            *(conv,) * 3,
            *(hid,) * 3,
            *(out,) * 3,
            *(P(),) * 3,
            *(P("mp"),) * 3,
        ),
        check_vma=False,
    )
```

```python
import functools

import jax
import jax.numpy as jnp
from jax import lax
from jax.experimental import pallas as pl
from jax.experimental.pallas import tpu as pltpu
from jax.sharding import PartitionSpec as P

KERNEL = 9
DILATION = 8
REACH = DILATION * (KERNEL // 2)
STEP = 10
ROWS = 256

NORM_EPS = 1e-05
BETA_ONE = 0.9
BETA_TWO = 0.999
ADAM_EPS = 1e-08
MATRIX_RATE = 0.03
VECTOR_RATE = 0.3
WEIGHT_DECAY = 0.01
CLIP_NORM = 1.0

f32 = jnp.float32
bf16 = jnp.bfloat16
NN = (((1,), (0,)), ((), ()))
NT = (((1,), (1,)), ((), ()))


def dot(a, b, dims=NN):
    return lax.dot_general(a, b, dims, preferred_element_type=f32)


def phi_of(v):
    return 0.5 * (1.0 + lax.erf(v * 0.7071067811865476))


def slope_of(v, phi):
    return phi + v * jnp.exp(-0.5 * v * v) * 0.3989422804014327


def norm_parts(v):
    centre = v - jnp.mean(v, axis=-1, keepdims=True)
    inverse = lax.rsqrt(jnp.mean(centre * centre, axis=-1, keepdims=True) + NORM_EPS)
    return centre * inverse, inverse


def norm_back(e, s, inverse):
    return inverse * (
        e - jnp.mean(e, axis=-1, keepdims=True) - s * jnp.mean(e * s, axis=-1, keepdims=True)
    )


def mult(v, n):
    return pl.multiple_of(v, n)


def relative(place, d, m):
    dp, mp = place[0], place[1]
    fx = (dp & 1) ^ (d & 1)
    fy = (mp >> 1) ^ (m >> 1)
    dz = (dp >> 1) ^ (d >> 1)
    if m & 1:
        return fx, fy, dz
    return fy, fx, dz


def source_of(place, dc, b, a, dz):
    dp, mp = place[0], place[1]
    flip = (mp & 1) ^ dc
    fx = jnp.where(flip == 0, a, b)
    fy = jnp.where(flip == 0, b, a)
    d = ((dp >> 1) ^ dz) * 2 + ((dp & 1) ^ fx)
    m = ((mp >> 1) ^ fy) * 2 + ((mp & 1) ^ dc)
    return d, m


def store_shares(place, keep, give, m, devices, store):
    same = (place[1] & 1) == (m & 1)

    @pl.when(same)
    def _():
        for d in range(devices):
            store(keep, relative(place, d, m), d)

    @pl.when(jnp.logical_not(same))
    def _():
        for d in range(devices):
            store(give, relative(place, d, m), d)


SLOTS = tuple((dc, b, a) for dc in (0, 1) for b, a in ((0, 0), (0, 1), (1, 0), (1, 1)))


def fetch_rows(place, parts, whole, sems):
    seq, own = whole.shape[0], parts[0].shape[1]
    copies = []
    for k, part in enumerate(parts):
        target = whole.at[:, pl.ds(mult((place[1] ^ k) * own, own), own)]
        copies.append(pltpu.make_async_copy(part.at[pl.ds(0, seq), :], target, sems.at[k]))
        copies[-1].start()
    return copies


def fetch_shards(shards, sems):
    copies = []
    for index, shard, whole, d, m in shards:
        di, cols = shard.shape[-2:]
        target = whole.at[
            (slice(None),) * (len(shard.shape) - 2)
            + (pl.ds(mult(d * di, di), di), pl.ds(mult(m * cols, cols), cols))
        ]
        copies.append(pltpu.make_async_copy(shard, target, sems.at[index]))
        copies[-1].start()
    return copies


def conv_forward(place, x0, x1, x2, x3, vec, *rest):
    pieces = rest[:8]
    w_out, x_out, na_out, conv_out, bias_out, nf, nab, whole, extra, sems, x_sem = rest[8:]
    full = vec.shape[1]
    seq, own = x_out.shape[0], x0.shape[1]
    blocks = place[3]

    x_parts = (x0, x1, x2, x3)
    rows = fetch_rows(place, x_parts, x_out, x_sem.at[0])
    shards = fetch_shards(
        [
            ((slot, z), piece.at[z], whole, *source_of(place, *index, z))
            for slot, (index, piece) in enumerate(zip(SLOTS, pieces))
            for z in range(piece.shape[0])
        ],
        sems,
    )
    extras = [
        pltpu.make_async_copy(part.at[pl.ds(seq, extra.shape[1]), :], extra.at[k], x_sem.at[1, k])
        for k, part in enumerate(x_parts)
    ]
    for copy in extras:
        copy.start()
    for copy in rows + extras:
        copy.wait()
    for k in range(len(x_parts)):
        values = extra[k].astype(f32)
        units = values.shape[0] // 4
        bias_out[place[1] ^ k] = (values[0:units] + values[units : 2 * units]) + values[
            2 * units : 3 * units
        ]

    nf[...] = jnp.zeros_like(nf)
    na_out[...] = jnp.zeros_like(na_out)
    conv_out[...] = jnp.zeros_like(conv_out)
    gain = vec[0:1, :]
    shift = vec[1:2, :]

    def norm_step(i, _):
        rows = pl.ds(mult(i * 128, 128), 128)
        scaled, _ = norm_parts(x_out[rows, :].astype(f32))
        nf[pl.ds(mult(i * 128 + REACH, 8), 128), :] = scaled * gain + shift
        return 0

    lax.fori_loop(0, blocks * (ROWS // 128), norm_step, 0)
    padded = nab.shape[1]

    def shift_step(i, _):
        row = mult(i * 64, 64)
        nab[0, pl.ds(row, 64), :] = nf[pl.ds(row, 64), :].astype(bf16)
        nab[1, pl.ds(row, 64), :] = nf[pl.ds(mult(row + 8, 8), 64), :].astype(bf16)
        return 0

    lax.fori_loop(0, padded // 64, shift_step, 0)
    for copy in shards:
        copy.wait()
    w_copy = pltpu.make_async_copy(whole, w_out, x_sem.at[2, 0])
    w_copy.start()

    def conv_step(i, _):
        row = mult(i * ROWS, ROWS)
        na_out[pl.ds(row, ROWS), :] = nab[0, pl.ds(mult(row + REACH, 32), ROWS), :]
        window = jnp.concatenate(
            [
                nab[t & 1, pl.ds(mult(row + DILATION * (t - (t & 1)), 16), ROWS), :]
                for t in range(KERNEL)
            ],
            axis=1,
        )
        weights = whole[...].reshape(KERNEL * full, full)
        conv_out[pl.ds(row, ROWS), :] = dot(window, weights) + vec[2:3, :]
        return 0

    lax.fori_loop(0, blocks, conv_step, 0)
    w_copy.wait()


def ffn(place, x_full, conv_out, c0, c1, c2, c3, vec, hbias, *rest):
    pieces = rest[:8]
    block_out, resid_out, cab, act, hg, sec, mg, vgrad, hbgrad = rest[8:17]
    whole, cf, sems, c_sem = rest[17:]
    wh, wo = whole.at[0], whole.at[1]
    seq, full = x_full.shape
    hidden = hbias.shape[1]
    own = c0.shape[1]
    blocks = place[3]

    rows = fetch_rows(place, (c0, c1, c2, c3), mg, c_sem)
    shards = []
    for slot, piece in enumerate(pieces):
        w, dc, dx = slot >> 2, (slot >> 1) & 1, slot & 1
        for z in range(piece.shape[0]):
            for dy in (0, 1):
                d = ((place[0] >> 1) ^ z) * 2 + ((place[0] & 1) ^ dx)
                m = place[1] ^ (dy * 2 + dc)
                shards.append(((slot, z, dy), piece.at[z, dy], whole.at[w], d, m))
    shards = fetch_shards(shards, sems)
    vgrad[...] = jnp.zeros_like(vgrad)
    hbgrad[...] = jnp.zeros_like(hbgrad)
    cf[...] = jnp.zeros_like(cf)
    for copy in rows + shards:
        copy.wait()

    def out_store(rows, values):
        for m in range(full // own):
            block_out[place[1] ^ m, rows, :] = values[:, m * own : (m + 1) * own]

    def row_step(i, _):
        rows = pl.ds(mult(i * ROWS, ROWS), ROWS)
        conv = conv_out[rows, :]
        residual = x_full[rows, :].astype(f32) + conv * phi_of(conv)
        s, inverse = norm_parts(residual)
        second = (s * vec[3:4, :] + vec[4:5, :]).astype(bf16)
        sec[rows, :] = second
        grad = mg[rows, :]
        for j in range(hidden // 512):
            cols = slice(j * 512, (j + 1) * 512)
            h = dot(second, wh[:, cols]) + hbias[0:1, cols]
            phi = phi_of(h)
            act[rows, cols] = (h * phi).astype(bf16)
            hidden_grad = (dot(grad, wo[:, cols]) * slope_of(h, phi)).astype(bf16)
            hg[rows, cols] = hidden_grad
            hbgrad[0:1, cols] += jnp.sum(hidden_grad.astype(f32), axis=0, keepdims=True)
        mixed = dot(act[rows, :], wo[...], NT)
        out_store(rows, (residual + (mixed + vec[5:6, :])).astype(bf16))
        second_grad = dot(hg[rows, :], wh[...], NT)
        up = grad.astype(f32)
        vgrad[3:4, :] += jnp.sum(second_grad * s, axis=0, keepdims=True)
        vgrad[4:5, :] += jnp.sum(second_grad, axis=0, keepdims=True)
        vgrad[5:6, :] += jnp.sum(up, axis=0, keepdims=True)
        resid_grad = up + norm_back(second_grad * vec[3:4, :], s, inverse)
        resid_out[rows, :] = resid_grad
        conv = conv_out[rows, :]
        conv_grad = (resid_grad * slope_of(conv, phi_of(conv))).astype(bf16)
        rounded = conv_grad.astype(f32)
        cf[pl.ds(mult(i * ROWS + REACH, 8), ROWS), :] = rounded
        vgrad[2:3, :] += jnp.sum(rounded, axis=0, keepdims=True)
        return 0

    def idle_step(i, _):
        rows = pl.ds(mult(i * ROWS, ROWS), ROWS)
        out_store(rows, x_full[rows, :])
        resid_out[rows, :] = mg[rows, :].astype(f32)
        for ref in (sec, mg):
            ref[rows, :] = jnp.zeros((ROWS, full), bf16)
        for ref in (act, hg):
            ref[rows, :] = jnp.zeros((ROWS, hidden), bf16)
        return 0

    lax.fori_loop(0, blocks, row_step, 0)
    lax.fori_loop(blocks, seq // ROWS, idle_step, 0)

    def shift_step(i, _):
        row = mult(i * 64, 64)
        cab[0, pl.ds(row, 64), :] = cf[pl.ds(row, 64), :].astype(bf16)
        cab[1, pl.ds(row, 64), :] = cf[pl.ds(mult(row + 8, 8), 64), :].astype(bf16)
        return 0

    lax.fori_loop(0, cab.shape[1] // 64, shift_step, 0)


def ffn_weight_grad(place, sec, hg, mg, act, keep, give):
    full, hidden = sec.shape[1], hg.shape[1]
    di, part = keep.shape[4:]
    sec_t = sec[...].T
    mg_t = mg[...].T
    for m in range(hidden // part):
        cols = slice(m * part, (m + 1) * part)
        for w, (left, right) in enumerate(((sec_t, hg), (mg_t, act))):
            value = dot(left, right[:, cols]).astype(bf16)

            def store(ref, index, d):
                ref[(*index, w)] = value[d * di : (d + 1) * di, :]

            store_shares(place, keep, give, m, full // di, store)


def shifted_rows(cab, u, row, count):
    odd = u & 1
    return cab[odd, pl.ds(mult(row + (u - odd) * DILATION, 16), count), :]


def conv_weight_grad(place, na, cab, keep, give):
    seq, full = na.shape
    taps, di, own = keep.shape[3:]
    na_t = na[...].T

    def tap_step(t, _):
        value = dot(na_t, shifted_rows(cab, KERNEL - 1 - t, 0, seq)).astype(bf16)
        for m in range(full // own):

            def store(ref, index, d):
                ref[(*index, t)] = value[d * di : (d + 1) * di, m * own : (m + 1) * own]

            store_shares(place, keep, give, m, full // di, store)
        return 0

    lax.fori_loop(0, taps, tap_step, 0)


def conv_backward(place, x_full, cab, resid, w, vec, in_grad, vgrad):
    seq, full = x_full.shape
    own = in_grad.shape[2]
    blocks = place[3]
    vgrad[...] = jnp.zeros_like(vgrad)

    def in_store(rows, values):
        values = values.astype(bf16)
        for m in range(full // own):
            in_grad[place[1] ^ m, rows, :] = values[:, m * own : (m + 1) * own]

    def row_step(i, _):
        row = mult(i * ROWS, ROWS)
        rows = pl.ds(row, ROWS)
        total = jnp.zeros((ROWS, full), f32)
        for t in range(KERNEL):
            shifted = shifted_rows(cab, KERNEL - 1 - t, row, ROWS)
            total = total + dot(shifted, w[t], NT)
        s, inverse = norm_parts(x_full[rows, :].astype(f32))
        vgrad[0:1, :] += jnp.sum(total * s, axis=0, keepdims=True)
        vgrad[1:2, :] += jnp.sum(total, axis=0, keepdims=True)
        in_store(rows, resid[rows, :] + norm_back(total * vec[0:1, :], s, inverse))
        return 0

    def idle_step(i, _):
        rows = pl.ds(mult(i * ROWS, ROWS), ROWS)
        in_store(rows, resid[rows, :])
        return 0

    lax.fori_loop(0, blocks, row_step, 0)
    lax.fori_loop(blocks, seq // ROWS, idle_step, 0)


def tie(*values):
    return lax.optimization_barrier(values)


def placed(kernel):
    def run(lengths, *refs):
        mp = lax.axis_index("mp")
        length = lengths[mp]
        kernel((lax.axis_index("dp"), mp, length, length // ROWS), *refs)

    return run


def call(kernel, lengths, args, outs, scratch, flops, mib, far=(), far_out=()):
    near = pl.BlockSpec(memory_space=pltpu.VMEM)
    left = pl.BlockSpec(memory_space=pltpu.HBM)
    moved = sum(a.size * a.dtype.itemsize for a in (*args, *outs))
    return pl.pallas_call(
        placed(kernel),
        out_shape=outs,
        in_specs=[pl.BlockSpec(memory_space=pltpu.SMEM)]
        + [left if i in far else near for i in range(len(args))],
        out_specs=[left if i in far_out else near for i in range(len(outs))],
        scratch_shapes=scratch,
        compiler_params=pltpu.CompilerParams(vmem_limit_bytes=mib * 2**20),
        cost_estimate=pl.CostEstimate(flops=flops, bytes_accessed=moved, transcendentals=0),
    )(lengths, *args)


def adam_step(weight, first_mom, second, gradient, clip_scale, step_rate, decay_rate):
    clipped = gradient * clip_scale
    first_new = BETA_ONE * first_mom + (1.0 - BETA_ONE) * clipped
    second_new = BETA_TWO * second + (1.0 - BETA_TWO) * clipped * clipped
    update_dir = (
        first_new
        / (1.0 - BETA_ONE**STEP)
        / (jnp.sqrt(second_new / (1.0 - BETA_TWO**STEP)) + ADAM_EPS)
    )
    return (weight - step_rate * (update_dir + decay_rate * weight), first_new, second_new)


def square_sum(values):
    return jnp.sum(values * values)


def per_device(
    ndp,
    nmp,
    inputs,
    cotangent,
    lengths,
    conv_master,
    hidden_master,
    output_master,
    conv_first,
    hidden_first,
    output_first,
    conv_second,
    hidden_second,
    output_second,
    vectors,
    vector_first,
    vector_second,
    hidden_bias,
    bias_first,
    bias_second,
):
    axes = ("dp", "mp")
    nz = ndp // 2
    seq, own = inputs.shape[1:]
    full = vectors.shape[1]
    part = hidden_bias.shape[0]
    hidden = part * nmp
    di = full // ndp
    mp = lax.axis_index("mp")

    def perm(move):
        pairs = []
        for i in range(ndp * nmp):
            d, m = divmod(i, nmp)
            z, x, y, c = move(d >> 1, d & 1, m >> 1, m & 1)
            pairs.append((i, (z * 2 + x) * nmp + y * 2 + c))
        return pairs

    across_z = [perm(lambda z, x, y, c, k=k: (z ^ k, x, y, c)) for k in range(nz)]
    step_x = perm(lambda z, x, y, c: (z, x ^ 1, y, c))
    step_y = perm(lambda z, x, y, c: (z, x, y ^ 1, c))
    step_c = perm(lambda z, x, y, c: (z, x, y, c ^ 1))
    step_xy = perm(lambda z, x, y, c: (z, x ^ 1, y, c) if c == 0 else (z, x, y ^ 1, c))
    step_yx = perm(lambda z, x, y, c: (z, x, y ^ 1, c) if c == 0 else (z, x ^ 1, y, c))
    within = [[(i, i ^ k) for i in range(nmp)] for k in range(nmp)]

    def send(values, pairs):
        return lax.ppermute(values, axes, pairs)

    def gather_z(shard):
        return [shard] + [send(shard, across_z[k]) for k in range(1, nz)]

    def add(*terms):
        total = terms[0].astype(f32)
        for term in terms[1:]:
            total = total + term.astype(f32)
        return total

    def scatter_b(k, r):
        return add(k[1], r[1]).astype(bf16)

    def scatter_a(k, r, rb):
        return add(k[0, 1], r[0, 1], rb[1]).astype(bf16)

    def scatter_z(k, r, rb, ra):
        total = add(k[0, 0, 0], r[0, 0, 0], rb[0, 0], ra[0])
        for j in range(1, nz):
            part = add(k[0, 0, j], r[0, 0, j], rb[0, j], ra[j]).astype(bf16)
            total = total + send(part, across_z[j]).astype(f32)
        return total

    def take_windows(values, extra=None):
        blocks = [lax.dynamic_index_in_dim(values, mp ^ k, 0, False) for k in range(nmp)]
        if extra is not None:
            blocks = [jnp.concatenate([block, extra]) for block in blocks]
        return blocks

    def swap(blocks):
        return [blocks[0]] + [lax.ppermute(blocks[k], "mp", within[k]) for k in range(1, nmp)]

    def in_order(pieces):
        for bit in range(nmp.bit_length() - 1):
            odd = ((mp >> bit) & 1) == 1
            pieces = [jnp.where(odd, pieces[k ^ (1 << bit)], pieces[k]) for k in range(nmp)]
        return jnp.stack(pieces)

    def all_sum(values):
        values = values + send(values, step_c)
        step = 1
        while step < nz:
            values = values + send(values, across_z[step])
            step *= 2
        values = values + send(values, step_x)
        return values + send(values, step_y)

    exact, rest = [], hidden_bias
    for _ in range(3):
        exact.append(lax.reduce_precision(rest, 8, 7))
        rest = rest - exact[-1]
    exact.append(jnp.zeros_like(rest))
    exact = jnp.concatenate(exact).reshape(4 * part // own, own).astype(bf16)
    ffn_shard = jnp.stack([hidden_master.astype(bf16), output_master.astype(bf16).T])

    x_blocks = take_windows(inputs, exact)
    *x_blocks, conv_shard = tie(*x_blocks, conv_master.astype(bf16))
    x_parts = swap(x_blocks)
    conv_z = gather_z(conv_shard)
    ffn_y = send(ffn_shard, step_y)
    *tied, ffn_shard, ffn_y = tie(*x_parts, *conv_z, ffn_shard, ffn_y)
    x_parts, conv_z = tied[:nmp], jnp.stack(tied[nmp:])
    first, last = [jnp.stack([ffn_shard[w], ffn_y[w]]) for w in (0, 1)]
    conv_a, conv_b = send(conv_z, step_xy), send(conv_z, step_yx)
    first = gather_z(first)
    conv_z, conv_a, conv_b, last, *first = tie(conv_z, conv_a, conv_b, last, *first)
    conv_ab = send(conv_a, step_yx)
    first = jnp.stack(first)
    first_x = send(first, step_x)
    last = gather_z(last)
    conv_z, conv_a, conv_b, conv_ab, cotangent, first, *last = tie(
        conv_z, conv_a, conv_b, conv_ab, cotangent, first, *last
    )
    conv_parts = [conv_z, conv_a, conv_b, conv_ab]
    conv_parts += [send(part_of, step_c) for part_of in conv_parts]
    last = jnp.stack(last)
    last_x = send(last, step_x)
    c_parts = swap(take_windows(cotangent))

    S = jax.ShapeDtypeStruct
    padded = seq + 2 * REACH
    last, *x_parts = tie(last, *x_parts)
    first_c, last_c = send(first, step_c), send(last, step_c)
    w_full, x_full, normed, conv_out, bias_all = call(
        conv_forward,
        lengths,
        (*x_parts, vectors, *conv_parts),
        (
            S((KERNEL, full, full), bf16),
            S((seq, full), bf16),
            S((seq, full), bf16),
            S((seq, full), f32),
            S((nmp, part // own, own), f32),
        ),
        [
            pltpu.VMEM((padded + 8, full), f32),
            pltpu.VMEM((2, padded, full), bf16),
            pltpu.VMEM((KERNEL, full, full), bf16),
            pltpu.VMEM((nmp, 4 * part // own, own), bf16),
            pltpu.SemaphoreType.DMA((8, nz)),
            pltpu.SemaphoreType.DMA((3, nmp)),
        ],
        2 * seq * KERNEL * full * full,
        24,
        (0, 1, 2, 3, *range(5, 13)),
        (0,),
    )
    *tied, conv_out = tie(first, first_x, first_c, last, last_x, last_c, *c_parts, conv_out)
    first, first_x, first_c, last, last_x, last_c, *c_parts = tied
    ffn_parts = [first, first_x, first_c, send(first_x, step_c)]
    ffn_parts += [last, last_x, last_c, send(last_x, step_c)]
    block_rel, resid_grad, conv_grad, active, hidden_grad, second, mix_grad, vgrad_two, bias_grad = call(
        ffn,
        lengths,
        (x_full, conv_out, *c_parts, vectors, bias_all.reshape(1, hidden), *ffn_parts),
        (
            S((nmp, seq, own), bf16),
            S((seq, full), f32),
            S((2, padded, full), bf16),
            *(S((seq, hidden), bf16),) * 2,
            *(S((seq, full), bf16),) * 2,
            S((8, full), f32),
            S((1, hidden), f32),
        ),
        [
            pltpu.VMEM((2, full, hidden), bf16),
            pltpu.VMEM((padded + 8, full), f32),
            pltpu.SemaphoreType.DMA((8, nz, 2)),
            pltpu.SemaphoreType.DMA((nmp,)),
        ],
        8 * seq * hidden * full,
        20,
        (2, 3, 4, 5, *range(8, 16)),
    )
    ffn_keep, ffn_give = call(
        ffn_weight_grad,
        lengths,
        (second, hidden_grad, mix_grad, active),
        (S((2, 2, nz, 2, di, part), bf16),) * 2,
        [],
        4 * seq * hidden * full,
        12,
    )
    ffn_r = send(ffn_give, step_c)
    ffn_keep, normed = tie(ffn_keep, normed)
    conv_keep, conv_give = call(
        conv_weight_grad,
        lengths,
        (normed, conv_grad),
        (S((2, 2, nz, KERNEL, di, own), bf16),) * 2,
        [],
        2 * seq * KERNEL * full * full,
        16,
    )
    conv_r = send(conv_give, step_c)
    ffn_sum, conv_keep, conv_grad = tie(scatter_b(ffn_keep, ffn_r), conv_keep, conv_grad)
    ffn_rb = send(ffn_sum, step_yx)
    in_rel, vgrad_one = call(
        conv_backward,
        lengths,
        (x_full, conv_grad, resid_grad, w_full, vectors),
        (S((nmp, seq, own), bf16), S((8, full), f32)),
        [],
        1,
        16,
    )
    conv_sum, in_rel = tie(scatter_b(conv_keep, conv_r), in_rel)
    conv_rb = send(conv_sum, step_yx)
    ffn_ra = send(scatter_a(ffn_keep, ffn_r, ffn_rb), step_xy)
    conv_ra = send(scatter_a(conv_keep, conv_r, conv_rb), step_xy)
    ffn_share = scatter_z(ffn_keep, ffn_r, ffn_rb, ffn_ra)
    conv_ra, in_rel, block_rel = tie(conv_ra, in_rel, block_rel)
    conv_share = scatter_z(conv_keep, conv_r, conv_rb, conv_ra)
    out_parts = [jnp.stack([block_rel[k], in_rel[k]]) for k in range(nmp)]
    for k in range(1, nmp):
        out_parts[k] = lax.ppermute(out_parts[k], "mp", within[k])
    conv_share, *out_parts[:-1] = tie(conv_share, *out_parts[:-1])
    ffn_share, out_parts[-1] = tie(ffn_share, out_parts[-1])
    outputs = in_order(out_parts)
    block_output, input_grad = outputs[:, 0], outputs[:, 1].astype(f32)

    squares = square_sum(conv_share) + square_sum(ffn_share)
    small = jnp.concatenate(
        [
            (vgrad_one + vgrad_two)[:6],
            bias_grad.reshape(hidden // full, full),
            jnp.broadcast_to(squares, (1, full)),
        ]
    )
    small = all_sum(small)
    vector_sum, bias_sum = small[:6], small[6:-1].reshape(hidden)
    hidden_share, output_share = ffn_share[0], ffn_share[1].T
    grad_norm = jnp.sqrt(small[-1, 0] + square_sum(small[:-1]))
    clip_scale = jnp.minimum(1.0, CLIP_NORM / (grad_norm + 1e-06))
    bias_share = lax.dynamic_slice_in_dim(bias_sum, mp * part, part, 0)
    matrices = (
        (conv_master, conv_first, conv_second, conv_share),
        (hidden_master, hidden_first, hidden_second, hidden_share),
        (output_master, output_first, output_second, output_share),
    )
    small_ones = (
        (vectors, vector_first, vector_second, vector_sum),
        (hidden_bias, bias_first, bias_second, bias_share),
    )
    updated = [adam_step(*m, clip_scale, MATRIX_RATE, WEIGHT_DECAY) for m in matrices]
    updated += [adam_step(*m, clip_scale, VECTOR_RATE, 0.0) for m in small_ones]
    return (block_output, input_grad, grad_norm, *(leaf for new in updated for leaf in new))


def solution(mesh):
    rows = P("dp", None, "mp")
    conv = P(None, "dp", "mp")
    hid = P("dp", "mp")
    out = P("mp", "dp")
    return jax.shard_map(
        functools.partial(per_device, mesh.shape["dp"], mesh.shape["mp"]),
        mesh=mesh,
        in_specs=(rows, rows, P("dp"), *(conv, hid, out) * 3, *(P(),) * 3, *(P("mp"),) * 3),
        out_specs=(
            rows,
            rows,
            P(),
            *(conv,) * 3,
            *(hid,) * 3,
            *(out,) * 3,
            *(P(),) * 3,
            *(P("mp"),) * 3,
        ),
        check_vma=False,
    )
```

```python
import functools

import jax
import jax.numpy as jnp
from jax import lax
from jax.experimental import pallas as pl
from jax.experimental.pallas import tpu as pltpu
from jax.sharding import PartitionSpec as P

KERNEL = 9
DILATION = 8
REACH = DILATION * (KERNEL // 2)
STEP = 10
ROWS = 256

NORM_EPS = 1e-05
BETA_ONE = 0.9
BETA_TWO = 0.999
ADAM_EPS = 1e-08
MATRIX_RATE = 0.03
VECTOR_RATE = 0.3
WEIGHT_DECAY = 0.01
CLIP_NORM = 1.0

f32 = jnp.float32
bf16 = jnp.bfloat16
NN = (((1,), (0,)), ((), ()))
NT = (((1,), (1,)), ((), ()))


def dot(a, b, dims=NN):
    return lax.dot_general(a, b, dims, preferred_element_type=f32)


def phi_of(v):
    return 0.5 * (1.0 + lax.erf(v * 0.7071067811865476))


def slope_of(v, phi):
    return phi + v * jnp.exp(-0.5 * v * v) * 0.3989422804014327


def norm_parts(v):
    centre = v - jnp.mean(v, axis=-1, keepdims=True)
    inverse = lax.rsqrt(jnp.mean(centre * centre, axis=-1, keepdims=True) + NORM_EPS)
    return centre * inverse, inverse


def norm_back(e, s, inverse):
    return inverse * (
        e - jnp.mean(e, axis=-1, keepdims=True) - s * jnp.mean(e * s, axis=-1, keepdims=True)
    )


def mult(v, n):
    return pl.multiple_of(v, n)


def relative(place, d, m):
    dp, mp = place[0], place[1]
    fx = (dp & 1) ^ (d & 1)
    fy = (mp >> 1) ^ (m >> 1)
    dz = (dp >> 1) ^ (d >> 1)
    if m & 1:
        return fx, fy, dz
    return fy, fx, dz


def source_of(place, dc, b, a, dz):
    dp, mp = place[0], place[1]
    flip = (mp & 1) ^ dc
    fx = jnp.where(flip == 0, a, b)
    fy = jnp.where(flip == 0, b, a)
    d = ((dp >> 1) ^ dz) * 2 + ((dp & 1) ^ fx)
    m = ((mp >> 1) ^ fy) * 2 + ((mp & 1) ^ dc)
    return d, m


def store_shares(place, keep, give, m, devices, store):
    same = (place[1] & 1) == (m & 1)

    @pl.when(same)
    def _():
        for d in range(devices):
            store(keep, relative(place, d, m), d)

    @pl.when(jnp.logical_not(same))
    def _():
        for d in range(devices):
            store(give, relative(place, d, m), d)


SLOTS = tuple((dc, b, a) for dc in (0, 1) for b, a in ((0, 0), (0, 1), (1, 0), (1, 1)))


def fetch_rows(place, parts, whole, sems):
    seq, own = whole.shape[0], parts[0].shape[1]
    copies = []
    for k, part in enumerate(parts):
        target = whole.at[:, pl.ds(mult((place[1] ^ k) * own, own), own)]
        copies.append(pltpu.make_async_copy(part.at[pl.ds(0, seq), :], target, sems.at[k]))
        copies[-1].start()
    return copies


def fetch_shards(shards, sems):
    copies = []
    for index, shard, whole, d, m in shards:
        di, cols = shard.shape[-2:]
        target = whole.at[
            (slice(None),) * (len(shard.shape) - 2)
            + (pl.ds(mult(d * di, di), di), pl.ds(mult(m * cols, cols), cols))
        ]
        copies.append(pltpu.make_async_copy(shard, target, sems.at[index]))
        copies[-1].start()
    return copies


def conv_forward(place, x0, x1, x2, x3, vec, *rest):
    pieces = rest[:8]
    w_out, x_out, na_out, resid, slope, bias_out, nf, nab, whole, extra, sems, x_sem = rest[8:]
    full = vec.shape[1]
    seq, own = x_out.shape[0], x0.shape[1]
    blocks = place[3]

    x_parts = (x0, x1, x2, x3)
    rows = fetch_rows(place, x_parts, x_out, x_sem.at[0])
    shards = fetch_shards(
        [
            ((slot, z), piece.at[z], whole, *source_of(place, *index, z))
            for slot, (index, piece) in enumerate(zip(SLOTS, pieces))
            for z in range(piece.shape[0])
        ],
        sems,
    )
    extras = [
        pltpu.make_async_copy(part.at[pl.ds(seq, extra.shape[1]), :], extra.at[k], x_sem.at[1, k])
        for k, part in enumerate(x_parts)
    ]
    for copy in extras:
        copy.start()
    for copy in rows + extras:
        copy.wait()
    for k in range(len(x_parts)):
        values = extra[k].astype(f32)
        units = values.shape[0] // 4
        bias_out[place[1] ^ k] = (values[0:units] + values[units : 2 * units]) + values[
            2 * units : 3 * units
        ]

    nf[...] = jnp.zeros_like(nf)
    na_out[...] = jnp.zeros_like(na_out)
    gain = vec[0:1, :]
    shift = vec[1:2, :]

    def norm_step(i, _):
        rows = pl.ds(mult(i * 128, 128), 128)
        scaled, _ = norm_parts(x_out[rows, :].astype(f32))
        nf[pl.ds(mult(i * 128 + REACH, 8), 128), :] = scaled * gain + shift
        return 0

    lax.fori_loop(0, blocks * (ROWS // 128), norm_step, 0)
    padded = nab.shape[1]

    def shift_step(i, _):
        row = mult(i * 64, 64)
        nab[0, pl.ds(row, 64), :] = nf[pl.ds(row, 64), :].astype(bf16)
        nab[1, pl.ds(row, 64), :] = nf[pl.ds(mult(row + 8, 8), 64), :].astype(bf16)
        return 0

    lax.fori_loop(0, padded // 64, shift_step, 0)
    for copy in shards:
        copy.wait()
    w_copy = pltpu.make_async_copy(whole, w_out, x_sem.at[2, 0])
    w_copy.start()

    def conv_step(i, _):
        row = mult(i * ROWS, ROWS)
        na_out[pl.ds(row, ROWS), :] = nab[0, pl.ds(mult(row + REACH, 32), ROWS), :]
        window = jnp.concatenate(
            [
                nab[t & 1, pl.ds(mult(row + DILATION * (t - (t & 1)), 16), ROWS), :]
                for t in range(KERNEL)
            ],
            axis=1,
        )
        weights = whole[...].reshape(KERNEL * full, full)
        rows = pl.ds(row, ROWS)
        conv = dot(window, weights) + vec[2:3, :]
        phi = phi_of(conv)
        resid[rows, :] = x_out[rows, :].astype(f32) + conv * phi
        slope[rows, :] = slope_of(conv, phi)
        return 0

    lax.fori_loop(0, blocks, conv_step, 0)
    w_copy.wait()


def ffn_hidden(place, x_full, resid, c0, c1, c2, c3, vec, hbias, *rest):
    pieces = rest[:8]
    block_out, act, hg, sec, mg, wh_out, hbgrad = rest[8:15]
    whole, sems, c_sem = rest[15:]
    wh, wo = whole.at[0], whole.at[1]
    seq, full = x_full.shape
    hidden = hbias.shape[1]
    own = c0.shape[1]
    blocks = place[3]

    rows = fetch_rows(place, (c0, c1, c2, c3), mg, c_sem.at[0])
    shards = []
    for slot, piece in enumerate(pieces):
        w, dc, dx = slot >> 2, (slot >> 1) & 1, slot & 1
        for z in range(piece.shape[0]):
            for dy in (0, 1):
                d = ((place[0] >> 1) ^ z) * 2 + ((place[0] & 1) ^ dx)
                m = place[1] ^ (dy * 2 + dc)
                shards.append(((slot, z, dy), piece.at[z, dy], whole.at[w], d, m))
    shards = fetch_shards(shards, sems)
    hbgrad[...] = jnp.zeros_like(hbgrad)
    for copy in rows + shards:
        copy.wait()
    wh_copy = pltpu.make_async_copy(wh, wh_out, c_sem.at[1, 0])
    wh_copy.start()

    def out_store(rows, values):
        for m in range(full // own):
            block_out[place[1] ^ m, rows, :] = values[:, m * own : (m + 1) * own]

    def row_step(i, _):
        rows = pl.ds(mult(i * ROWS, ROWS), ROWS)
        residual = resid[rows, :]
        s, _ = norm_parts(residual)
        second = (s * vec[3:4, :] + vec[4:5, :]).astype(bf16)
        sec[rows, :] = second
        grad = mg[rows, :]
        for j in range(hidden // 512):
            cols = slice(j * 512, (j + 1) * 512)
            h = dot(second, wh[:, cols]) + hbias[0:1, cols]
            phi = phi_of(h)
            act[rows, cols] = (h * phi).astype(bf16)
            hidden_grad = (dot(grad, wo[:, cols]) * slope_of(h, phi)).astype(bf16)
            hg[rows, cols] = hidden_grad
            hbgrad[0:1, cols] += jnp.sum(hidden_grad.astype(f32), axis=0, keepdims=True)
        mixed = dot(act[rows, :], wo[...], NT)
        out_store(rows, (residual + (mixed + vec[5:6, :])).astype(bf16))
        return 0

    def idle_step(i, _):
        rows = pl.ds(mult(i * ROWS, ROWS), ROWS)
        out_store(rows, x_full[rows, :])
        sec[rows, :] = jnp.zeros((ROWS, full), bf16)
        for ref in (act, hg):
            ref[rows, :] = jnp.zeros((ROWS, hidden), bf16)
        return 0

    lax.fori_loop(0, blocks, row_step, 0)
    lax.fori_loop(blocks, seq // ROWS, idle_step, 0)
    wh_copy.wait()


def norm_backward(place, resid, slope, grad, hg, wh, vec, resid_out, cab, vgrad, cf):
    seq = resid.shape[0]
    blocks = place[3]
    vgrad[...] = jnp.zeros_like(vgrad)
    cf[...] = jnp.zeros_like(cf)

    def row_step(i, _):
        rows = pl.ds(mult(i * ROWS, ROWS), ROWS)
        second_grad = dot(hg[rows, :], wh[...], NT)
        s, inverse = norm_parts(resid[rows, :])
        up = grad[rows, :].astype(f32)
        vgrad[3:4, :] += jnp.sum(second_grad * s, axis=0, keepdims=True)
        vgrad[4:5, :] += jnp.sum(second_grad, axis=0, keepdims=True)
        vgrad[5:6, :] += jnp.sum(up, axis=0, keepdims=True)
        resid_grad = up + norm_back(second_grad * vec[3:4, :], s, inverse)
        resid_out[rows, :] = resid_grad
        rounded = (resid_grad * slope[rows, :]).astype(bf16).astype(f32)
        cf[pl.ds(mult(i * ROWS + REACH, 8), ROWS), :] = rounded
        vgrad[2:3, :] += jnp.sum(rounded, axis=0, keepdims=True)
        return 0

    def idle_step(i, _):
        rows = pl.ds(mult(i * ROWS, ROWS), ROWS)
        resid_out[rows, :] = grad[rows, :].astype(f32)
        return 0

    lax.fori_loop(0, blocks, row_step, 0)
    lax.fori_loop(blocks, seq // ROWS, idle_step, 0)

    def shift_step(i, _):
        row = mult(i * 64, 64)
        cab[0, pl.ds(row, 64), :] = cf[pl.ds(row, 64), :].astype(bf16)
        cab[1, pl.ds(row, 64), :] = cf[pl.ds(mult(row + 8, 8), 64), :].astype(bf16)
        return 0

    lax.fori_loop(0, cab.shape[1] // 64, shift_step, 0)


def ffn_weight_grad(place, sec, hg, mg, act, keep, give):
    full, hidden = sec.shape[1], hg.shape[1]
    di, part = keep.shape[4:]
    sec_t = sec[...].T
    mg_t = mg[...].T
    for m in range(hidden // part):
        cols = slice(m * part, (m + 1) * part)
        for w, (left, right) in enumerate(((sec_t, hg), (mg_t, act))):
            value = dot(left, right[:, cols]).astype(bf16)

            def store(ref, index, d):
                ref[(*index, w)] = value[d * di : (d + 1) * di, :]

            store_shares(place, keep, give, m, full // di, store)


def shifted_rows(cab, u, row, count):
    odd = u & 1
    return cab[odd, pl.ds(mult(row + (u - odd) * DILATION, 16), count), :]


def conv_weight_grad(place, na, cab, keep, give):
    seq, full = na.shape
    taps, di, own = keep.shape[3:]
    na_t = na[...].T

    def tap_step(t, _):
        value = dot(na_t, shifted_rows(cab, KERNEL - 1 - t, 0, seq)).astype(bf16)
        for m in range(full // own):

            def store(ref, index, d):
                ref[(*index, t)] = value[d * di : (d + 1) * di, m * own : (m + 1) * own]

            store_shares(place, keep, give, m, full // di, store)
        return 0

    lax.fori_loop(0, taps, tap_step, 0)


def conv_backward(place, x_full, cab, resid, w, vec, in_grad, vgrad):
    seq, full = x_full.shape
    own = in_grad.shape[2]
    blocks = place[3]
    vgrad[...] = jnp.zeros_like(vgrad)

    def in_store(rows, values):
        values = values.astype(bf16)
        for m in range(full // own):
            in_grad[place[1] ^ m, rows, :] = values[:, m * own : (m + 1) * own]

    def row_step(i, _):
        row = mult(i * ROWS, ROWS)
        rows = pl.ds(row, ROWS)
        total = jnp.zeros((ROWS, full), f32)
        for t in range(KERNEL):
            shifted = shifted_rows(cab, KERNEL - 1 - t, row, ROWS)
            total = total + dot(shifted, w[t], NT)
        s, inverse = norm_parts(x_full[rows, :].astype(f32))
        vgrad[0:1, :] += jnp.sum(total * s, axis=0, keepdims=True)
        vgrad[1:2, :] += jnp.sum(total, axis=0, keepdims=True)
        in_store(rows, resid[rows, :] + norm_back(total * vec[0:1, :], s, inverse))
        return 0

    def idle_step(i, _):
        rows = pl.ds(mult(i * ROWS, ROWS), ROWS)
        in_store(rows, resid[rows, :])
        return 0

    lax.fori_loop(0, blocks, row_step, 0)
    lax.fori_loop(blocks, seq // ROWS, idle_step, 0)


def tie(*values):
    return lax.optimization_barrier(values)


def placed(kernel):
    def run(lengths, *refs):
        mp = lax.axis_index("mp")
        length = lengths[mp]
        kernel((lax.axis_index("dp"), mp, length, length // ROWS), *refs)

    return run


def call(kernel, lengths, args, outs, scratch, flops, mib, far=(), far_out=()):
    near = pl.BlockSpec(memory_space=pltpu.VMEM)
    left = pl.BlockSpec(memory_space=pltpu.HBM)
    moved = sum(a.size * a.dtype.itemsize for a in (*args, *outs))
    return pl.pallas_call(
        placed(kernel),
        out_shape=outs,
        in_specs=[pl.BlockSpec(memory_space=pltpu.SMEM)]
        + [left if i in far else near for i in range(len(args))],
        out_specs=[left if i in far_out else near for i in range(len(outs))],
        scratch_shapes=scratch,
        compiler_params=pltpu.CompilerParams(vmem_limit_bytes=mib * 2**20),
        cost_estimate=pl.CostEstimate(flops=flops, bytes_accessed=moved, transcendentals=0),
    )(lengths, *args)


def total_share(place, conv_own, c1, c2, c3, ffn_share, v1, v2, bias_grad, conv_share, small):
    full = small.shape[1]
    total = conv_own[...]
    for part in (c1, c2, c3):
        total = total + part[...].astype(f32)
    conv_share[...] = total
    squares = jnp.sum(total * total) + jnp.sum(ffn_share[...] * ffn_share[...])
    small[0:6, :] = (v1[...] + v2[...])[0:6, :]
    units = bias_grad.shape[1] // full
    for row in range(units):
        small[6 + row : 7 + row, :] = bias_grad[:, row * full : (row + 1) * full]
    small[6 + units :, :] = jnp.full((small.shape[0] - 6 - units, full), squares, f32)


def adam(weight, first_mom, second, gradient, clip_scale, step_rate, decay_rate):
    clipped = gradient * clip_scale
    first_new = BETA_ONE * first_mom + (1.0 - BETA_ONE) * clipped
    second_new = BETA_TWO * second + (1.0 - BETA_TWO) * clipped * clipped
    update_dir = (
        first_new
        / (1.0 - BETA_ONE**STEP)
        / (jnp.sqrt(second_new / (1.0 - BETA_TWO**STEP)) + ADAM_EPS)
    )
    return (weight - step_rate * (update_dir + decay_rate * weight), first_new, second_new)


def update(place, small, small_far, conv_share, ffn_share, *rest):
    states, outs, total = rest[:15], rest[15:31], rest[31]
    total[...] = small[...] + small_far[...]
    rows = total.shape[0] - 1
    own_rows = total[0:rows, :]
    squares = jnp.sum(own_rows * own_rows, axis=(0, 1), keepdims=True) + total[rows:, 0:1]
    norm = jnp.sqrt(squares)
    outs[15][...] = jnp.broadcast_to(norm, outs[15].shape)
    clip_scale = jnp.minimum(1.0, CLIP_NORM / (norm + 1e-06))
    gradients = [
        conv_share[...],
        ffn_share[0],
        ffn_share[1],
        total[0:6, :],
        total[pl.ds(6 + place[1], 1), :],
    ]
    for i, gradient in enumerate(gradients):
        rates = (MATRIX_RATE, WEIGHT_DECAY) if i < 3 else (VECTOR_RATE, 0.0)
        scale = clip_scale.reshape((1,) * gradient.ndim)
        state = [ref[...] for ref in states[3 * i : 3 * i + 3]]
        for ref, value in zip(outs[3 * i : 3 * i + 3], adam(*state, gradient, scale, *rates)):
            ref[...] = value


def per_device(
    ndp,
    nmp,
    inputs,
    cotangent,
    lengths,
    conv_master,
    hidden_master,
    output_master,
    conv_first,
    hidden_first,
    output_first,
    conv_second,
    hidden_second,
    output_second,
    vectors,
    vector_first,
    vector_second,
    hidden_bias,
    bias_first,
    bias_second,
):
    axes = ("dp", "mp")
    nz = ndp // 2
    seq, own = inputs.shape[1:]
    full = vectors.shape[1]
    part = hidden_bias.shape[0]
    hidden = part * nmp
    di = full // ndp
    mp = lax.axis_index("mp")

    def perm(move):
        pairs = []
        for i in range(ndp * nmp):
            d, m = divmod(i, nmp)
            z, x, y, c = move(d >> 1, d & 1, m >> 1, m & 1)
            pairs.append((i, (z * 2 + x) * nmp + y * 2 + c))
        return pairs

    across_z = [perm(lambda z, x, y, c, k=k: (z ^ k, x, y, c)) for k in range(nz)]
    step_x = perm(lambda z, x, y, c: (z, x ^ 1, y, c))
    step_y = perm(lambda z, x, y, c: (z, x, y ^ 1, c))
    step_c = perm(lambda z, x, y, c: (z, x, y, c ^ 1))
    step_xy = perm(lambda z, x, y, c: (z, x ^ 1, y, c) if c == 0 else (z, x, y ^ 1, c))
    step_yx = perm(lambda z, x, y, c: (z, x, y ^ 1, c) if c == 0 else (z, x ^ 1, y, c))
    within = [[(i, i ^ k) for i in range(nmp)] for k in range(nmp)]

    def send(values, pairs):
        return lax.ppermute(values, axes, pairs)

    def gather_z(shard):
        return [shard] + [send(shard, across_z[k]) for k in range(1, nz)]

    def add(*terms):
        total = terms[0].astype(f32)
        for term in terms[1:]:
            total = total + term.astype(f32)
        return total

    def scatter_b(k, r):
        return add(k[1], r[1]).astype(bf16)

    def scatter_a(k, r, rb):
        return add(k[0, 1], r[0, 1], rb[1]).astype(bf16)

    def scatter_z(k, r, rb, ra):
        own_part = add(k[0, 0, 0], r[0, 0, 0], rb[0, 0], ra[0])
        parts = [add(k[0, 0, j], r[0, 0, j], rb[0, j], ra[j]).astype(bf16) for j in range(1, nz)]
        return own_part, [send(part_of, across_z[j + 1]) for j, part_of in enumerate(parts)]

    def take_windows(values, extra=None):
        blocks = [lax.dynamic_index_in_dim(values, mp ^ k, 0, False) for k in range(nmp)]
        if extra is not None:
            blocks = [jnp.concatenate([block, extra]) for block in blocks]
        return blocks

    def swap(blocks):
        return [blocks[0]] + [lax.ppermute(blocks[k], "mp", within[k]) for k in range(1, nmp)]

    def in_order(pieces):
        for bit in range(nmp.bit_length() - 1):
            odd = ((mp >> bit) & 1) == 1
            pieces = [jnp.where(odd, pieces[k ^ (1 << bit)], pieces[k]) for k in range(nmp)]
        return jnp.stack(pieces)

    def all_sum(values):
        values = values + send(values, step_c)
        step = 1
        while step < nz:
            values = values + send(values, across_z[step])
            step *= 2
        values = values + send(values, step_x)
        return values, send(values, step_y)

    exact, rest = [], hidden_bias
    for _ in range(3):
        exact.append(lax.reduce_precision(rest, 8, 7))
        rest = rest - exact[-1]
    exact.append(jnp.zeros_like(rest))
    exact = jnp.concatenate(exact).reshape(4 * part // own, own).astype(bf16)
    ffn_shard = jnp.stack([hidden_master.astype(bf16), output_master.astype(bf16).T])

    x_blocks = take_windows(inputs, exact)
    *x_blocks, conv_shard = tie(*x_blocks, conv_master.astype(bf16))
    x_parts = swap(x_blocks)
    conv_z = gather_z(conv_shard)
    ffn_y = send(ffn_shard, step_y)
    *tied, ffn_shard, ffn_y = tie(*x_parts, *conv_z, ffn_shard, ffn_y)
    x_parts, conv_z = tied[:nmp], jnp.stack(tied[nmp:])
    first, last = [jnp.stack([ffn_shard[w], ffn_y[w]]) for w in (0, 1)]
    conv_a, conv_b = send(conv_z, step_xy), send(conv_z, step_yx)
    first = gather_z(first)
    conv_z, conv_a, conv_b, last, *first = tie(conv_z, conv_a, conv_b, last, *first)
    conv_ab = send(conv_a, step_yx)
    first = jnp.stack(first)
    first_x = send(first, step_x)
    last = gather_z(last)
    conv_z, conv_a, conv_b, conv_ab, cotangent, first, first_x, *last = tie(
        conv_z, conv_a, conv_b, conv_ab, cotangent, first, first_x, *last
    )
    conv_parts = [conv_z, conv_a, conv_b, conv_ab]
    conv_parts += [send(part_of, step_c) for part_of in conv_parts]
    last = jnp.stack(last)
    last_x = send(last, step_x)
    c_blocks = take_windows(cotangent)
    c_parts = [lax.ppermute(c_blocks[k], "mp", within[k]) for k in range(2, nmp)]

    S = jax.ShapeDtypeStruct
    padded = seq + 2 * REACH
    last, *x_parts = tie(last, *x_parts)
    first_c, last_c = send(first, step_c), send(last, step_c)
    w_full, x_full, normed, residual, slope, bias_all = call(
        conv_forward,
        lengths,
        (*x_parts, vectors, *conv_parts),
        (
            S((KERNEL, full, full), bf16),
            S((seq, full), bf16),
            S((seq, full), bf16),
            *(S((seq, full), f32),) * 2,
            S((nmp, part // own, own), f32),
        ),
        [
            pltpu.VMEM((padded + 8, full), f32),
            pltpu.VMEM((2, padded, full), bf16),
            pltpu.VMEM((KERNEL, full, full), bf16),
            pltpu.VMEM((nmp, 4 * part // own, own), bf16),
            pltpu.SemaphoreType.DMA((8, nz)),
            pltpu.SemaphoreType.DMA((3, nmp)),
        ],
        2 * seq * KERNEL * full * full,
        24,
        (0, 1, 2, 3, *range(5, 13)),
        (0,),
    )
    *tied, residual = tie(first, first_x, first_c, last, last_x, last_c, *c_blocks[:2], *c_parts, residual)
    first, first_x, first_c, last, last_x, last_c, *c_parts = tied
    c_parts[1] = lax.ppermute(c_parts[1], "mp", within[1])
    ffn_parts = [first, first_x, first_c, send(first_x, step_c)]
    ffn_parts += [last, last_x, last_c, send(last_x, step_c)]
    block_rel, active, hidden_grad, second, mix_grad, hidden_full, bias_grad = call(
        ffn_hidden,
        lengths,
        (x_full, residual, *c_parts, vectors, bias_all.reshape(1, hidden), *ffn_parts),
        (
            S((nmp, seq, own), bf16),
            *(S((seq, hidden), bf16),) * 2,
            *(S((seq, full), bf16),) * 2,
            S((full, hidden), bf16),
            S((1, hidden), f32),
        ),
        [
            pltpu.VMEM((2, full, hidden), bf16),
            pltpu.SemaphoreType.DMA((8, nz, 2)),
            pltpu.SemaphoreType.DMA((2, nmp)),
        ],
        6 * seq * hidden * full,
        20,
        (2, 3, 4, 5, *range(8, 16)),
        (5,),
    )
    block_parts = [block_rel[k] for k in range(nmp)]
    for k in (1, 2):
        block_parts[k] = lax.ppermute(block_parts[k], "mp", within[k])
    ffn_keep, ffn_give = call(
        ffn_weight_grad,
        lengths,
        (second, hidden_grad, mix_grad, active),
        (S((2, 2, nz, 2, di, part), bf16),) * 2,
        [],
        4 * seq * hidden * full,
        12,
    )
    ffn_give, ffn_keep, hidden_grad, *block_parts[1:] = tie(
        ffn_give, ffn_keep, hidden_grad, *block_parts[1:]
    )
    ffn_r = send(ffn_give, step_c)
    block_parts[3] = lax.ppermute(block_parts[3], "mp", within[3])
    resid_grad, conv_grad, vgrad_two = call(
        norm_backward,
        lengths,
        (residual, slope, mix_grad, hidden_grad, hidden_full, vectors),
        (S((seq, full), f32), S((2, padded, full), bf16), S((8, full), f32)),
        [pltpu.VMEM((padded + 8, full), f32)],
        2 * seq * hidden * full,
        16,
    )
    ffn_sum, conv_grad, block_parts[3] = tie(scatter_b(ffn_keep, ffn_r), conv_grad, block_parts[3])
    ffn_rb = send(ffn_sum, step_yx)
    conv_keep, conv_give = call(
        conv_weight_grad,
        lengths,
        (normed, conv_grad),
        (S((2, 2, nz, KERNEL, di, own), bf16),) * 2,
        [],
        2 * seq * KERNEL * full * full,
        16,
    )
    conv_give, conv_keep, conv_grad, ffn_rb = tie(conv_give, conv_keep, conv_grad, ffn_rb)
    conv_r = send(conv_give, step_c)
    ffn_ra = send(scatter_a(ffn_keep, ffn_r, ffn_rb), step_xy)
    in_rel, vgrad_one = call(
        conv_backward,
        lengths,
        (x_full, conv_grad, resid_grad, w_full, vectors),
        (S((nmp, seq, own), bf16), S((8, full), f32)),
        [],
        1,
        16,
    )
    conv_sum, in_rel, ffn_ra = tie(scatter_b(conv_keep, conv_r), in_rel, ffn_ra)
    conv_rb = send(conv_sum, step_yx)
    ffn_own, ffn_rest = scatter_z(ffn_keep, ffn_r, ffn_rb, ffn_ra)
    ffn_share = add(ffn_own, *ffn_rest)
    conv_sum, ffn_share = tie(scatter_a(conv_keep, conv_r, conv_rb), ffn_share)
    conv_ra = send(conv_sum, step_xy)
    conv_ra, in_rel = tie(conv_ra, in_rel)
    conv_own, conv_rest = scatter_z(conv_keep, conv_r, conv_rb, conv_ra)
    for part_of in conv_rest[3:]:
        conv_own = conv_own + part_of.astype(f32)
    in_parts = swap([in_rel[k] for k in range(nmp)])
    conv_own, *tied = tie(conv_own, *conv_rest[:3], *in_parts)
    conv_rest, in_parts = tied[:3], tied[3:]
    block_output = in_order(block_parts)
    input_grad = in_order(in_parts).astype(f32)

    conv_share, small = call(
        total_share,
        lengths,
        (conv_own, *conv_rest, ffn_share, vgrad_one, vgrad_two, bias_grad),
        (S((KERNEL, di, own), f32), S((7 + hidden // full, full), f32)),
        [],
        1,
        16,
    )
    small, small_far = all_sum(small)
    matrices = (
        *(conv_master, conv_first, conv_second),
        *(hidden_master, hidden_first, hidden_second),
        *(output_master.T, output_first.T, output_second.T),
    )
    vector_ones = (vectors, vector_first, vector_second)
    bias_ones = [v.reshape(1, part) for v in (hidden_bias, bias_first, bias_second)]
    states = (*matrices, *vector_ones, *bias_ones)
    *updated, norm = call(
        update,
        lengths,
        (small, small_far, conv_share, ffn_share, *states),
        (*(S(v.shape, f32) for v in states), S((1, 1), f32)),
        [pltpu.VMEM(small.shape, f32)],
        1,
        16,
    )
    updated[6:9] = [v.T for v in updated[6:9]]
    updated[12:] = [v.reshape(part) for v in updated[12:]]
    return (block_output, input_grad, norm.reshape(()), *updated)


def solution(mesh):
    rows = P("dp", None, "mp")
    conv = P(None, "dp", "mp")
    hid = P("dp", "mp")
    out = P("mp", "dp")
    return jax.shard_map(
        functools.partial(per_device, mesh.shape["dp"], mesh.shape["mp"]),
        mesh=mesh,
        in_specs=(rows, rows, P("dp"), *(conv, hid, out) * 3, *(P(),) * 3, *(P("mp"),) * 3),
        out_specs=(
            rows,
            rows,
            P(),
            *(conv,) * 3,
            *(hid,) * 3,
            *(out,) * 3,
            *(P(),) * 3,
            *(P("mp"),) * 3,
        ),
        check_vma=False,
    )
```

```python
import functools

import jax
import jax.numpy as jnp
from jax import lax
from jax.experimental import pallas as pl
from jax.experimental.pallas import tpu as pltpu
from jax.sharding import PartitionSpec as P

KERNEL = 9
DILATION = 8
REACH = DILATION * (KERNEL // 2)
STEP = 10
ROWS = 256

NORM_EPS = 1e-05
BETA_ONE = 0.9
BETA_TWO = 0.999
ADAM_EPS = 1e-08
MATRIX_RATE = 0.03
VECTOR_RATE = 0.3
WEIGHT_DECAY = 0.01
CLIP_NORM = 1.0

f32 = jnp.float32
bf16 = jnp.bfloat16
NN = (((1,), (0,)), ((), ()))
NT = (((1,), (1,)), ((), ()))


def dot(a, b, dims=NN):
    return lax.dot_general(a, b, dims, preferred_element_type=f32)


def phi_of(v):
    return 0.5 * (1.0 + lax.erf(v * 0.7071067811865476))


def slope_of(v, phi):
    return phi + v * jnp.exp(-0.5 * v * v) * 0.3989422804014327


def norm_parts(v):
    centre = v - jnp.mean(v, axis=-1, keepdims=True)
    inverse = lax.rsqrt(jnp.mean(centre * centre, axis=-1, keepdims=True) + NORM_EPS)
    return centre * inverse, inverse


def norm_back(e, s, inverse):
    return inverse * (
        e - jnp.mean(e, axis=-1, keepdims=True) - s * jnp.mean(e * s, axis=-1, keepdims=True)
    )


def source_of(place, dc, b, a, dz):
    dp, mp = place[0], place[1]
    flip = (mp & 1) ^ dc
    fx = jnp.where(flip == 0, a, b)
    fy = jnp.where(flip == 0, b, a)
    d = ((dp >> 1) ^ dz) * 2 + ((dp & 1) ^ fx)
    m = ((mp >> 1) ^ fy) * 2 + ((mp & 1) ^ dc)
    return d, m


def share_index(place, d, parity, j):
    dp, mp = place[0], place[1]
    fx = (dp & 1) ^ (d & 1)
    fy = (mp >> 1) ^ j
    odd = parity == 1
    return jnp.where(odd, fx, fy), jnp.where(odd, fy, fx), (dp >> 1) ^ (d >> 1)


def store_columns(place, outs, rows, values):
    for k, out in enumerate(outs):
        own = out.shape[1]
        out[rows, :] = values[:, pl.ds(mult((place[1] ^ k) * own, own), own)]


def for_blocks(blocks, most, step):
    @pl.when(blocks == most)
    def _():
        for i in range(most):
            step(i, 0)

    @pl.when(blocks != most)
    def _():
        lax.fori_loop(0, blocks, step, 0)


def mult(v, n):
    return v if isinstance(v, int) else pl.multiple_of(v, n)


def put_shifted(pair, last, row, values):
    count = values.shape[0]
    pair[0, pl.ds(mult(row + REACH, 16), count), :] = values.astype(bf16)
    moved = jnp.concatenate([last[...], values[: count - DILATION]])
    pair[1, pl.ds(mult(row + REACH - 2 * DILATION, 16), count), :] = moved.astype(bf16)
    last[...] = values[count - DILATION :]


def clear_shifted(pair, last):
    width = pair.shape[2]
    pair[0, 0:REACH, :] = jnp.zeros((REACH, width), bf16)
    pair[1, 0 : REACH - 2 * DILATION, :] = jnp.zeros((REACH - 2 * DILATION, width), bf16)
    last[...] = jnp.zeros_like(last)


def end_shifted(pair, last, length, blocks, most):
    width = pair.shape[2]
    tail = jnp.concatenate([last[...], jnp.zeros_like(last)]).astype(bf16)
    pair[1, pl.ds(mult(length + REACH - 2 * DILATION, 16), 2 * DILATION), :] = tail

    def clear(i, _):
        for j in (0, 1):
            rows = pl.ds(mult(i * ROWS + REACH, 16), ROWS)
            pair[j, rows, :] = jnp.zeros((ROWS, width), bf16)
        return 0

    lax.fori_loop(blocks, most, clear, 0)
    for j in (0, 1):
        pair[j, most * ROWS + REACH :, :] = jnp.zeros((REACH, width), bf16)


SLOTS = tuple((dc, b, a) for dc in (0, 1) for b, a in ((0, 0), (0, 1), (1, 0), (1, 1)))


def fetch_rows(place, parts, whole, sems):
    seq, own = whole.shape[0], parts[0].shape[1]
    copies = []
    for k, part in enumerate(parts):
        target = whole.at[:, pl.ds(mult((place[1] ^ k) * own, own), own)]
        copies.append(pltpu.make_async_copy(part.at[pl.ds(0, seq), :], target, sems.at[k]))
        copies[-1].start()
    return copies


def fetch_shards(shards, sems):
    copies = []
    for index, shard, whole, d, m in shards:
        di, cols = shard.shape[-2:]
        target = whole.at[
            (slice(None),) * (len(shard.shape) - 2)
            + (pl.ds(mult(d * di, di), di), pl.ds(mult(m * cols, cols), cols))
        ]
        copies.append(pltpu.make_async_copy(shard, target, sems.at[index]))
        copies[-1].start()
    return copies


def conv_forward(place, x0, x1, x2, x3, vec, *rest):
    pieces = rest[:8]
    w_out, x_out, na_out, resid, slope, bias_out, nab, last, whole, extra, sems, x_sem = rest[8:]
    full = vec.shape[1]
    seq, own = x_out.shape[0], x0.shape[1]
    length, blocks = place[2:]

    x_parts = (x0, x1, x2, x3)
    rows = fetch_rows(place, x_parts, x_out, x_sem.at[0])
    shards = fetch_shards(
        [
            ((slot, z), piece.at[z], whole, *source_of(place, *index, z))
            for slot, (index, piece) in enumerate(zip(SLOTS, pieces))
            for z in range(piece.shape[0])
        ],
        sems,
    )
    extras = [
        pltpu.make_async_copy(part.at[pl.ds(seq, extra.shape[1]), :], extra.at[k], x_sem.at[1, k])
        for k, part in enumerate(x_parts)
    ]
    for copy in extras:
        copy.start()
    for copy in rows + extras:
        copy.wait()
    for k in range(len(x_parts)):
        values = extra[k].astype(f32)
        units = values.shape[0] // 4
        bias_out[place[1] ^ k] = (values[0:units] + values[units : 2 * units]) + values[
            2 * units : 3 * units
        ]

    gain = vec[0:1, :]
    shift = vec[1:2, :]
    clear_shifted(nab, last)

    def norm_step(i, _):
        row = mult(i * ROWS, ROWS)
        rows = pl.ds(row, ROWS)
        scaled, _ = norm_parts(x_out[rows, :].astype(f32))
        values = scaled * gain + shift
        put_shifted(nab, last, row, values)
        na_out[rows, :] = values.astype(bf16)
        return 0

    def idle_step(i, _):
        na_out[pl.ds(mult(i * ROWS, ROWS), ROWS), :] = jnp.zeros((ROWS, full), bf16)
        return 0

    lax.fori_loop(0, blocks, norm_step, 0)
    lax.fori_loop(blocks, seq // ROWS, idle_step, 0)
    end_shifted(nab, last, length, blocks, seq // ROWS)
    for copy in shards:
        copy.wait()
    w_copy = pltpu.make_async_copy(whole, w_out, x_sem.at[2, 0])
    w_copy.start()

    def conv_step(i, _):
        row = mult(i * ROWS, ROWS)
        window = jnp.concatenate(
            [
                nab[t & 1, pl.ds(mult(row + DILATION * (t - (t & 1)), 16), ROWS), :]
                for t in range(KERNEL)
            ],
            axis=1,
        )
        weights = whole[...].reshape(KERNEL * full, full)
        rows = pl.ds(row, ROWS)
        conv = dot(window, weights) + vec[2:3, :]
        phi = phi_of(conv)
        resid[rows, :] = x_out[rows, :].astype(f32) + conv * phi
        slope[rows, :] = slope_of(conv, phi)
        return 0

    for_blocks(blocks, seq // ROWS, conv_step)
    w_copy.wait()


def ffn_hidden(place, x_full, resid, c0, c1, c2, c3, vec, hbias, *rest):
    pieces = rest[:8]
    outs, (act, hg, sec, mg, wh_out) = rest[8:12], rest[12:17]
    whole, values_ref, sems, c_sem = rest[17:]
    wh, wo = whole.at[0], whole.at[1]
    seq, full = x_full.shape
    hidden = hbias.shape[1]
    blocks = place[3]

    rows = fetch_rows(place, (c0, c1, c2, c3), mg, c_sem.at[0])
    shards = []
    for slot, piece in enumerate(pieces):
        w, dc, dx = slot >> 2, (slot >> 1) & 1, slot & 1
        for z in range(piece.shape[0]):
            for dy in (0, 1):
                d = ((place[0] >> 1) ^ z) * 2 + ((place[0] & 1) ^ dx)
                m = place[1] ^ (dy * 2 + dc)
                shards.append(((slot, z, dy), piece.at[z, dy], whole.at[w], d, m))
    shards = fetch_shards(shards, sems)
    for copy in rows + shards:
        copy.wait()
    wh_copy = pltpu.make_async_copy(wh, wh_out, c_sem.at[1, 0])
    wh_copy.start()

    def row_step(i, _):
        rows = pl.ds(mult(i * ROWS, ROWS), ROWS)
        residual = resid[rows, :]
        s, _ = norm_parts(residual)
        second = (s * vec[3:4, :] + vec[4:5, :]).astype(bf16)
        sec[rows, :] = second
        grad = mg[rows, :]
        for j in range(hidden // 512):
            cols = slice(j * 512, (j + 1) * 512)
            h = dot(second, wh[:, cols]) + hbias[0:1, cols]
            phi = phi_of(h)
            act[rows, cols] = (h * phi).astype(bf16)
            hidden_grad = (dot(grad, wo[:, cols]) * slope_of(h, phi)).astype(bf16)
            hg[rows, cols] = hidden_grad
        mixed = dot(act[rows, :], wo[...], NT)
        values_ref[...] = (residual + (mixed + vec[5:6, :])).astype(bf16)
        store_columns(place, outs, rows, values_ref)
        return 0

    def idle_step(i, _):
        rows = pl.ds(mult(i * ROWS, ROWS), ROWS)
        values_ref[...] = x_full[rows, :]
        store_columns(place, outs, rows, values_ref)
        sec[rows, :] = jnp.zeros((ROWS, full), bf16)
        for ref in (act, hg):
            ref[rows, :] = jnp.zeros((ROWS, hidden), bf16)
        return 0

    for_blocks(blocks, seq // ROWS, row_step)
    lax.fori_loop(blocks, seq // ROWS, idle_step, 0)
    wh_copy.wait()


def norm_backward(place, resid, slope, grad, hg, wh, vec, resid_out, cab, vgrad, last):
    seq = resid.shape[0]
    length, blocks = place[2:]
    vgrad[...] = jnp.zeros_like(vgrad)
    clear_shifted(cab, last)

    def row_step(i, _):
        row = mult(i * ROWS, ROWS)
        rows = pl.ds(row, ROWS)
        second_grad = dot(hg[rows, :], wh[...], NT)
        s, inverse = norm_parts(resid[rows, :])
        up = grad[rows, :].astype(f32)
        vgrad[3:4, :] += jnp.sum(second_grad * s, axis=0, keepdims=True)
        vgrad[4:5, :] += jnp.sum(second_grad, axis=0, keepdims=True)
        vgrad[5:6, :] += jnp.sum(up, axis=0, keepdims=True)
        resid_grad = up + norm_back(second_grad * vec[3:4, :], s, inverse)
        resid_out[rows, :] = resid_grad
        rounded = (resid_grad * slope[rows, :]).astype(bf16).astype(f32)
        put_shifted(cab, last, row, rounded)
        vgrad[2:3, :] += jnp.sum(rounded, axis=0, keepdims=True)
        return 0

    def idle_step(i, _):
        rows = pl.ds(mult(i * ROWS, ROWS), ROWS)
        resid_out[rows, :] = grad[rows, :].astype(f32)
        return 0

    for_blocks(blocks, seq // ROWS, row_step)
    lax.fori_loop(blocks, seq // ROWS, idle_step, 0)

    end_shifted(cab, last, length, blocks, seq // ROWS)


def ffn_weight_grad(place, sec, hg, mg, act, keep, give, hbgrad):
    seq, full = sec.shape
    di, part = keep.shape[4:]
    sec_t = jnp.concatenate([sec[...].T, jnp.ones((16, seq), bf16)])
    mg_t = mg[...].T
    for half, ref in enumerate((keep, give)):
        parity = (place[1] & 1) ^ half
        for j in range(keep.shape[1]):
            cols = pl.ds(mult((parity + 2 * j) * part, part), part)
            for w, (left, right) in enumerate(((sec_t, hg), (mg_t, act))):
                value = dot(left, right[:, cols])
                if w == 0:
                    hbgrad[0:1, cols] = value[full : full + 1, :]
                value = value.astype(bf16)
                for d in range(full // di):
                    index = share_index(place, d, parity, j)
                    ref[(*index, w)] = value[d * di : (d + 1) * di, :]


def shifted_rows(cab, u, row, count):
    odd = u & 1
    return cab[odd, pl.ds(mult(row + (u - odd) * DILATION, 16), count), :]


def conv_weight_grad(place, na, cab, keep, *gives):
    seq, full = na.shape
    taps, di, own = keep.shape[3:]
    na_t = na[...].T
    for t in range(taps):
        u = KERNEL - 1 - t
        odd = u & 1
        rows = pl.ds((u - odd) * DILATION, seq)
        group, local = divmod(t, gives[0].shape[3])
        for half, (ref, tap) in enumerate(((keep, t), (gives[group], local))):
            parity = (place[1] & 1) ^ half
            blocks = range(keep.shape[1])
            cols = [pl.ds(mult((parity + 2 * j) * own, own), own) for j in blocks]
            right = jnp.concatenate([cab[odd, rows, c] for c in cols], axis=1)
            value = dot(na_t, right).astype(bf16)
            for j in blocks:
                for d in range(full // di):
                    index = share_index(place, d, parity, j)
                    ref[(*index, tap)] = value[d * di : (d + 1) * di, j * own : (j + 1) * own]


def pair_sum(place, keep, r0, r1, r2, onward, own):
    count = r0.shape[3]
    for group, received in enumerate((r0, r1, r2)):
        taps = pl.ds(group * count, count)
        for a in range(keep.shape[1]):
            both = keep[1, a, :, taps].astype(f32) + received[1, a].astype(f32)
            onward[a, :, taps] = both.astype(bf16)
            own[a, :, taps] = keep[0, a, :, taps].astype(f32) + received[0, a].astype(f32)


def conv_backward(place, x_full, cab, resid, w, vec, *rest):
    outs, (vgrad, values_ref) = rest[:4], rest[4:]
    seq, full = x_full.shape
    blocks = place[3]
    vgrad[...] = jnp.zeros_like(vgrad)

    def in_store(rows, values):
        values_ref[...] = values.astype(bf16)
        store_columns(place, outs, rows, values_ref)

    def row_step(i, _):
        row = mult(i * ROWS, ROWS)
        rows = pl.ds(row, ROWS)
        total = jnp.zeros((ROWS, full), f32)
        for t in range(KERNEL):
            shifted = shifted_rows(cab, KERNEL - 1 - t, row, ROWS)
            total = total + dot(shifted, w[t], NT)
        s, inverse = norm_parts(x_full[rows, :].astype(f32))
        vgrad[0:1, :] += jnp.sum(total * s, axis=0, keepdims=True)
        vgrad[1:2, :] += jnp.sum(total, axis=0, keepdims=True)
        in_store(rows, resid[rows, :] + norm_back(total * vec[0:1, :], s, inverse))
        return 0

    def idle_step(i, _):
        rows = pl.ds(mult(i * ROWS, ROWS), ROWS)
        in_store(rows, resid[rows, :])
        return 0

    for_blocks(blocks, seq // ROWS, row_step)
    lax.fori_loop(blocks, seq // ROWS, idle_step, 0)


def tie(*values):
    return lax.optimization_barrier(values)


def placed(kernel):
    def run(lengths, *refs):
        mp = lax.axis_index("mp")
        length = lengths[mp]
        kernel((lax.axis_index("dp"), mp, length, length // ROWS), *refs)

    return run


def call(kernel, lengths, args, outs, scratch, flops, mib, far=(), far_out=()):
    near = pl.BlockSpec(memory_space=pltpu.VMEM)
    left = pl.BlockSpec(memory_space=pltpu.HBM)
    moved = sum(a.size * a.dtype.itemsize for a in (*args, *outs))
    return pl.pallas_call(
        placed(kernel),
        out_shape=outs,
        in_specs=[pl.BlockSpec(memory_space=pltpu.SMEM)]
        + [left if i in far else near for i in range(len(args))],
        out_specs=[left if i in far_out else near for i in range(len(outs))],
        scratch_shapes=scratch,
        compiler_params=pltpu.CompilerParams(vmem_limit_bytes=mib * 2**20),
        cost_estimate=pl.CostEstimate(flops=flops, bytes_accessed=moved, transcendentals=0),
    )(lengths, *args)


def total_share(place, conv_own, c1, c2, c3, ffn_share, v1, v2, bias_grad, conv_share, small):
    full = small.shape[1]
    total = conv_own[...]
    for part in (c1, c2, c3):
        total = total + part[...].astype(f32)
    conv_share[...] = total
    squares = jnp.sum(total * total) + jnp.sum(ffn_share[...] * ffn_share[...])
    small[0:6, :] = (v1[...] + v2[...])[0:6, :]
    units = bias_grad.shape[1] // full
    for row in range(units):
        small[6 + row : 7 + row, :] = bias_grad[:, row * full : (row + 1) * full]
    small[6 + units :, :] = jnp.full((small.shape[0] - 6 - units, full), squares, f32)


def adam(weight, first_mom, second, gradient, clip_scale, step_rate, decay_rate):
    clipped = gradient * clip_scale
    first_new = BETA_ONE * first_mom + (1.0 - BETA_ONE) * clipped
    second_new = BETA_TWO * second + (1.0 - BETA_TWO) * clipped * clipped
    update_dir = (
        first_new
        / (1.0 - BETA_ONE**STEP)
        / (jnp.sqrt(second_new / (1.0 - BETA_TWO**STEP)) + ADAM_EPS)
    )
    return (weight - step_rate * (update_dir + decay_rate * weight), first_new, second_new)


def update(place, small, small_far, conv_share, ffn_share, *rest):
    states, outs, total = rest[:15], rest[15:31], rest[31]
    total[...] = small[...] + small_far[...]
    rows = total.shape[0] - 1
    own_rows = total[0:rows, :]
    squares = jnp.sum(own_rows * own_rows, axis=(0, 1), keepdims=True) + total[rows:, 0:1]
    norm = jnp.sqrt(squares)
    outs[15][...] = jnp.broadcast_to(norm, outs[15].shape)
    clip_scale = jnp.minimum(1.0, CLIP_NORM / (norm + 1e-06))
    gradients = [
        conv_share[...],
        ffn_share[0],
        ffn_share[1],
        total[0:6, :],
        total[pl.ds(6 + place[1], 1), :],
    ]
    for i, gradient in enumerate(gradients):
        rates = (MATRIX_RATE, WEIGHT_DECAY) if i < 3 else (VECTOR_RATE, 0.0)
        scale = clip_scale.reshape((1,) * gradient.ndim)
        state = [ref[...] for ref in states[3 * i : 3 * i + 3]]
        for ref, value in zip(outs[3 * i : 3 * i + 3], adam(*state, gradient, scale, *rates)):
            ref[...] = value


def per_device(
    ndp,
    nmp,
    inputs,
    cotangent,
    lengths,
    conv_master,
    hidden_master,
    output_master,
    conv_first,
    hidden_first,
    output_first,
    conv_second,
    hidden_second,
    output_second,
    vectors,
    vector_first,
    vector_second,
    hidden_bias,
    bias_first,
    bias_second,
):
    axes = ("dp", "mp")
    nz = ndp // 2
    seq, own = inputs.shape[1:]
    full = vectors.shape[1]
    part = hidden_bias.shape[0]
    hidden = part * nmp
    di = full // ndp
    mp = lax.axis_index("mp")

    def perm(move):
        pairs = []
        for i in range(ndp * nmp):
            d, m = divmod(i, nmp)
            z, x, y, c = move(d >> 1, d & 1, m >> 1, m & 1)
            pairs.append((i, (z * 2 + x) * nmp + y * 2 + c))
        return pairs

    across_z = [perm(lambda z, x, y, c, k=k: (z ^ k, x, y, c)) for k in range(nz)]
    step_x = perm(lambda z, x, y, c: (z, x ^ 1, y, c))
    step_y = perm(lambda z, x, y, c: (z, x, y ^ 1, c))
    step_c = perm(lambda z, x, y, c: (z, x, y, c ^ 1))
    step_xy = perm(lambda z, x, y, c: (z, x ^ 1, y, c) if c == 0 else (z, x, y ^ 1, c))
    step_yx = perm(lambda z, x, y, c: (z, x, y ^ 1, c) if c == 0 else (z, x ^ 1, y, c))
    within = [[(i, i ^ k) for i in range(nmp)] for k in range(nmp)]

    def send(values, pairs):
        return lax.ppermute(values, axes, pairs)

    def gather_z(shard):
        return [shard] + [send(shard, across_z[k]) for k in range(1, nz)]

    def add(*terms):
        total = terms[0].astype(f32)
        for term in terms[1:]:
            total = total + term.astype(f32)
        return total

    def scatter_b(k, r):
        return add(k[1], r[1]).astype(bf16)

    def scatter_a(k, r, rb):
        return add(k[0, 1], r[0, 1], rb[1]).astype(bf16)

    def scatter_z(*terms):
        own_part = add(*(t[0] for t in terms))
        parts = [add(*(t[j] for t in terms)).astype(bf16) for j in range(1, nz)]
        return own_part, [send(part_of, across_z[j + 1]) for j, part_of in enumerate(parts)]

    def take_windows(values, extra=None):
        blocks = [lax.dynamic_index_in_dim(values, mp ^ k, 0, False) for k in range(nmp)]
        if extra is not None:
            blocks = [jnp.concatenate([block, extra]) for block in blocks]
        return blocks

    def swap(blocks):
        return [blocks[0]] + [lax.ppermute(blocks[k], "mp", within[k]) for k in range(1, nmp)]

    def in_order(pieces):
        for bit in range(nmp.bit_length() - 1):
            odd = ((mp >> bit) & 1) == 1
            pieces = [jnp.where(odd, pieces[k ^ (1 << bit)], pieces[k]) for k in range(nmp)]
        return jnp.stack(pieces)

    def all_sum(values):
        values = values + send(values, step_c)
        step = 1
        while step < nz:
            values = values + send(values, across_z[step])
            step *= 2
        values = values + send(values, step_x)
        return values, send(values, step_y)

    exact, rest = [], hidden_bias
    for _ in range(3):
        exact.append(lax.reduce_precision(rest, 8, 7))
        rest = rest - exact[-1]
    exact.append(jnp.zeros_like(rest))
    exact = jnp.concatenate(exact).reshape(4 * part // own, own).astype(bf16)
    ffn_shard = jnp.stack([hidden_master.astype(bf16), output_master.astype(bf16).T])

    x_blocks = take_windows(inputs, exact)
    *x_blocks, conv_shard = tie(*x_blocks, conv_master.astype(bf16))
    x_parts = swap(x_blocks)
    conv_z = gather_z(conv_shard)
    ffn_y = send(ffn_shard, step_y)
    *tied, ffn_shard, ffn_y = tie(*x_parts, *conv_z, ffn_shard, ffn_y)
    x_parts, conv_z = tied[:nmp], jnp.stack(tied[nmp:])
    first, last = [jnp.stack([ffn_shard[w], ffn_y[w]]) for w in (0, 1)]
    conv_a, conv_b = send(conv_z, step_xy), send(conv_z, step_yx)
    first = gather_z(first)
    conv_z, conv_a, conv_b, last, *first = tie(conv_z, conv_a, conv_b, last, *first)
    conv_ab = send(conv_a, step_yx)
    first = jnp.stack(first)
    first_x = send(first, step_x)
    last = gather_z(last)
    conv_z, conv_a, conv_b, conv_ab, cotangent, first, first_x, *last = tie(
        conv_z, conv_a, conv_b, conv_ab, cotangent, first, first_x, *last
    )
    conv_parts = [conv_z, conv_a, conv_b, conv_ab]
    conv_parts += [send(part_of, step_c) for part_of in conv_parts]
    last = jnp.stack(last)
    last_x = send(last, step_x)
    c_blocks = take_windows(cotangent)
    c_parts = [lax.ppermute(c_blocks[k], "mp", within[k]) for k in range(2, nmp)]

    S = jax.ShapeDtypeStruct
    padded = seq + 2 * REACH
    last, *x_parts = tie(last, *x_parts)
    first_c, last_c = send(first, step_c), send(last, step_c)
    w_full, x_full, normed, residual, slope, bias_all = call(
        conv_forward,
        lengths,
        (*x_parts, vectors, *conv_parts),
        (
            S((KERNEL, full, full), bf16),
            S((seq, full), bf16),
            S((seq, full), bf16),
            *(S((seq, full), f32),) * 2,
            S((nmp, part // own, own), f32),
        ),
        [
            pltpu.VMEM((2, padded, full), bf16),
            pltpu.VMEM((DILATION, full), f32),
            pltpu.VMEM((KERNEL, full, full), bf16),
            pltpu.VMEM((nmp, 4 * part // own, own), bf16),
            pltpu.SemaphoreType.DMA((8, nz)),
            pltpu.SemaphoreType.DMA((3, nmp)),
        ],
        2 * seq * KERNEL * full * full,
        24,
        (0, 1, 2, 3, *range(5, 13)),
        (0,),
    )
    *tied, residual = tie(first, first_x, first_c, last, last_x, last_c, *c_blocks[:2], *c_parts, residual)
    first, first_x, first_c, last, last_x, last_c, *c_parts = tied
    c_parts[1] = lax.ppermute(c_parts[1], "mp", within[1])
    ffn_parts = [first, first_x, first_c, send(first_x, step_c)]
    ffn_parts += [last, last_x, last_c, send(last_x, step_c)]
    *block_parts, active, hidden_grad, second, mix_grad, hidden_full = call(
        ffn_hidden,
        lengths,
        (x_full, residual, *c_parts, vectors, bias_all.reshape(1, hidden), *ffn_parts),
        (
            *(S((seq, own), bf16),) * nmp,
            *(S((seq, hidden), bf16),) * 2,
            *(S((seq, full), bf16),) * 2,
            S((full, hidden), bf16),
        ),
        [
            pltpu.VMEM((2, full, hidden), bf16),
            pltpu.VMEM((ROWS, full), bf16),
            pltpu.SemaphoreType.DMA((8, nz, 2)),
            pltpu.SemaphoreType.DMA((2, nmp)),
        ],
        6 * seq * hidden * full,
        20,
        (2, 3, 4, 5, *range(8, 16)),
        (8,),
    )
    for k in (1, 2):
        block_parts[k] = lax.ppermute(block_parts[k], "mp", within[k])
    ffn_keep, ffn_give, bias_grad = call(
        ffn_weight_grad,
        lengths,
        (second, hidden_grad, mix_grad, active),
        (*(S((2, 2, nz, 2, di, part), bf16),) * 2, S((1, hidden), f32)),
        [],
        1,
        12,
    )
    ffn_give, ffn_keep, hidden_grad, *block_parts[1:] = tie(
        ffn_give, ffn_keep, hidden_grad, *block_parts[1:]
    )
    ffn_r = send(ffn_give, step_c)
    block_parts[3] = lax.ppermute(block_parts[3], "mp", within[3])
    resid_grad, conv_grad, vgrad_two = call(
        norm_backward,
        lengths,
        (residual, slope, mix_grad, hidden_grad, hidden_full, vectors),
        (S((seq, full), f32), S((2, padded, full), bf16), S((8, full), f32)),
        [pltpu.VMEM((DILATION, full), f32)],
        1,
        16,
    )
    ffn_sum, conv_grad, block_parts[3] = tie(scatter_b(ffn_keep, ffn_r), conv_grad, block_parts[3])
    ffn_rb = send(ffn_sum, step_yx)
    conv_keep, *conv_give = call(
        conv_weight_grad,
        lengths,
        (normed, conv_grad),
        (S((2, 2, nz, KERNEL, di, own), bf16), *(S((2, 2, nz, KERNEL // 3, di, own), bf16),) * 3),
        [],
        1,
        16,
    )
    *conv_give, conv_keep, conv_grad = tie(*conv_give, conv_keep, conv_grad)
    conv_r = [send(give, step_c) for give in conv_give]
    *in_parts, vgrad_one = call(
        conv_backward,
        lengths,
        (x_full, conv_grad, resid_grad, w_full, vectors),
        (*(S((seq, own), bf16),) * nmp, S((8, full), f32)),
        [pltpu.VMEM((ROWS, full), bf16)],
        1,
        16,
    )
    ffn_sum = scatter_a(ffn_keep, ffn_r, ffn_rb)
    *conv_r, ffn_sum, in_parts[1] = tie(*conv_r, ffn_sum, in_parts[1])
    conv_sum, conv_own = call(
        pair_sum,
        lengths,
        (conv_keep, *conv_r),
        (S((2, nz, KERNEL, di, own), bf16), S((2, nz, KERNEL, di, own), f32)),
        [],
        1,
        16,
    )
    conv_rb = send(conv_sum, step_yx)
    ffn_ra = send(ffn_sum, step_xy)
    ffn_own, ffn_rest = scatter_z(ffn_keep[0, 0], ffn_r[0, 0], ffn_rb[0], ffn_ra)
    ffn_share = add(ffn_own, *ffn_rest)
    conv_ra = send(add(conv_own[1], conv_rb[1]).astype(bf16), step_xy)
    conv_ra, *in_parts[2:] = tie(conv_ra, *in_parts[2:])
    conv_own, conv_rest = scatter_z(conv_own[0], conv_rb[0], conv_ra)
    for part_of in conv_rest[3:]:
        conv_own = conv_own + part_of.astype(f32)
    for k in range(1, nmp):
        in_parts[k] = lax.ppermute(in_parts[k], "mp", within[k])
    conv_own, *tied = tie(conv_own, *conv_rest[:3], *in_parts)
    conv_rest, in_parts = tied[:3], tied[3:]
    block_output = in_order(block_parts)
    input_grad = in_order(in_parts).astype(f32)

    conv_share, small = call(
        total_share,
        lengths,
        (conv_own, *conv_rest, ffn_share, vgrad_one, vgrad_two, bias_grad),
        (S((KERNEL, di, own), f32), S((7 + hidden // full, full), f32)),
        [],
        1,
        16,
    )
    small, small_far = all_sum(small)
    matrices = (
        *(conv_master, conv_first, conv_second),
        *(hidden_master, hidden_first, hidden_second),
        *(output_master.T, output_first.T, output_second.T),
    )
    vector_ones = (vectors, vector_first, vector_second)
    bias_ones = [v.reshape(1, part) for v in (hidden_bias, bias_first, bias_second)]
    states = (*matrices, *vector_ones, *bias_ones)
    *updated, norm = call(
        update,
        lengths,
        (small, small_far, conv_share, ffn_share, *states),
        (*(S(v.shape, f32) for v in states), S((1, 1), f32)),
        [pltpu.VMEM(small.shape, f32)],
        1,
        16,
    )
    updated[6:9] = [v.T for v in updated[6:9]]
    updated[12:] = [v.reshape(part) for v in updated[12:]]
    return (block_output, input_grad, norm.reshape(()), *updated)


def solution(mesh):
    rows = P("dp", None, "mp")
    conv = P(None, "dp", "mp")
    hid = P("dp", "mp")
    out = P("mp", "dp")
    return jax.shard_map(
        functools.partial(per_device, mesh.shape["dp"], mesh.shape["mp"]),
        mesh=mesh,
        in_specs=(rows, rows, P("dp"), *(conv, hid, out) * 3, *(P(),) * 3, *(P("mp"),) * 3),
        out_specs=(
            rows,
            rows,
            P(),
            *(conv,) * 3,
            *(hid,) * 3,
            *(out,) * 3,
            *(P(),) * 3,
            *(P("mp"),) * 3,
        ),
        check_vma=False,
    )
```

```python
import functools

import jax
import jax.numpy as jnp
from jax import lax
from jax.experimental import pallas as pl
from jax.experimental.pallas import tpu as pltpu
from jax.sharding import PartitionSpec as P

KERNEL = 9
DILATION = 8
REACH = DILATION * (KERNEL // 2)
STEP = 10
ROWS = 256

NORM_EPS = 1e-05
BETA_ONE = 0.9
BETA_TWO = 0.999
ADAM_EPS = 1e-08
MATRIX_RATE = 0.03
VECTOR_RATE = 0.3
WEIGHT_DECAY = 0.01
CLIP_NORM = 1.0

f32 = jnp.float32
bf16 = jnp.bfloat16
NN = (((1,), (0,)), ((), ()))
NT = (((1,), (1,)), ((), ()))


def dot(a, b, dims=NN):
    return lax.dot_general(a, b, dims, preferred_element_type=f32)


def phi_of(v):
    return 0.5 * (1.0 + lax.erf(v * 0.7071067811865476))


def slope_of(v, phi):
    return phi + v * jnp.exp(-0.5 * v * v) * 0.3989422804014327


def norm_parts(v):
    centre = v - jnp.mean(v, axis=-1, keepdims=True)
    inverse = lax.rsqrt(jnp.mean(centre * centre, axis=-1, keepdims=True) + NORM_EPS)
    return centre * inverse, inverse


def norm_back(e, s, inverse):
    return inverse * (
        e - jnp.mean(e, axis=-1, keepdims=True) - s * jnp.mean(e * s, axis=-1, keepdims=True)
    )


def source_of(place, dc, b, a, dz):
    dp, mp = place[0], place[1]
    flip = (mp & 1) ^ dc
    fx = jnp.where(flip == 0, a, b)
    fy = jnp.where(flip == 0, b, a)
    d = ((dp >> 1) ^ dz) * 2 + ((dp & 1) ^ fx)
    m = ((mp >> 1) ^ fy) * 2 + ((mp & 1) ^ dc)
    return d, m


def share_index(place, d, parity, j):
    dp, mp = place[0], place[1]
    fx = (dp & 1) ^ (d & 1)
    fy = (mp >> 1) ^ j
    odd = parity == 1
    return jnp.where(odd, fx, fy), jnp.where(odd, fy, fx), (dp >> 1) ^ (d >> 1)


def store_columns(place, outs, rows, values):
    for k, out in enumerate(outs):
        own = out.shape[1]
        out[rows, :] = values[:, pl.ds(mult((place[1] ^ k) * own, own), own)]


def mult(v, n):
    return v if isinstance(v, int) else pl.multiple_of(v, n)


def put_shifted(pair, last, row, values):
    count = values.shape[0]
    pair[0, pl.ds(mult(row + REACH, 16), count), :] = values.astype(bf16)
    moved = jnp.concatenate([last[...], values[: count - DILATION]])
    pair[1, pl.ds(mult(row + REACH - 2 * DILATION, 16), count), :] = moved.astype(bf16)
    last[...] = values[count - DILATION :]


def clear_shifted(pair, last):
    width = pair.shape[2]
    pair[0, 0:REACH, :] = jnp.zeros((REACH, width), bf16)
    pair[1, 0 : REACH - 2 * DILATION, :] = jnp.zeros((REACH - 2 * DILATION, width), bf16)
    last[...] = jnp.zeros_like(last)


def end_shifted(pair, last, length, blocks, most):
    width = pair.shape[2]
    tail = jnp.concatenate([last[...], jnp.zeros_like(last)]).astype(bf16)
    pair[1, pl.ds(mult(length + REACH - 2 * DILATION, 16), 2 * DILATION), :] = tail

    def clear(i, _):
        for j in (0, 1):
            rows = pl.ds(mult(i * ROWS + REACH, 16), ROWS)
            pair[j, rows, :] = jnp.zeros((ROWS, width), bf16)
        return 0

    lax.fori_loop(blocks, most, clear, 0)
    for j in (0, 1):
        pair[j, most * ROWS + REACH :, :] = jnp.zeros((REACH, width), bf16)


SLOTS = tuple((dc, b, a) for dc in (0, 1) for b, a in ((0, 0), (0, 1), (1, 0), (1, 1)))


def fetch_rows(place, parts, whole, sems):
    seq, own = whole.shape[0], parts[0].shape[1]
    copies = []
    for k, part in enumerate(parts):
        target = whole.at[:, pl.ds(mult((place[1] ^ k) * own, own), own)]
        copies.append(pltpu.make_async_copy(part.at[pl.ds(0, seq), :], target, sems.at[k]))
        copies[-1].start()
    return copies


def fetch_shards(shards, sems):
    copies = []
    for index, shard, whole, d, m in shards:
        di, cols = shard.shape[-2:]
        target = whole.at[
            (slice(None),) * (len(shard.shape) - 2)
            + (pl.ds(mult(d * di, di), di), pl.ds(mult(m * cols, cols), cols))
        ]
        copies.append(pltpu.make_async_copy(shard, target, sems.at[index]))
        copies[-1].start()
    return copies


def conv_forward(place, x0, x1, x2, x3, vec, *rest):
    pieces = rest[:8]
    w_out, x_out, na_out, resid, slope, bias_out, nab, last, whole, extra, sems, x_sem = rest[8:]
    full = vec.shape[1]
    seq, own = x_out.shape[0], x0.shape[1]
    length, blocks = place[2:]

    x_parts = (x0, x1, x2, x3)
    rows = fetch_rows(place, x_parts, x_out, x_sem.at[0])
    shards = fetch_shards(
        [
            ((slot, z), piece.at[z], whole, *source_of(place, *index, z))
            for slot, (index, piece) in enumerate(zip(SLOTS, pieces))
            for z in range(piece.shape[0])
        ],
        sems,
    )
    extras = [
        pltpu.make_async_copy(part.at[pl.ds(seq, extra.shape[1]), :], extra.at[k], x_sem.at[1, k])
        for k, part in enumerate(x_parts)
    ]
    for copy in extras:
        copy.start()
    for copy in rows + extras:
        copy.wait()
    for k in range(len(x_parts)):
        values = extra[k].astype(f32)
        units = values.shape[0] // 4
        bias_out[place[1] ^ k] = (values[0:units] + values[units : 2 * units]) + values[
            2 * units : 3 * units
        ]

    gain = vec[0:1, :]
    shift = vec[1:2, :]
    clear_shifted(nab, last)

    def norm_step(i, _):
        row = mult(i * ROWS, ROWS)
        rows = pl.ds(row, ROWS)
        scaled, _ = norm_parts(x_out[rows, :].astype(f32))
        values = scaled * gain + shift
        put_shifted(nab, last, row, values)
        na_out[rows, :] = values.astype(bf16)
        return 0

    def idle_step(i, _):
        na_out[pl.ds(mult(i * ROWS, ROWS), ROWS), :] = jnp.zeros((ROWS, full), bf16)
        return 0

    lax.fori_loop(0, blocks, norm_step, 0)
    lax.fori_loop(blocks, seq // ROWS, idle_step, 0)
    end_shifted(nab, last, length, blocks, seq // ROWS)
    for copy in shards:
        copy.wait()
    w_copy = pltpu.make_async_copy(whole, w_out, x_sem.at[2, 0])
    w_copy.start()

    def conv_step(i, _):
        row = mult(i * ROWS, ROWS)
        window = jnp.concatenate(
            [
                nab[t & 1, pl.ds(mult(row + DILATION * (t - (t & 1)), 16), ROWS), :]
                for t in range(KERNEL)
            ],
            axis=1,
        )
        weights = whole[...].reshape(KERNEL * full, full)
        rows = pl.ds(row, ROWS)
        conv = dot(window, weights) + vec[2:3, :]
        phi = phi_of(conv)
        resid[rows, :] = x_out[rows, :].astype(f32) + conv * phi
        slope[rows, :] = slope_of(conv, phi)
        return 0

    lax.fori_loop(0, blocks, conv_step, 0)
    w_copy.wait()


def ffn_hidden(place, x_full, resid, c0, c1, c2, c3, vec, hbias, *rest):
    pieces = rest[:8]
    outs, (act, hg, sec, mg, wh_out) = rest[8:12], rest[12:17]
    whole, values_ref, sems, c_sem = rest[17:]
    wh, wo = whole.at[0], whole.at[1]
    seq, full = x_full.shape
    hidden = hbias.shape[1]
    blocks = place[3]

    rows = fetch_rows(place, (c0, c1, c2, c3), mg, c_sem.at[0])
    shards = []
    for slot, piece in enumerate(pieces):
        w, dc, dx = slot >> 2, (slot >> 1) & 1, slot & 1
        for z in range(piece.shape[0]):
            for dy in (0, 1):
                d = ((place[0] >> 1) ^ z) * 2 + ((place[0] & 1) ^ dx)
                m = place[1] ^ (dy * 2 + dc)
                shards.append(((slot, z, dy), piece.at[z, dy], whole.at[w], d, m))
    shards = fetch_shards(shards, sems)
    for copy in rows + shards:
        copy.wait()
    wh_copy = pltpu.make_async_copy(wh, wh_out, c_sem.at[1, 0])
    wh_copy.start()

    def row_step(i, _):
        rows = pl.ds(mult(i * ROWS, ROWS), ROWS)
        residual = resid[rows, :]
        s, _ = norm_parts(residual)
        second = (s * vec[3:4, :] + vec[4:5, :]).astype(bf16)
        sec[rows, :] = second
        grad = mg[rows, :]
        for j in range(hidden // 512):
            cols = slice(j * 512, (j + 1) * 512)
            h = dot(second, wh[:, cols]) + hbias[0:1, cols]
            phi = phi_of(h)
            act[rows, cols] = (h * phi).astype(bf16)
            hidden_grad = (dot(grad, wo[:, cols]) * slope_of(h, phi)).astype(bf16)
            hg[rows, cols] = hidden_grad
        mixed = dot(act[rows, :], wo[...], NT)
        values_ref[...] = (residual + (mixed + vec[5:6, :])).astype(bf16)
        store_columns(place, outs, rows, values_ref)
        return 0

    def idle_step(i, _):
        rows = pl.ds(mult(i * ROWS, ROWS), ROWS)
        values_ref[...] = x_full[rows, :]
        store_columns(place, outs, rows, values_ref)
        sec[rows, :] = jnp.zeros((ROWS, full), bf16)
        for ref in (act, hg):
            ref[rows, :] = jnp.zeros((ROWS, hidden), bf16)
        return 0

    lax.fori_loop(0, blocks, row_step, 0)
    lax.fori_loop(blocks, seq // ROWS, idle_step, 0)
    wh_copy.wait()


def norm_backward(place, resid, slope, grad, hg, wh, vec, resid_out, cab, vgrad, last):
    seq = resid.shape[0]
    length, blocks = place[2:]
    vgrad[...] = jnp.zeros_like(vgrad)
    clear_shifted(cab, last)

    def row_step(i, _):
        row = mult(i * ROWS, ROWS)
        rows = pl.ds(row, ROWS)
        second_grad = dot(hg[rows, :], wh[...], NT)
        s, inverse = norm_parts(resid[rows, :])
        up = grad[rows, :].astype(f32)
        vgrad[3:4, :] += jnp.sum(second_grad * s, axis=0, keepdims=True)
        vgrad[4:5, :] += jnp.sum(second_grad, axis=0, keepdims=True)
        vgrad[5:6, :] += jnp.sum(up, axis=0, keepdims=True)
        resid_grad = up + norm_back(second_grad * vec[3:4, :], s, inverse)
        resid_out[rows, :] = resid_grad
        rounded = (resid_grad * slope[rows, :]).astype(bf16).astype(f32)
        put_shifted(cab, last, row, rounded)
        vgrad[2:3, :] += jnp.sum(rounded, axis=0, keepdims=True)
        return 0

    def idle_step(i, _):
        rows = pl.ds(mult(i * ROWS, ROWS), ROWS)
        resid_out[rows, :] = grad[rows, :].astype(f32)
        return 0

    lax.fori_loop(0, blocks, row_step, 0)
    lax.fori_loop(blocks, seq // ROWS, idle_step, 0)

    end_shifted(cab, last, length, blocks, seq // ROWS)


def ffn_weight_grad(place, sec, hg, mg, act, keep, give, hbgrad):
    seq, full = sec.shape
    di, part = keep.shape[4:]
    sec_t = jnp.concatenate([sec[...].T, jnp.ones((16, seq), bf16)])
    mg_t = mg[...].T
    for half, ref in enumerate((keep, give)):
        parity = (place[1] & 1) ^ half
        for j in range(keep.shape[1]):
            cols = pl.ds(mult((parity + 2 * j) * part, part), part)
            for w, (left, right) in enumerate(((sec_t, hg), (mg_t, act))):
                value = dot(left, right[:, cols])
                if w == 0:
                    hbgrad[0:1, cols] = value[full : full + 1, :]
                value = value.astype(bf16)
                for d in range(full // di):
                    index = share_index(place, d, parity, j)
                    ref[(*index, w)] = value[d * di : (d + 1) * di, :]


def shifted_rows(cab, u, row, count):
    odd = u & 1
    return cab[odd, pl.ds(mult(row + (u - odd) * DILATION, 16), count), :]


def conv_weight_grad(place, na, cab, keep, *gives):
    seq, full = na.shape
    taps, di, own = keep.shape[3:]
    na_t = na[...].T
    for t in range(taps):
        u = KERNEL - 1 - t
        odd = u & 1
        rows = pl.ds((u - odd) * DILATION, seq)
        group, local = divmod(t, gives[0].shape[3])
        for half, (ref, tap) in enumerate(((keep, t), (gives[group], local))):
            parity = (place[1] & 1) ^ half
            blocks = range(keep.shape[1])
            cols = [pl.ds(mult((parity + 2 * j) * own, own), own) for j in blocks]
            right = jnp.concatenate([cab[odd, rows, c] for c in cols], axis=1)
            value = dot(na_t, right).astype(bf16)
            for j in blocks:
                for d in range(full // di):
                    index = share_index(place, d, parity, j)
                    ref[(*index, tap)] = value[d * di : (d + 1) * di, j * own : (j + 1) * own]


def pair_sum(place, keep, r0, r1, r2, onward, own):
    count = r0.shape[3]
    for group, received in enumerate((r0, r1, r2)):
        taps = pl.ds(group * count, count)
        for a in range(keep.shape[1]):
            both = keep[1, a, :, taps].astype(f32) + received[1, a].astype(f32)
            onward[a, :, taps] = both.astype(bf16)
            own[a, :, taps] = keep[0, a, :, taps].astype(f32) + received[0, a].astype(f32)


def conv_backward(place, x_full, cab, resid, w, vec, *rest):
    outs, (vgrad, values_ref) = rest[:4], rest[4:]
    seq, full = x_full.shape
    blocks = place[3]
    vgrad[...] = jnp.zeros_like(vgrad)

    def in_store(rows, values):
        values_ref[...] = values.astype(bf16)
        store_columns(place, outs, rows, values_ref)

    def row_step(i, _):
        row = mult(i * ROWS, ROWS)
        rows = pl.ds(row, ROWS)
        total = jnp.zeros((ROWS, full), f32)
        for t in range(KERNEL):
            shifted = shifted_rows(cab, KERNEL - 1 - t, row, ROWS)
            total = total + dot(shifted, w[t], NT)
        s, inverse = norm_parts(x_full[rows, :].astype(f32))
        vgrad[0:1, :] += jnp.sum(total * s, axis=0, keepdims=True)
        vgrad[1:2, :] += jnp.sum(total, axis=0, keepdims=True)
        in_store(rows, resid[rows, :] + norm_back(total * vec[0:1, :], s, inverse))
        return 0

    def idle_step(i, _):
        rows = pl.ds(mult(i * ROWS, ROWS), ROWS)
        in_store(rows, resid[rows, :])
        return 0

    lax.fori_loop(0, blocks, row_step, 0)
    lax.fori_loop(blocks, seq // ROWS, idle_step, 0)


def tie(*values):
    return lax.optimization_barrier(values)


def placed(kernel):
    def run(lengths, *refs):
        mp = lax.axis_index("mp")
        length = lengths[mp]
        kernel((lax.axis_index("dp"), mp, length, length // ROWS), *refs)

    return run


def call(kernel, lengths, args, outs, scratch, flops, mib, far=(), far_out=()):
    near = pl.BlockSpec(memory_space=pltpu.VMEM)
    left = pl.BlockSpec(memory_space=pltpu.HBM)
    moved = sum(a.size * a.dtype.itemsize for a in (*args, *outs))
    return pl.pallas_call(
        placed(kernel),
        out_shape=outs,
        in_specs=[pl.BlockSpec(memory_space=pltpu.SMEM)]
        + [left if i in far else near for i in range(len(args))],
        out_specs=[left if i in far_out else near for i in range(len(outs))],
        scratch_shapes=scratch,
        compiler_params=pltpu.CompilerParams(vmem_limit_bytes=mib * 2**20),
        cost_estimate=pl.CostEstimate(flops=flops, bytes_accessed=moved, transcendentals=0),
    )(lengths, *args)


def total_share(place, conv_own, c1, c2, c3, ffn_share, v1, v2, bias_grad, conv_share, small):
    full = small.shape[1]
    total = conv_own[...]
    for part in (c1, c2, c3):
        total = total + part[...].astype(f32)
    conv_share[...] = total
    squares = jnp.sum(total * total) + jnp.sum(ffn_share[...] * ffn_share[...])
    small[0:6, :] = (v1[...] + v2[...])[0:6, :]
    units = bias_grad.shape[1] // full
    for row in range(units):
        small[6 + row : 7 + row, :] = bias_grad[:, row * full : (row + 1) * full]
    small[6 + units :, :] = jnp.full((small.shape[0] - 6 - units, full), squares, f32)


def adam(weight, first_mom, second, gradient, clip_scale, step_rate, decay_rate):
    clipped = gradient * clip_scale
    first_new = BETA_ONE * first_mom + (1.0 - BETA_ONE) * clipped
    second_new = BETA_TWO * second + (1.0 - BETA_TWO) * clipped * clipped
    update_dir = (
        first_new
        / (1.0 - BETA_ONE**STEP)
        / (jnp.sqrt(second_new / (1.0 - BETA_TWO**STEP)) + ADAM_EPS)
    )
    return (weight - step_rate * (update_dir + decay_rate * weight), first_new, second_new)


def update(place, small, small_far, conv_share, ffn_share, *rest):
    states, outs, total = rest[:15], rest[15:31], rest[31]
    total[...] = small[...] + small_far[...]
    rows = total.shape[0] - 1
    own_rows = total[0:rows, :]
    squares = jnp.sum(own_rows * own_rows, axis=(0, 1), keepdims=True) + total[rows:, 0:1]
    norm = jnp.sqrt(squares)
    outs[15][...] = jnp.broadcast_to(norm, outs[15].shape)
    clip_scale = jnp.minimum(1.0, CLIP_NORM / (norm + 1e-06))
    gradients = [
        conv_share[...],
        ffn_share[0],
        ffn_share[1],
        total[0:6, :],
        total[pl.ds(6 + place[1], 1), :],
    ]
    for i, gradient in enumerate(gradients):
        rates = (MATRIX_RATE, WEIGHT_DECAY) if i < 3 else (VECTOR_RATE, 0.0)
        scale = clip_scale.reshape((1,) * gradient.ndim)
        state = [ref[...] for ref in states[3 * i : 3 * i + 3]]
        for ref, value in zip(outs[3 * i : 3 * i + 3], adam(*state, gradient, scale, *rates)):
            ref[...] = value


def per_device(
    ndp,
    nmp,
    inputs,
    cotangent,
    lengths,
    conv_master,
    hidden_master,
    output_master,
    conv_first,
    hidden_first,
    output_first,
    conv_second,
    hidden_second,
    output_second,
    vectors,
    vector_first,
    vector_second,
    hidden_bias,
    bias_first,
    bias_second,
):
    axes = ("dp", "mp")
    nz = ndp // 2
    seq, own = inputs.shape[1:]
    full = vectors.shape[1]
    part = hidden_bias.shape[0]
    hidden = part * nmp
    di = full // ndp
    mp = lax.axis_index("mp")

    def perm(move):
        pairs = []
        for i in range(ndp * nmp):
            d, m = divmod(i, nmp)
            z, x, y, c = move(d >> 1, d & 1, m >> 1, m & 1)
            pairs.append((i, (z * 2 + x) * nmp + y * 2 + c))
        return pairs

    across_z = [perm(lambda z, x, y, c, k=k: (z ^ k, x, y, c)) for k in range(nz)]
    step_x = perm(lambda z, x, y, c: (z, x ^ 1, y, c))
    step_y = perm(lambda z, x, y, c: (z, x, y ^ 1, c))
    step_c = perm(lambda z, x, y, c: (z, x, y, c ^ 1))
    step_xy = perm(lambda z, x, y, c: (z, x ^ 1, y, c) if c == 0 else (z, x, y ^ 1, c))
    step_yx = perm(lambda z, x, y, c: (z, x, y ^ 1, c) if c == 0 else (z, x ^ 1, y, c))
    within = [[(i, i ^ k) for i in range(nmp)] for k in range(nmp)]

    def send(values, pairs):
        return lax.ppermute(values, axes, pairs)

    def gather_z(shard):
        return [shard] + [send(shard, across_z[k]) for k in range(1, nz)]

    def add(*terms):
        total = terms[0].astype(f32)
        for term in terms[1:]:
            total = total + term.astype(f32)
        return total

    def scatter_b(k, r):
        return add(k[1], r[1]).astype(bf16)

    def scatter_a(k, r, rb):
        return add(k[0, 1], r[0, 1], rb[1]).astype(bf16)

    def scatter_z(*terms):
        own_part = add(*(t[0] for t in terms))
        parts = [add(*(t[j] for t in terms)).astype(bf16) for j in range(1, nz)]
        return own_part, [send(part_of, across_z[j + 1]) for j, part_of in enumerate(parts)]

    def take_windows(values, extra=None):
        blocks = [lax.dynamic_index_in_dim(values, mp ^ k, 0, False) for k in range(nmp)]
        if extra is not None:
            blocks = [jnp.concatenate([block, extra]) for block in blocks]
        return blocks

    def swap(blocks):
        return [blocks[0]] + [lax.ppermute(blocks[k], "mp", within[k]) for k in range(1, nmp)]

    def in_order(pieces):
        for bit in range(nmp.bit_length() - 1):
            odd = ((mp >> bit) & 1) == 1
            pieces = [jnp.where(odd, pieces[k ^ (1 << bit)], pieces[k]) for k in range(nmp)]
        return jnp.stack(pieces)

    def all_sum(values):
        values = values + send(values, step_c)
        step = 1
        while step < nz:
            values = values + send(values, across_z[step])
            step *= 2
        values = values + send(values, step_x)
        return values, send(values, step_y)

    exact, rest = [], hidden_bias
    for _ in range(3):
        exact.append(lax.reduce_precision(rest, 8, 7))
        rest = rest - exact[-1]
    exact.append(jnp.zeros_like(rest))
    exact = jnp.concatenate(exact).reshape(4 * part // own, own).astype(bf16)
    ffn_shard = jnp.stack([hidden_master.astype(bf16), output_master.astype(bf16).T])

    x_blocks = take_windows(inputs, exact)
    *x_blocks, conv_shard = tie(*x_blocks, conv_master.astype(bf16))
    x_parts = swap(x_blocks)
    conv_z = gather_z(conv_shard)
    ffn_y = send(ffn_shard, step_y)
    *tied, ffn_shard, ffn_y = tie(*x_parts, *conv_z, ffn_shard, ffn_y)
    x_parts, conv_z = tied[:nmp], jnp.stack(tied[nmp:])
    first, last = [jnp.stack([ffn_shard[w], ffn_y[w]]) for w in (0, 1)]
    conv_a, conv_b = send(conv_z, step_xy), send(conv_z, step_yx)
    first = gather_z(first)
    conv_z, conv_a, conv_b, last, *first = tie(conv_z, conv_a, conv_b, last, *first)
    conv_ab = send(conv_a, step_yx)
    first = jnp.stack(first)
    first_x = send(first, step_x)
    last = gather_z(last)
    conv_z, conv_a, conv_b, conv_ab, cotangent, first, first_x, *last = tie(
        conv_z, conv_a, conv_b, conv_ab, cotangent, first, first_x, *last
    )
    conv_parts = [conv_z, conv_a, conv_b, conv_ab]
    conv_parts += [send(part_of, step_c) for part_of in conv_parts]
    last = jnp.stack(last)
    last_x = send(last, step_x)
    c_blocks = take_windows(cotangent)
    c_parts = [lax.ppermute(c_blocks[k], "mp", within[k]) for k in range(2, nmp)]

    S = jax.ShapeDtypeStruct
    padded = seq + 2 * REACH
    last, *x_parts = tie(last, *x_parts)
    first_c, last_c = send(first, step_c), send(last, step_c)
    w_full, x_full, normed, residual, slope, bias_all = call(
        conv_forward,
        lengths,
        (*x_parts, vectors, *conv_parts),
        (
            S((KERNEL, full, full), bf16),
            S((seq, full), bf16),
            S((seq, full), bf16),
            *(S((seq, full), f32),) * 2,
            S((nmp, part // own, own), f32),
        ),
        [
            pltpu.VMEM((2, padded, full), bf16),
            pltpu.VMEM((DILATION, full), f32),
            pltpu.VMEM((KERNEL, full, full), bf16),
            pltpu.VMEM((nmp, 4 * part // own, own), bf16),
            pltpu.SemaphoreType.DMA((8, nz)),
            pltpu.SemaphoreType.DMA((3, nmp)),
        ],
        2 * seq * KERNEL * full * full,
        24,
        (0, 1, 2, 3, *range(5, 13)),
        (0,),
    )
    *tied, residual = tie(first, first_x, first_c, last, last_x, last_c, *c_blocks[:2], *c_parts, residual)
    first, first_x, first_c, last, last_x, last_c, *c_parts = tied
    c_parts[1] = lax.ppermute(c_parts[1], "mp", within[1])
    ffn_parts = [first, first_x, first_c, send(first_x, step_c)]
    ffn_parts += [last, last_x, last_c, send(last_x, step_c)]
    *block_parts, active, hidden_grad, second, mix_grad, hidden_full = call(
        ffn_hidden,
        lengths,
        (x_full, residual, *c_parts, vectors, bias_all.reshape(1, hidden), *ffn_parts),
        (
            *(S((seq, own), bf16),) * nmp,
            *(S((seq, hidden), bf16),) * 2,
            *(S((seq, full), bf16),) * 2,
            S((full, hidden), bf16),
        ),
        [
            pltpu.VMEM((2, full, hidden), bf16),
            pltpu.VMEM((ROWS, full), bf16),
            pltpu.SemaphoreType.DMA((8, nz, 2)),
            pltpu.SemaphoreType.DMA((2, nmp)),
        ],
        6 * seq * hidden * full,
        20,
        (2, 3, 4, 5, *range(8, 16)),
        (8,),
    )
    for k in (1, 2):
        block_parts[k] = lax.ppermute(block_parts[k], "mp", within[k])
    ffn_keep, ffn_give, bias_grad = call(
        ffn_weight_grad,
        lengths,
        (second, hidden_grad, mix_grad, active),
        (*(S((2, 2, nz, 2, di, part), bf16),) * 2, S((1, hidden), f32)),
        [],
        1,
        12,
    )
    ffn_give, ffn_keep, hidden_grad, *block_parts[1:] = tie(
        ffn_give, ffn_keep, hidden_grad, *block_parts[1:]
    )
    ffn_r = send(ffn_give, step_c)
    block_parts[3] = lax.ppermute(block_parts[3], "mp", within[3])
    resid_grad, conv_grad, vgrad_two = call(
        norm_backward,
        lengths,
        (residual, slope, mix_grad, hidden_grad, hidden_full, vectors),
        (S((seq, full), f32), S((2, padded, full), bf16), S((8, full), f32)),
        [pltpu.VMEM((DILATION, full), f32)],
        1,
        16,
    )
    ffn_sum, conv_grad, block_parts[3] = tie(scatter_b(ffn_keep, ffn_r), conv_grad, block_parts[3])
    ffn_rb = send(ffn_sum, step_yx)
    conv_keep, *conv_give = call(
        conv_weight_grad,
        lengths,
        (normed, conv_grad),
        (S((2, 2, nz, KERNEL, di, own), bf16), *(S((2, 2, nz, KERNEL // 3, di, own), bf16),) * 3),
        [],
        1,
        16,
    )
    *conv_give, conv_keep, conv_grad = tie(*conv_give, conv_keep, conv_grad)
    conv_r = [send(give, step_c) for give in conv_give]
    *in_parts, vgrad_one = call(
        conv_backward,
        lengths,
        (x_full, conv_grad, resid_grad, w_full, vectors),
        (*(S((seq, own), bf16),) * nmp, S((8, full), f32)),
        [pltpu.VMEM((ROWS, full), bf16)],
        1,
        16,
    )
    ffn_sum = scatter_a(ffn_keep, ffn_r, ffn_rb)
    *conv_r, ffn_sum, in_parts[1] = tie(*conv_r, ffn_sum, in_parts[1])
    conv_sum, conv_own = call(
        pair_sum,
        lengths,
        (conv_keep, *conv_r),
        (S((2, nz, KERNEL, di, own), bf16), S((2, nz, KERNEL, di, own), f32)),
        [],
        1,
        16,
    )
    conv_rb = send(conv_sum, step_yx)
    ffn_ra = send(ffn_sum, step_xy)
    ffn_own, ffn_rest = scatter_z(ffn_keep[0, 0], ffn_r[0, 0], ffn_rb[0], ffn_ra)
    ffn_share = add(ffn_own, *ffn_rest)
    conv_ra = send(add(conv_own[1], conv_rb[1]).astype(bf16), step_xy)
    conv_ra, *in_parts[2:] = tie(conv_ra, *in_parts[2:])
    conv_own, conv_rest = scatter_z(conv_own[0], conv_rb[0], conv_ra)
    for part_of in conv_rest[3:]:
        conv_own = conv_own + part_of.astype(f32)
    for k in range(1, nmp):
        in_parts[k] = lax.ppermute(in_parts[k], "mp", within[k])
    conv_own, *tied = tie(conv_own, *conv_rest[:3], *in_parts)
    conv_rest, in_parts = tied[:3], tied[3:]
    block_output = in_order(block_parts)
    input_grad = in_order(in_parts).astype(f32)

    conv_share, small = call(
        total_share,
        lengths,
        (conv_own, *conv_rest, ffn_share, vgrad_one, vgrad_two, bias_grad),
        (S((KERNEL, di, own), f32), S((7 + hidden // full, full), f32)),
        [],
        1,
        16,
    )
    small, small_far = all_sum(small)
    matrices = (
        *(conv_master, conv_first, conv_second),
        *(hidden_master, hidden_first, hidden_second),
        *(output_master.T, output_first.T, output_second.T),
    )
    vector_ones = (vectors, vector_first, vector_second)
    bias_ones = [v.reshape(1, part) for v in (hidden_bias, bias_first, bias_second)]
    states = (*matrices, *vector_ones, *bias_ones)
    *updated, norm = call(
        update,
        lengths,
        (small, small_far, conv_share, ffn_share, *states),
        (*(S(v.shape, f32) for v in states), S((1, 1), f32)),
        [pltpu.VMEM(small.shape, f32)],
        1,
        16,
    )
    updated[6:9] = [v.T for v in updated[6:9]]
    updated[12:] = [v.reshape(part) for v in updated[12:]]
    return (block_output, input_grad, norm.reshape(()), *updated)


def solution(mesh):
    rows = P("dp", None, "mp")
    conv = P(None, "dp", "mp")
    hid = P("dp", "mp")
    out = P("mp", "dp")
    return jax.shard_map(
        functools.partial(per_device, mesh.shape["dp"], mesh.shape["mp"]),
        mesh=mesh,
        in_specs=(rows, rows, P("dp"), *(conv, hid, out) * 3, *(P(),) * 3, *(P("mp"),) * 3),
        out_specs=(
            rows,
            rows,
            P(),
            *(conv,) * 3,
            *(hid,) * 3,
            *(out,) * 3,
            *(P(),) * 3,
            *(P("mp"),) * 3,
        ),
        check_vma=False,
    )
```

```python
import functools

import jax
import jax.numpy as jnp
from jax import lax
from jax.experimental import pallas as pl
from jax.experimental.pallas import tpu as pltpu
from jax.sharding import PartitionSpec as P

KERNEL = 9
DILATION = 8
REACH = DILATION * (KERNEL // 2)
STEP = 10
ROWS = 256

NORM_EPS = 1e-05
BETA_ONE = 0.9
BETA_TWO = 0.999
ADAM_EPS = 1e-08
MATRIX_RATE = 0.03
VECTOR_RATE = 0.3
WEIGHT_DECAY = 0.01
CLIP_NORM = 1.0

f32 = jnp.float32
bf16 = jnp.bfloat16
NN = (((1,), (0,)), ((), ()))
NT = (((1,), (1,)), ((), ()))


def dot(a, b, dims=NN):
    return lax.dot_general(a, b, dims, preferred_element_type=f32)


def phi_of(v):
    return 0.5 * (1.0 + lax.erf(v * 0.7071067811865476))


def slope_of(v, phi):
    return phi + v * jnp.exp(-0.5 * v * v) * 0.3989422804014327


def norm_parts(v):
    centre = v - jnp.mean(v, axis=-1, keepdims=True)
    inverse = lax.rsqrt(jnp.mean(centre * centre, axis=-1, keepdims=True) + NORM_EPS)
    return centre * inverse, inverse


def norm_back(e, s, inverse):
    return inverse * (
        e - jnp.mean(e, axis=-1, keepdims=True) - s * jnp.mean(e * s, axis=-1, keepdims=True)
    )


def source_of(place, dc, b, a, dz):
    dp, mp = place[0], place[1]
    flip = (mp & 1) ^ dc
    fx = jnp.where(flip == 0, a, b)
    fy = jnp.where(flip == 0, b, a)
    d = ((dp >> 1) ^ dz) * 2 + ((dp & 1) ^ fx)
    m = ((mp >> 1) ^ fy) * 2 + ((mp & 1) ^ dc)
    return d, m


def share_index(place, d, parity, j):
    dp, mp = place[0], place[1]
    fx = (dp & 1) ^ (d & 1)
    fy = (mp >> 1) ^ j
    odd = parity == 1
    return jnp.where(odd, fx, fy), jnp.where(odd, fy, fx), (dp >> 1) ^ (d >> 1)


def store_columns(place, outs, rows, values):
    for k, out in enumerate(outs):
        own = out.shape[1]
        out[rows, :] = values[:, pl.ds(mult((place[1] ^ k) * own, own), own)]


def mult(v, n):
    return v if isinstance(v, int) else pl.multiple_of(v, n)


def put_shifted(pair, last, row, values):
    count = values.shape[0]
    pair[0, pl.ds(mult(row + REACH, 16), count), :] = values.astype(bf16)
    moved = jnp.concatenate([last[...], values[: count - DILATION]])
    pair[1, pl.ds(mult(row + REACH - 2 * DILATION, 16), count), :] = moved.astype(bf16)
    last[...] = values[count - DILATION :]


def clear_shifted(pair, last):
    width = pair.shape[2]
    pair[0, 0:REACH, :] = jnp.zeros((REACH, width), bf16)
    pair[1, 0 : REACH - 2 * DILATION, :] = jnp.zeros((REACH - 2 * DILATION, width), bf16)
    last[...] = jnp.zeros_like(last)


def end_shifted(pair, last, length, blocks, most):
    width = pair.shape[2]
    tail = jnp.concatenate([last[...], jnp.zeros_like(last)]).astype(bf16)
    pair[1, pl.ds(mult(length + REACH - 2 * DILATION, 16), 2 * DILATION), :] = tail

    def clear(i, _):
        for j in (0, 1):
            rows = pl.ds(mult(i * ROWS + REACH, 16), ROWS)
            pair[j, rows, :] = jnp.zeros((ROWS, width), bf16)
        return 0

    lax.fori_loop(blocks, most, clear, 0)
    for j in (0, 1):
        pair[j, most * ROWS + REACH :, :] = jnp.zeros((REACH, width), bf16)


SLOTS = tuple((dc, b, a) for dc in (0, 1) for b, a in ((0, 0), (0, 1), (1, 0), (1, 1)))


def fetch_rows(place, parts, whole, sems):
    seq, own = whole.shape[0], parts[0].shape[1]
    copies = []
    for k, part in enumerate(parts):
        target = whole.at[:, pl.ds(mult((place[1] ^ k) * own, own), own)]
        copies.append(pltpu.make_async_copy(part.at[pl.ds(0, seq), :], target, sems.at[k]))
        copies[-1].start()
    return copies


def fetch_shards(shards, sems):
    copies = []
    for index, shard, whole, d, m in shards:
        di, cols = shard.shape[-2:]
        target = whole.at[
            (slice(None),) * (len(shard.shape) - 2)
            + (pl.ds(mult(d * di, di), di), pl.ds(mult(m * cols, cols), cols))
        ]
        copies.append(pltpu.make_async_copy(shard, target, sems.at[index]))
        copies[-1].start()
    return copies


def conv_forward(place, x0, x1, x2, x3, vec, *rest):
    pieces = rest[:8]
    w_out, x_out, na_out, resid, slope, bias_out, nab, last, whole, extra, sems, x_sem = rest[8:]
    full = vec.shape[1]
    seq, own = x_out.shape[0], x0.shape[1]
    length, blocks = place[2:]

    x_parts = (x0, x1, x2, x3)
    rows = fetch_rows(place, x_parts, x_out, x_sem.at[0])
    shards = fetch_shards(
        [
            ((slot, z), piece.at[z], whole, *source_of(place, *index, z))
            for slot, (index, piece) in enumerate(zip(SLOTS, pieces))
            for z in range(piece.shape[0])
        ],
        sems,
    )
    extras = [
        pltpu.make_async_copy(part.at[pl.ds(seq, extra.shape[1]), :], extra.at[k], x_sem.at[1, k])
        for k, part in enumerate(x_parts)
    ]
    for copy in extras:
        copy.start()
    for copy in rows + extras:
        copy.wait()
    for k in range(len(x_parts)):
        values = extra[k].astype(f32)
        units = values.shape[0] // 4
        bias_out[place[1] ^ k] = (values[0:units] + values[units : 2 * units]) + values[
            2 * units : 3 * units
        ]

    gain = vec[0:1, :]
    shift = vec[1:2, :]
    clear_shifted(nab, last)

    def norm_step(i, _):
        row = mult(i * ROWS, ROWS)
        rows = pl.ds(row, ROWS)
        scaled, _ = norm_parts(x_out[rows, :].astype(f32))
        values = scaled * gain + shift
        put_shifted(nab, last, row, values)
        na_out[rows, :] = values.astype(bf16)
        return 0

    def idle_step(i, _):
        na_out[pl.ds(mult(i * ROWS, ROWS), ROWS), :] = jnp.zeros((ROWS, full), bf16)
        return 0

    lax.fori_loop(0, blocks, norm_step, 0)
    lax.fori_loop(blocks, seq // ROWS, idle_step, 0)
    end_shifted(nab, last, length, blocks, seq // ROWS)
    for copy in shards:
        copy.wait()
    w_copy = pltpu.make_async_copy(whole, w_out, x_sem.at[2, 0])
    w_copy.start()

    def conv_step(i, _):
        row = mult(i * ROWS, ROWS)
        window = jnp.concatenate(
            [
                nab[t & 1, pl.ds(mult(row + DILATION * (t - (t & 1)), 16), ROWS), :]
                for t in range(KERNEL)
            ],
            axis=1,
        )
        weights = whole[...].reshape(KERNEL * full, full)
        rows = pl.ds(row, ROWS)
        conv = dot(window, weights) + vec[2:3, :]
        phi = phi_of(conv)
        resid[rows, :] = x_out[rows, :].astype(f32) + conv * phi
        slope[rows, :] = slope_of(conv, phi)
        return 0

    lax.fori_loop(0, blocks, conv_step, 0)
    w_copy.wait()


def ffn_hidden(place, x_full, resid, c0, c1, c2, c3, vec, hbias, *rest):
    pieces = rest[:8]
    outs, (act, hg, sec, mg, wh_out) = rest[8:12], rest[12:17]
    whole, values_ref, sems, c_sem = rest[17:]
    wh, wo = whole.at[0], whole.at[1]
    seq, full = x_full.shape
    hidden = hbias.shape[1]
    blocks = place[3]

    rows = fetch_rows(place, (c0, c1, c2, c3), mg, c_sem.at[0])
    shards = []
    for slot, piece in enumerate(pieces):
        w, dc, dx = slot >> 2, (slot >> 1) & 1, slot & 1
        for z in range(piece.shape[0]):
            for dy in (0, 1):
                d = ((place[0] >> 1) ^ z) * 2 + ((place[0] & 1) ^ dx)
                m = place[1] ^ (dy * 2 + dc)
                shards.append(((slot, z, dy), piece.at[z, dy], whole.at[w], d, m))
    shards = fetch_shards(shards, sems)
    for copy in rows + shards:
        copy.wait()
    wh_copy = pltpu.make_async_copy(wh, wh_out, c_sem.at[1, 0])
    wh_copy.start()

    def row_step(i, _):
        rows = pl.ds(mult(i * ROWS, ROWS), ROWS)
        residual = resid[rows, :]
        s, _ = norm_parts(residual)
        second = (s * vec[3:4, :] + vec[4:5, :]).astype(bf16)
        sec[rows, :] = second
        grad = mg[rows, :]
        for j in range(hidden // ROWS):
            cols = slice(j * ROWS, (j + 1) * ROWS)
            back = dot(grad, wo[:, cols])
            h = dot(second, wh[:, cols]) + hbias[0:1, cols]
            phi = phi_of(h)
            act[rows, cols] = (h * phi).astype(bf16)
            hg[rows, cols] = (back * slope_of(h, phi)).astype(bf16)
        mixed = dot(act[rows, :], wo[...], NT)
        values_ref[...] = (residual + (mixed + vec[5:6, :])).astype(bf16)
        store_columns(place, outs, rows, values_ref)
        return 0

    def idle_step(i, _):
        rows = pl.ds(mult(i * ROWS, ROWS), ROWS)
        values_ref[...] = x_full[rows, :]
        store_columns(place, outs, rows, values_ref)
        sec[rows, :] = jnp.zeros((ROWS, full), bf16)
        for ref in (act, hg):
            ref[rows, :] = jnp.zeros((ROWS, hidden), bf16)
        return 0

    lax.fori_loop(0, blocks, row_step, 0)
    lax.fori_loop(blocks, seq // ROWS, idle_step, 0)
    wh_copy.wait()


def norm_backward(place, resid, slope, grad, hg, wh, vec, resid_out, cab, vgrad, last):
    seq = resid.shape[0]
    length, blocks = place[2:]
    vgrad[...] = jnp.zeros_like(vgrad)
    clear_shifted(cab, last)

    def row_step(i, _):
        row = mult(i * ROWS, ROWS)
        rows = pl.ds(row, ROWS)
        second_grad = dot(hg[rows, :], wh[...], NT)
        s, inverse = norm_parts(resid[rows, :])
        up = grad[rows, :].astype(f32)
        vgrad[3:4, :] += jnp.sum(second_grad * s, axis=0, keepdims=True)
        vgrad[4:5, :] += jnp.sum(second_grad, axis=0, keepdims=True)
        vgrad[5:6, :] += jnp.sum(up, axis=0, keepdims=True)
        resid_grad = up + norm_back(second_grad * vec[3:4, :], s, inverse)
        resid_out[rows, :] = resid_grad
        rounded = (resid_grad * slope[rows, :]).astype(bf16).astype(f32)
        put_shifted(cab, last, row, rounded)
        vgrad[2:3, :] += jnp.sum(rounded, axis=0, keepdims=True)
        return 0

    def idle_step(i, _):
        rows = pl.ds(mult(i * ROWS, ROWS), ROWS)
        resid_out[rows, :] = grad[rows, :].astype(f32)
        return 0

    lax.fori_loop(0, blocks, row_step, 0)
    lax.fori_loop(blocks, seq // ROWS, idle_step, 0)

    end_shifted(cab, last, length, blocks, seq // ROWS)


def ffn_weight_grad(place, sec, hg, mg, act, keep, give, hbgrad):
    seq, full = sec.shape
    di, part = keep.shape[4:]
    sec_t = jnp.concatenate([sec[...].T, jnp.ones((16, seq), bf16)])
    mg_t = mg[...].T
    for half, ref in enumerate((keep, give)):
        parity = (place[1] & 1) ^ half
        for j in range(keep.shape[1]):
            cols = pl.ds(mult((parity + 2 * j) * part, part), part)
            for w, (left, right) in enumerate(((sec_t, hg), (mg_t, act))):
                value = dot(left, right[:, cols])
                if w == 0:
                    hbgrad[0:1, cols] = value[full : full + 1, :]
                value = value.astype(bf16)
                for d in range(full // di):
                    index = share_index(place, d, parity, j)
                    ref[(*index, w)] = value[d * di : (d + 1) * di, :]


def shifted_rows(cab, u, row, count):
    odd = u & 1
    return cab[odd, pl.ds(mult(row + (u - odd) * DILATION, 16), count), :]


def conv_weight_grad(place, na, cab, keep, *gives):
    seq, full = na.shape
    taps, di, own = keep.shape[3:]
    na_t = na[...].T
    for t in range(taps):
        u = KERNEL - 1 - t
        odd = u & 1
        rows = pl.ds((u - odd) * DILATION, seq)
        group, local = divmod(t, gives[0].shape[3])
        for half, (ref, tap) in enumerate(((keep, t), (gives[group], local))):
            parity = (place[1] & 1) ^ half
            blocks = range(keep.shape[1])
            cols = [pl.ds(mult((parity + 2 * j) * own, own), own) for j in blocks]
            right = jnp.concatenate([cab[odd, rows, c] for c in cols], axis=1)
            value = dot(na_t, right).astype(bf16)
            for j in blocks:
                for d in range(full // di):
                    index = share_index(place, d, parity, j)
                    ref[(*index, tap)] = value[d * di : (d + 1) * di, j * own : (j + 1) * own]


def pair_sum(place, keep, r0, r1, r2, onward, own):
    count = r0.shape[3]
    for group, received in enumerate((r0, r1, r2)):
        taps = pl.ds(group * count, count)
        for a in range(keep.shape[1]):
            both = keep[1, a, :, taps].astype(f32) + received[1, a].astype(f32)
            onward[a, :, taps] = both.astype(bf16)
            own[a, :, taps] = keep[0, a, :, taps].astype(f32) + received[0, a].astype(f32)


def conv_backward(place, x_full, cab, resid, w, vec, *rest):
    outs, (vgrad, values_ref) = rest[:4], rest[4:]
    seq, full = x_full.shape
    blocks = place[3]
    vgrad[...] = jnp.zeros_like(vgrad)

    def in_store(rows, values):
        values_ref[...] = values.astype(bf16)
        store_columns(place, outs, rows, values_ref)

    def row_step(i, _):
        row = mult(i * ROWS, ROWS)
        rows = pl.ds(row, ROWS)
        total = jnp.zeros((ROWS, full), f32)
        for t in range(KERNEL):
            shifted = shifted_rows(cab, KERNEL - 1 - t, row, ROWS)
            total = total + dot(shifted, w[t], NT)
        s, inverse = norm_parts(x_full[rows, :].astype(f32))
        vgrad[0:1, :] += jnp.sum(total * s, axis=0, keepdims=True)
        vgrad[1:2, :] += jnp.sum(total, axis=0, keepdims=True)
        in_store(rows, resid[rows, :] + norm_back(total * vec[0:1, :], s, inverse))
        return 0

    def idle_step(i, _):
        rows = pl.ds(mult(i * ROWS, ROWS), ROWS)
        in_store(rows, resid[rows, :])
        return 0

    lax.fori_loop(0, blocks, row_step, 0)
    lax.fori_loop(blocks, seq // ROWS, idle_step, 0)


def tie(*values):
    return lax.optimization_barrier(values)


def placed(kernel):
    def run(lengths, *refs):
        mp = lax.axis_index("mp")
        length = lengths[mp]
        kernel((lax.axis_index("dp"), mp, length, length // ROWS), *refs)

    return run


def call(kernel, lengths, args, outs, scratch, flops, mib, far=(), far_out=()):
    near = pl.BlockSpec(memory_space=pltpu.VMEM)
    left = pl.BlockSpec(memory_space=pltpu.HBM)
    moved = sum(a.size * a.dtype.itemsize for a in (*args, *outs))
    return pl.pallas_call(
        placed(kernel),
        out_shape=outs,
        in_specs=[pl.BlockSpec(memory_space=pltpu.SMEM)]
        + [left if i in far else near for i in range(len(args))],
        out_specs=[left if i in far_out else near for i in range(len(outs))],
        scratch_shapes=scratch,
        compiler_params=pltpu.CompilerParams(vmem_limit_bytes=mib * 2**20),
        cost_estimate=pl.CostEstimate(flops=flops, bytes_accessed=moved, transcendentals=0),
    )(lengths, *args)


def total_share(place, conv_own, c1, c2, c3, ffn_share, v1, v2, bias_grad, conv_share, small):
    full = small.shape[1]
    total = conv_own[...]
    for part in (c1, c2, c3):
        total = total + part[...].astype(f32)
    conv_share[...] = total
    squares = jnp.sum(total * total) + jnp.sum(ffn_share[...] * ffn_share[...])
    small[0:6, :] = (v1[...] + v2[...])[0:6, :]
    units = bias_grad.shape[1] // full
    for row in range(units):
        small[6 + row : 7 + row, :] = bias_grad[:, row * full : (row + 1) * full]
    small[6 + units :, :] = jnp.full((small.shape[0] - 6 - units, full), squares, f32)


def adam(weight, first_mom, second, gradient, clip_scale, step_rate, decay_rate):
    clipped = gradient * clip_scale
    first_new = BETA_ONE * first_mom + (1.0 - BETA_ONE) * clipped
    second_new = BETA_TWO * second + (1.0 - BETA_TWO) * clipped * clipped
    update_dir = (
        first_new
        / (1.0 - BETA_ONE**STEP)
        / (jnp.sqrt(second_new / (1.0 - BETA_TWO**STEP)) + ADAM_EPS)
    )
    return (weight - step_rate * (update_dir + decay_rate * weight), first_new, second_new)


def update(place, small, small_far, conv_share, ffn_share, *rest):
    states, outs, total = rest[:15], rest[15:31], rest[31]
    total[...] = small[...] + small_far[...]
    rows = total.shape[0] - 1
    own_rows = total[0:rows, :]
    squares = jnp.sum(own_rows * own_rows, axis=(0, 1), keepdims=True) + total[rows:, 0:1]
    norm = jnp.sqrt(squares)
    outs[15][...] = jnp.broadcast_to(norm, outs[15].shape)
    clip_scale = jnp.minimum(1.0, CLIP_NORM / (norm + 1e-06))
    gradients = [
        conv_share[...],
        ffn_share[0],
        ffn_share[1],
        total[0:6, :],
        total[pl.ds(6 + place[1], 1), :],
    ]
    for i, gradient in enumerate(gradients):
        rates = (MATRIX_RATE, WEIGHT_DECAY) if i < 3 else (VECTOR_RATE, 0.0)
        scale = clip_scale.reshape((1,) * gradient.ndim)
        state = [ref[...] for ref in states[3 * i : 3 * i + 3]]
        for ref, value in zip(outs[3 * i : 3 * i + 3], adam(*state, gradient, scale, *rates)):
            ref[...] = value


def per_device(
    ndp,
    nmp,
    inputs,
    cotangent,
    lengths,
    conv_master,
    hidden_master,
    output_master,
    conv_first,
    hidden_first,
    output_first,
    conv_second,
    hidden_second,
    output_second,
    vectors,
    vector_first,
    vector_second,
    hidden_bias,
    bias_first,
    bias_second,
):
    axes = ("dp", "mp")
    nz = ndp // 2
    seq, own = inputs.shape[1:]
    full = vectors.shape[1]
    part = hidden_bias.shape[0]
    hidden = part * nmp
    di = full // ndp
    mp = lax.axis_index("mp")

    def perm(move):
        pairs = []
        for i in range(ndp * nmp):
            d, m = divmod(i, nmp)
            z, x, y, c = move(d >> 1, d & 1, m >> 1, m & 1)
            pairs.append((i, (z * 2 + x) * nmp + y * 2 + c))
        return pairs

    across_z = [perm(lambda z, x, y, c, k=k: (z ^ k, x, y, c)) for k in range(nz)]
    step_x = perm(lambda z, x, y, c: (z, x ^ 1, y, c))
    step_y = perm(lambda z, x, y, c: (z, x, y ^ 1, c))
    step_c = perm(lambda z, x, y, c: (z, x, y, c ^ 1))
    step_xy = perm(lambda z, x, y, c: (z, x ^ 1, y, c) if c == 0 else (z, x, y ^ 1, c))
    step_yx = perm(lambda z, x, y, c: (z, x, y ^ 1, c) if c == 0 else (z, x ^ 1, y, c))
    within = [[(i, i ^ k) for i in range(nmp)] for k in range(nmp)]

    def send(values, pairs):
        return lax.ppermute(values, axes, pairs)

    def gather_z(shard):
        return [shard] + [send(shard, across_z[k]) for k in range(1, nz)]

    def add(*terms):
        total = terms[0].astype(f32)
        for term in terms[1:]:
            total = total + term.astype(f32)
        return total

    def scatter_b(k, r):
        return add(k[1], r[1]).astype(bf16)

    def scatter_a(k, r, rb):
        return add(k[0, 1], r[0, 1], rb[1]).astype(bf16)

    def scatter_z(*terms):
        own_part = add(*(t[0] for t in terms))
        parts = [add(*(t[j] for t in terms)).astype(bf16) for j in range(1, nz)]
        return own_part, [send(part_of, across_z[j + 1]) for j, part_of in enumerate(parts)]

    def take_windows(values, extra=None):
        blocks = [lax.dynamic_index_in_dim(values, mp ^ k, 0, False) for k in range(nmp)]
        if extra is not None:
            blocks = [jnp.concatenate([block, extra]) for block in blocks]
        return blocks

    def swap(blocks):
        return [blocks[0]] + [lax.ppermute(blocks[k], "mp", within[k]) for k in range(1, nmp)]

    def in_order(pieces):
        for bit in range(nmp.bit_length() - 1):
            odd = ((mp >> bit) & 1) == 1
            pieces = [jnp.where(odd, pieces[k ^ (1 << bit)], pieces[k]) for k in range(nmp)]
        return jnp.stack(pieces)

    def all_sum(values):
        values = values + send(values, step_c)
        step = 1
        while step < nz:
            values = values + send(values, across_z[step])
            step *= 2
        values = values + send(values, step_x)
        return values, send(values, step_y)

    exact, rest = [], hidden_bias
    for _ in range(3):
        exact.append(lax.reduce_precision(rest, 8, 7))
        rest = rest - exact[-1]
    exact.append(jnp.zeros_like(rest))
    exact = jnp.concatenate(exact).reshape(4 * part // own, own).astype(bf16)
    ffn_shard = jnp.stack([hidden_master.astype(bf16), output_master.astype(bf16).T])

    x_blocks = take_windows(inputs, exact)
    *x_blocks, conv_shard = tie(*x_blocks, conv_master.astype(bf16))
    x_parts = swap(x_blocks)
    conv_z = gather_z(conv_shard)
    ffn_y = send(ffn_shard, step_y)
    *tied, ffn_shard, ffn_y = tie(*x_parts, *conv_z, ffn_shard, ffn_y)
    x_parts, conv_z = tied[:nmp], jnp.stack(tied[nmp:])
    first, last = [jnp.stack([ffn_shard[w], ffn_y[w]]) for w in (0, 1)]
    conv_a, conv_b = send(conv_z, step_xy), send(conv_z, step_yx)
    first = gather_z(first)
    conv_z, conv_a, conv_b, last, *first = tie(conv_z, conv_a, conv_b, last, *first)
    conv_ab = send(conv_a, step_yx)
    first = jnp.stack(first)
    first_x = send(first, step_x)
    last = gather_z(last)
    conv_z, conv_a, conv_b, conv_ab, cotangent, first, first_x, *last = tie(
        conv_z, conv_a, conv_b, conv_ab, cotangent, first, first_x, *last
    )
    conv_parts = [conv_z, conv_a, conv_b, conv_ab]
    conv_parts += [send(part_of, step_c) for part_of in conv_parts]
    last = jnp.stack(last)
    last_x = send(last, step_x)
    c_blocks = take_windows(cotangent)
    c_parts = [lax.ppermute(c_blocks[k], "mp", within[k]) for k in range(2, nmp)]

    S = jax.ShapeDtypeStruct
    padded = seq + 2 * REACH
    last, *x_parts = tie(last, *x_parts)
    first_c, last_c = send(first, step_c), send(last, step_c)
    w_full, x_full, normed, residual, slope, bias_all = call(
        conv_forward,
        lengths,
        (*x_parts, vectors, *conv_parts),
        (
            S((KERNEL, full, full), bf16),
            S((seq, full), bf16),
            S((seq, full), bf16),
            *(S((seq, full), f32),) * 2,
            S((nmp, part // own, own), f32),
        ),
        [
            pltpu.VMEM((2, padded, full), bf16),
            pltpu.VMEM((DILATION, full), f32),
            pltpu.VMEM((KERNEL, full, full), bf16),
            pltpu.VMEM((nmp, 4 * part // own, own), bf16),
            pltpu.SemaphoreType.DMA((8, nz)),
            pltpu.SemaphoreType.DMA((3, nmp)),
        ],
        2 * seq * KERNEL * full * full,
        24,
        (0, 1, 2, 3, *range(5, 13)),
        (0,),
    )
    *tied, residual = tie(first, first_x, first_c, last, last_x, last_c, *c_blocks[:2], *c_parts, residual)
    first, first_x, first_c, last, last_x, last_c, *c_parts = tied
    c_parts[1] = lax.ppermute(c_parts[1], "mp", within[1])
    ffn_parts = [first, first_x, first_c, send(first_x, step_c)]
    ffn_parts += [last, last_x, last_c, send(last_x, step_c)]
    *block_parts, active, hidden_grad, second, mix_grad, hidden_full = call(
        ffn_hidden,
        lengths,
        (x_full, residual, *c_parts, vectors, bias_all.reshape(1, hidden), *ffn_parts),
        (
            *(S((seq, own), bf16),) * nmp,
            *(S((seq, hidden), bf16),) * 2,
            *(S((seq, full), bf16),) * 2,
            S((full, hidden), bf16),
        ),
        [
            pltpu.VMEM((2, full, hidden), bf16),
            pltpu.VMEM((ROWS, full), bf16),
            pltpu.SemaphoreType.DMA((8, nz, 2)),
            pltpu.SemaphoreType.DMA((2, nmp)),
        ],
        6 * seq * hidden * full,
        20,
        (2, 3, 4, 5, *range(8, 16)),
        (8,),
    )
    for k in (1, 2):
        block_parts[k] = lax.ppermute(block_parts[k], "mp", within[k])
    ffn_keep, ffn_give, bias_grad = call(
        ffn_weight_grad,
        lengths,
        (second, hidden_grad, mix_grad, active),
        (*(S((2, 2, nz, 2, di, part), bf16),) * 2, S((1, hidden), f32)),
        [],
        1,
        12,
    )
    ffn_give, ffn_keep, hidden_grad, *block_parts[1:] = tie(
        ffn_give, ffn_keep, hidden_grad, *block_parts[1:]
    )
    ffn_r = send(ffn_give, step_c)
    block_parts[3] = lax.ppermute(block_parts[3], "mp", within[3])
    resid_grad, conv_grad, vgrad_two = call(
        norm_backward,
        lengths,
        (residual, slope, mix_grad, hidden_grad, hidden_full, vectors),
        (S((seq, full), f32), S((2, padded, full), bf16), S((8, full), f32)),
        [pltpu.VMEM((DILATION, full), f32)],
        1,
        16,
    )
    ffn_sum, conv_grad, block_parts[3] = tie(scatter_b(ffn_keep, ffn_r), conv_grad, block_parts[3])
    ffn_rb = send(ffn_sum, step_yx)
    conv_keep, *conv_give = call(
        conv_weight_grad,
        lengths,
        (normed, conv_grad),
        (S((2, 2, nz, KERNEL, di, own), bf16), *(S((2, 2, nz, KERNEL // 3, di, own), bf16),) * 3),
        [],
        1,
        16,
    )
    *conv_give, conv_keep, conv_grad = tie(*conv_give, conv_keep, conv_grad)
    conv_r = [send(give, step_c) for give in conv_give]
    *in_parts, vgrad_one = call(
        conv_backward,
        lengths,
        (x_full, conv_grad, resid_grad, w_full, vectors),
        (*(S((seq, own), bf16),) * nmp, S((8, full), f32)),
        [pltpu.VMEM((ROWS, full), bf16)],
        1,
        16,
    )
    ffn_sum = scatter_a(ffn_keep, ffn_r, ffn_rb)
    *conv_r, ffn_sum, in_parts[1] = tie(*conv_r, ffn_sum, in_parts[1])
    conv_sum, conv_own = call(
        pair_sum,
        lengths,
        (conv_keep, *conv_r),
        (S((2, nz, KERNEL, di, own), bf16), S((2, nz, KERNEL, di, own), f32)),
        [],
        1,
        16,
    )
    conv_rb = send(conv_sum, step_yx)
    ffn_ra = send(ffn_sum, step_xy)
    ffn_own, ffn_rest = scatter_z(ffn_keep[0, 0], ffn_r[0, 0], ffn_rb[0], ffn_ra)
    ffn_share = add(ffn_own, *ffn_rest)
    conv_ra = send(add(conv_own[1], conv_rb[1]).astype(bf16), step_xy)
    conv_ra, *in_parts[2:] = tie(conv_ra, *in_parts[2:])
    conv_own, conv_rest = scatter_z(conv_own[0], conv_rb[0], conv_ra)
    for part_of in conv_rest[3:]:
        conv_own = conv_own + part_of.astype(f32)
    for k in range(1, nmp):
        in_parts[k] = lax.ppermute(in_parts[k], "mp", within[k])
    conv_own, *tied = tie(conv_own, *conv_rest[:3], *in_parts)
    conv_rest, in_parts = tied[:3], tied[3:]
    block_output = in_order(block_parts)
    input_grad = in_order(in_parts).astype(f32)

    conv_share, small = call(
        total_share,
        lengths,
        (conv_own, *conv_rest, ffn_share, vgrad_one, vgrad_two, bias_grad),
        (S((KERNEL, di, own), f32), S((7 + hidden // full, full), f32)),
        [],
        1,
        16,
    )
    small, small_far = all_sum(small)
    matrices = (
        *(conv_master, conv_first, conv_second),
        *(hidden_master, hidden_first, hidden_second),
        *(output_master.T, output_first.T, output_second.T),
    )
    vector_ones = (vectors, vector_first, vector_second)
    bias_ones = [v.reshape(1, part) for v in (hidden_bias, bias_first, bias_second)]
    states = (*matrices, *vector_ones, *bias_ones)
    *updated, norm = call(
        update,
        lengths,
        (small, small_far, conv_share, ffn_share, *states),
        (*(S(v.shape, f32) for v in states), S((1, 1), f32)),
        [pltpu.VMEM(small.shape, f32)],
        1,
        16,
    )
    updated[6:9] = [v.T for v in updated[6:9]]
    updated[12:] = [v.reshape(part) for v in updated[12:]]
    return (block_output, input_grad, norm.reshape(()), *updated)


def solution(mesh):
    rows = P("dp", None, "mp")
    conv = P(None, "dp", "mp")
    hid = P("dp", "mp")
    out = P("mp", "dp")
    return jax.shard_map(
        functools.partial(per_device, mesh.shape["dp"], mesh.shape["mp"]),
        mesh=mesh,
        in_specs=(rows, rows, P("dp"), *(conv, hid, out) * 3, *(P(),) * 3, *(P("mp"),) * 3),
        out_specs=(
            rows,
            rows,
            P(),
            *(conv,) * 3,
            *(hid,) * 3,
            *(out,) * 3,
            *(P(),) * 3,
            *(P("mp"),) * 3,
        ),
        check_vma=False,
    )
```
